32 devices in a mesh: dp: 16 (over z, y, x), mp: 2 (over core).
Axes of the slice: x: 2, y: 2, z: 4, core: 2. Of those that a mesh axis runs over, the one named last changes fastest.
Arguments:
- media: bfloat16 [32, 2048, 1536], P('dp', 'mp'), may hold values from -6 to 6
- frame_counts: int32 [32], P('dp'), may hold values from 1 to 8, as said below
- latents: bfloat16 [32, 64, 1536], P('dp', 'mp'), may hold values from -6 to 6
- norm_media_gain: bfloat16 [1536], replicated, may hold values from 0.5 to 1.5
- norm_media_shift: bfloat16 [1536], replicated, may hold values from -1.75 to 1.75
- norm_latent_gain: bfloat16 [1536], replicated, may hold values from 0.5 to 1.5
- norm_latent_shift: bfloat16 [1536], replicated, may hold values from -1.75 to 1.75
- time_embed: bfloat16 [8, 1536], replicated, may hold values from -3 to 3
- query_weight: bfloat16 [1536, 1536], replicated, may hold values from -0.15625 to 0.15625
- key_value_weight: bfloat16 [1536, 3072], replicated, may hold values from -0.15625 to 0.15625
- out_weight: bfloat16 [1536, 1536], replicated, may hold values from -3.5 to 3.5
- ffn_norm_gain: bfloat16 [1536], replicated, may hold values from 0.5 to 1.5
- ffn_norm_shift: bfloat16 [1536], replicated, may hold values from -1.75 to 1.75
- ffn_in_weight: bfloat16 [1536, 6144], P(None, 'mp'), may hold values from -0.15625 to 0.15625
- ffn_out_weight: bfloat16 [6144, 1536], P('mp'), may hold values from -0.078125 to 0.078125
- out_cotangent: bfloat16 [32, 64, 1536], P('dp', 'mp'), may hold values from -6 to 6
Outputs:
- latent_out: bfloat16 [32, 64, 1536], P('dp', 'mp')
- latent_grad: float32 [32, 64, 1536], P('dp', 'mp')
- media_grad: float32 [32, 2048, 1536], P('dp', 'mp')
- norm_media_gain_grad: float32 [1536], P(('dp', 'mp'))
- norm_media_shift_grad: float32 [1536], P(('dp', 'mp'))
- norm_latent_gain_grad: float32 [1536], P(('dp', 'mp'))
- norm_latent_shift_grad: float32 [1536], P(('dp', 'mp'))
- time_embed_grad: float32 [8, 1536], P(None, ('dp', 'mp'))
- query_weight_grad: float32 [1536, 1536], P(('dp', 'mp'))
- key_value_weight_grad: float32 [1536, 3072], P(('dp', 'mp'))
- out_weight_grad: float32 [1536, 1536], P(None, ('dp', 'mp'))
- ffn_norm_gain_grad: float32 [1536], P(('dp', 'mp'))
- ffn_norm_shift_grad: float32 [1536], P(('dp', 'mp'))
- ffn_in_weight_grad: float32 [1536, 6144], P('dp', 'mp')
- ffn_out_weight_grad: float32 [6144, 1536], P('mp', 'dp')
The draws below stay inside these ranges and needn't reach their ends.
Inputs may be any that keep to these rules, and one draw needn't show every extreme that they name: `frame_counts`: each group of 2 consecutive items holds one item with all 8 frames and one single-frame image.
All inputs are finite; a program needn't handle non-finite values.
Results may differ from the reference program's by a relative error of at most 0.014.
Values may be sent and summed in bfloat16 or wider, within the bound.
A program may use at most 256 MiB of HBM per device.

```python
import jax
import jax.numpy as jnp
from jax import lax

D = 1536
HEADS = 16
HEAD_DIM = 96
FF = 6144
LATENTS = 64
FRAMES = 8
PATCH = 256
ITEMS = 2
ITEMS_ALL = 32


def draw_frame_counts(key, part):
    key = jax.random.fold_in(key, 7)
    key_counts, key_full, key_image = jax.random.split(key, 3)
    groups = ITEMS_ALL // ITEMS
    counts = jax.random.randint(key_counts, (ITEMS_ALL,), 1, FRAMES + 1)
    position = jnp.arange(ITEMS_ALL) % ITEMS
    group_of = jnp.arange(ITEMS_ALL) // ITEMS
    full_pick = jax.random.randint(key_full, (groups,), 0, ITEMS)
    image_step = jax.random.randint(key_image, (groups,), 1, max(ITEMS, 2))
    image_pick = (full_pick + image_step) % ITEMS
    counts = jnp.where(position == image_pick[group_of], 1, counts)
    counts = jnp.where(position == full_pick[group_of], FRAMES, counts)
    return counts.astype(jnp.int32)


def shard_levels(rng, dims, shards, least, top_value):
    def one(axis_at, shards_of):
        steps = jax.random.uniform(jax.random.fold_in(jax.random.fold_in(rng, 6), axis_at), (shards_of,), jnp.float32, least / len(shards), top_value / len(shards))
        return jnp.repeat(jnp.exp(steps), dims[axis_at] // shards_of).reshape((-1,) + (1,) * (len(dims) - axis_at - 1))

    level = one(*shards[0])
    for cut in shards[1:]:
        level = level * one(*cut)
    return level


def normal_values(stream_key, extent, spread, reach, cuts=(), dtype=jnp.bfloat16):
    entries = jax.random.normal(stream_key, extent, jnp.float32) * spread
    if len(cuts) > 0:
        entries = shard_levels(stream_key, extent, cuts, -0.22, 0.18) * entries
    return jnp.clip(entries, min=-reach, max=reach).astype(dtype)


def setup_inputs(seed: int = 0) -> dict:
    key_of = jax.random.split(jax.random.key(seed), 17)
    media = normal_values(key_of[0], (ITEMS_ALL, FRAMES * PATCH, D), 1.0, 6.0, ((0, 16), (1, 2)))
    frame_counts = draw_frame_counts(jax.random.fold_in(key_of[16], 71), 0)
    latents = normal_values(key_of[2], (ITEMS_ALL, LATENTS, D), 1.0, 6.0, ((0, 16), (1, 2)))
    norm_media_gain = jnp.clip(1.0 + 0.1 * jax.random.normal(key_of[3], (D,), jnp.float32), 0.5, 1.5).astype(jnp.bfloat16)
    norm_media_shift = normal_values(key_of[4], (D,), 0.3, 1.75)
    norm_latent_gain = jnp.clip(1.0 + 0.1 * jax.random.normal(key_of[5], (D,), jnp.float32), 0.5, 1.5).astype(jnp.bfloat16)
    norm_latent_shift = normal_values(key_of[6], (D,), 0.3, 1.75)
    time_embed = normal_values(key_of[7], (FRAMES, D), 0.5, 3.0)
    query_weight = normal_values(key_of[8], (D, HEADS * HEAD_DIM), D ** -0.5, 0.15625)
    key_value_weight = normal_values(key_of[9], (D, 2 * HEADS * HEAD_DIM), D ** -0.5, 0.15625)
    out_weight = normal_values(key_of[10], (HEADS * HEAD_DIM, D), (max(1, D // 512)) ** -0.5, 3.5)
    ffn_norm_gain = jnp.clip(1.0 + 0.1 * jax.random.normal(key_of[11], (D,), jnp.float32), 0.5, 1.5).astype(jnp.bfloat16)
    ffn_norm_shift = normal_values(key_of[12], (D,), 0.3, 1.75)
    ffn_in_weight = normal_values(key_of[13], (D, FF), D ** -0.5, 0.15625, ((1, 2),))
    ffn_out_weight = normal_values(key_of[14], (FF, D), FF ** -0.5, 0.078125, ((0, 2),))
    out_cotangent = normal_values(key_of[15], (ITEMS_ALL, LATENTS, D), 1.0, 6.0, ((0, 16), (1, 2)))
    return dict(media=media, frame_counts=frame_counts, latents=latents, norm_media_gain=norm_media_gain, norm_media_shift=norm_media_shift, norm_latent_gain=norm_latent_gain, norm_latent_shift=norm_latent_shift, time_embed=time_embed, query_weight=query_weight, key_value_weight=key_value_weight, out_weight=out_weight, ffn_norm_gain=ffn_norm_gain, ffn_norm_shift=ffn_norm_shift, ffn_in_weight=ffn_in_weight, ffn_out_weight=ffn_out_weight, out_cotangent=out_cotangent)


epsilon = 1e-05
highest = lax.Precision.HIGHEST

@jax.custom_vjp
def low(v):
    return lax.optimization_barrier(v.astype(jnp.bfloat16)).astype(jnp.float32)

@jax.custom_vjp
def low_back(v):
    return v

def low_keep(v):
    return (low(v), None)

def low_pass(kept, grad):
    return (grad,)

def back_keep(v):
    return (v, None)

def back_low(kept, grad):
    return (low(grad),)
low.defvjp(low_keep, low_pass)
low_back.defvjp(back_keep, back_low)

def layer_norm(values_in, gain, shift):
    row_mean = lax.optimization_barrier(jnp.mean(values_in, -1, keepdims=True))
    centered = values_in - row_mean
    variance = lax.optimization_barrier(jnp.mean(centered * centered, -1, keepdims=True))
    return centered * lax.rsqrt(variance + epsilon) * gain + shift

def matmul(left, right):
    return jnp.dot(left, right, precision=highest)

def item_forward(parameters, media_item, frame_total, latent_item):
    gain_m, shift_m, gain_l, shift_l, time_rows, w_query, w_kv, w_out, gain_f, shift_f, w_in, w_down = parameters
    inner = HEADS * HEAD_DIM
    with_time = media_item + jnp.repeat(time_rows, PATCH, axis=0)
    media_norm = low(layer_norm(with_time, gain_m, shift_m))
    latent_norm = low(layer_norm(latent_item, gain_l, shift_l))
    queries = low_back(low(matmul(latent_norm, w_query)))
    keys_values = low_back(low(matmul(jnp.concatenate([media_norm, latent_norm], 0), w_kv)))
    key_heads = keys_values[:, :inner].reshape(-1, HEADS, HEAD_DIM)
    value_heads = keys_values[:, inner:].reshape(-1, HEADS, HEAD_DIM)
    query_heads = queries.reshape(LATENTS, HEADS, HEAD_DIM)
    scores = low_back(jnp.einsum('qhd,khd->hqk', query_heads, key_heads, precision=highest) * HEAD_DIM ** (-0.5))
    frame_alive = jnp.arange(FRAMES) < frame_total
    key_alive = jnp.concatenate([jnp.repeat(frame_alive, PATCH), jnp.ones((LATENTS,), bool)])
    masked = jnp.where(key_alive[None, None, :], scores, -1e+30)
    peak = lax.optimization_barrier(jnp.max(masked, -1, keepdims=True))
    weights = jnp.where(key_alive[None, None, :], jnp.exp(masked - peak), 0.0)
    probability = weights / lax.optimization_barrier(jnp.sum(weights, -1, keepdims=True))
    attended = jnp.einsum('hqk,khd->qhd', low(probability), value_heads, precision=highest).reshape(LATENTS, inner)
    attended = low_back(low(attended))
    update = low_back(matmul(attended, w_out))
    hidden_state = latent_item + update
    ffn_norm = low(layer_norm(hidden_state, gain_f, shift_f))
    pre_act = low_back(matmul(ffn_norm, w_in))
    activated = low(jax.nn.gelu(pre_act, approximate=False))
    return hidden_state + matmul(activated, w_down)

def reference(media, frame_counts, latents, norm_media_gain, norm_media_shift, norm_latent_gain, norm_latent_shift, time_embed, query_weight, key_value_weight, out_weight, ffn_norm_gain, ffn_norm_shift, ffn_in_weight, ffn_out_weight, out_cotangent):
    parameters = tuple((p.astype(jnp.float32) for p in (norm_media_gain, norm_media_shift, norm_latent_gain, norm_latent_shift, time_embed, query_weight, key_value_weight, out_weight, ffn_norm_gain, ffn_norm_shift, ffn_in_weight, ffn_out_weight)))

    def scan_step(totals, item_data):
        media_item, frame_total, latent_item, cotangent = item_data

        def forward(prm, media_rows, latent_rows):
            return item_forward(prm, media_rows, frame_total, latent_rows)
        result, pullback = jax.vjp(forward, parameters, media_item.astype(jnp.float32), latent_item.astype(jnp.float32))
        gradients = pullback(cotangent.astype(jnp.float32))
        totals = jax.tree.map(jnp.add, totals, gradients[0])
        return (totals, (result.astype(jnp.bfloat16), gradients[2], gradients[1]))
    zeros = jax.tree.map(jnp.zeros_like, parameters)
    totals, (latent_out, latent_grad, media_grad) = lax.scan(scan_step, zeros, (media, frame_counts, latents, out_cotangent))
    return (latent_out, latent_grad, media_grad, totals[0], totals[1], totals[2], totals[3], totals[4], totals[5], totals[6], totals[7], totals[8], totals[9], totals[10], totals[11])
```

```python
import functools

import jax
import jax.numpy as jnp
from jax import lax
from jax.experimental import pallas as pl
from jax.experimental.pallas import tpu as pltpu
from jax.sharding import PartitionSpec as P

HEADS = 16
HEAD_DIM = 96
PATCH = 256
GROUP = 4
SPAN = GROUP * HEAD_DIM
GROUPS = HEADS // GROUP
LATENT_PAD = 32
EPSILON = 1e-05
SCALE = HEAD_DIM ** (-0.5)
F32 = jnp.float32
BF16 = jnp.bfloat16
MESH = pl.DeviceIdType.MESH
VMEM_LIMIT = 60 * 1024 * 1024

VMEM = pl.BlockSpec(memory_space=pltpu.VMEM)
SMEM = pl.BlockSpec(memory_space=pltpu.SMEM)
ANY = pl.BlockSpec(memory_space=pl.ANY)


def dot(left, right, left_axis, right_axis):
    return lax.dot_general(
        left,
        right,
        (((left_axis,), (right_axis,)), ((), ())),
        preferred_element_type=F32,
    )


def normalize(rows):
    mean = jnp.mean(rows, -1, keepdims=True)
    centered = rows - mean
    variance = jnp.mean(centered * centered, -1, keepdims=True)
    inverse = lax.rsqrt(variance + EPSILON)
    return centered * inverse, inverse


def norm_back(unit, inverse, gain, gradient):
    scaled = gradient * gain
    return inverse * (
        scaled
        - jnp.mean(scaled, -1, keepdims=True)
        - unit * jnp.mean(scaled * unit, -1, keepdims=True)
    )


def lane_head(rows):
    column = lax.broadcasted_iota(jnp.int32, (rows, SPAN), 1)
    head = jnp.zeros((rows, SPAN), jnp.int32)
    for h in range(1, GROUP):
        head += (column >= h * HEAD_DIM).astype(jnp.int32)
    return head


def spread_heads(rows):
    head = lane_head(rows.shape[0])
    zero = jnp.zeros_like(rows)
    return jnp.concatenate([jnp.where(head == h, rows, zero) for h in range(GROUP)], 0)


def fold_heads(rows):
    count = rows.shape[0] // GROUP
    head = lane_head(count)
    total = jnp.zeros((count, SPAN), F32)
    for h in range(GROUP):
        total += jnp.where(head == h, rows[h * count : (h + 1) * count], 0.0)
    return total


def dot_exact(left, selector):
    total = None
    for _ in range(3):
        term = left.astype(BF16)
        left = left - term.astype(F32)
        part = dot(term, selector, 1, 0)
        total = part if total is None else total + part
    return total


def head_selector():
    low = lax.broadcasted_iota(jnp.int32, (128, HEADS * HEAD_DIM), 0) * HEAD_DIM
    column = lax.broadcasted_iota(jnp.int32, (128, HEADS * HEAD_DIM), 1)
    return ((column >= low) & (column < low + HEAD_DIM)).astype(F32).astype(BF16)


def head_sums(rows):
    count = rows.shape[0]
    head = lane_head(count)
    lane = lax.broadcasted_iota(jnp.int32, (count, 128), 1)
    result = jnp.zeros((count, 128), F32)
    for group in range(GROUPS):
        span = rows[:, group * SPAN : (group + 1) * SPAN]
        for h in range(GROUP):
            total = jnp.sum(jnp.where(head == h, span, 0.0), 1, keepdims=True)
            result += jnp.where(lane == group * GROUP + h, total, 0.0)
    return result


def own_columns(rows, head):
    lane = lax.broadcasted_iota(jnp.int32, rows.shape, 1)
    return jnp.sum(jnp.where(lane == head, rows, 0.0), 1, keepdims=True)


def across_lanes(column):
    return jnp.transpose(jnp.broadcast_to(column, (column.shape[0], 128)))[0:1]


def down_rows(row):
    return jnp.transpose(jnp.broadcast_to(row, (128, row.shape[1])))


def vector(ref):
    return ref[...].astype(F32).reshape(1, ref.shape[-1])


def gelu_parts(pre):
    cdf = 0.5 * (1.0 + lax.erf(pre * (0.5**0.5)))
    return pre * cdf, cdf + pre * (jnp.exp(-0.5 * pre * pre) * 0.3989422804014327)


def params(**more):
    return pltpu.CompilerParams(vmem_limit_bytes=VMEM_LIMIT, **more)


def greet(devices):
    barrier = pltpu.get_barrier_semaphore()
    for device in devices:
        pl.semaphore_signal(barrier, inc=1, device_id=device, device_id_type=MESH)
    pl.semaphore_wait(barrier, len(devices))


def others(axis_size, me):
    return [lax.rem(me + k, axis_size) for k in range(1, axis_size)]


class Place:
    def __init__(self, lines, size, send_sem, recv_sem):
        self.lines, self.size = lines, size
        self.dp, self.me = lax.axis_index("dp"), lax.axis_index("mp")
        self.line = self.dp // 4
        self.high = lax.rem(self.dp // 2, 2)
        self.low = lax.rem(self.dp, 2)
        self.send_sem, self.recv_sem = send_sem, recv_sem
        self.used = 0

    def at(self, line, high, low):
        return (line * 4 + high * 2 + low, self.me)

    def low_peer(self):
        return self.at(self.line, self.high, 1 - self.low)

    def high_peer(self):
        return self.at(self.line, 1 - self.high, self.low)

    def across(self):
        return self.at(self.line, 1 - self.high, 1 - self.low)

    def greet(self):
        greet(
            [self.low_peer(), self.high_peer(), self.across()]
            + [self.at(peer, self.high, self.low) for peer in others(self.lines, self.line)]
            + [(self.dp, peer) for peer in others(self.size, self.me)]
        )

    def exchange(self, source, target, land, device):
        index = self.used
        self.used += 1

        def copy(destination):
            return pltpu.make_async_remote_copy(
                src_ref=source,
                dst_ref=destination,
                send_sem=self.send_sem.at[index],
                recv_sem=self.recv_sem.at[index],
                device_id=device,
                device_id_type=MESH,
            )

        pair = (copy(target), copy(land))
        pair[0].start()
        return pair

    def swap(self, me, count, device_of, source_of, land_of):
        pairs = []
        for k in range(1, count):
            peer, origin = lax.rem(me + k, count), lax.rem(me + count - k, count)
            pairs.append(
                self.exchange(source_of(peer), land_of(me), land_of(origin), device_of(peer))
            )
        return pairs

    def swap_cores(self, source_of, land_of):
        return self.swap(self.me, self.size, lambda p: (self.dp, p), source_of, land_of)

    def swap_lines(self, source_of, land_of):
        return self.swap(
            self.line, self.lines, lambda p: self.at(p, self.high, self.low), source_of, land_of
        )


def finish_sends(pairs):
    for copy, _ in pairs:
        copy.wait_send()


def finish_arrivals(pairs):
    for _, arrival in pairs:
        arrival.wait_recv()


def finish(pairs):
    finish_arrivals(pairs)
    finish_sends(pairs)


class Gather:
    def __init__(self, place, rows, out, sem):
        self.place, self.rows, self.out, self.sem = place, rows, out, sem

    def along_line(self):
        p, out = self.place, self.out
        self.keep = pltpu.make_async_copy(
            self.rows, out.at[p.line, p.high, p.low], self.sem
        )
        self.keep.start()
        self.pairs = p.swap_lines(
            lambda peer: self.rows, lambda line: out.at[line, p.high, p.low]
        )

    def first_half(self):
        p, out = self.place, self.out
        self.keep.wait()
        finish(self.pairs)
        half = p.lines // 2
        near, far = pl.ds(0, half), pl.ds(half, p.lines - half)
        self.pairs = [
            p.exchange(
                out.at[near, p.high, p.low],
                out.at[near, p.high, p.low],
                out.at[near, p.high, 1 - p.low],
                p.low_peer(),
            ),
            p.exchange(
                out.at[far, p.high, p.low],
                out.at[far, p.high, p.low],
                out.at[far, 1 - p.high, p.low],
                p.high_peer(),
            ),
        ]

    def second_half(self):
        p, out = self.place, self.out
        finish(self.pairs)
        half = p.lines // 2
        near, far = pl.ds(0, half), pl.ds(half, p.lines - half)
        self.pairs = [
            p.exchange(
                out.at[near, p.high],
                out.at[near, p.high],
                out.at[near, 1 - p.high],
                p.high_peer(),
            ),
            p.exchange(
                out.at[far, :, p.low],
                out.at[far, :, p.low],
                out.at[far, :, 1 - p.low],
                p.low_peer(),
            ),
        ]

    def end(self):
        finish(self.pairs)


class Scatter:
    def __init__(self, place, blocks, lands, temp, sem, out):
        self.place, self.blocks, self.lands, self.out = place, blocks, lands, out
        self.temp, self.sem = temp, sem

    @staticmethod
    def lands(lines, rows, columns):
        half = lines // 2
        return [
            jax.ShapeDtypeStruct((2, half, 2, rows, columns), BF16),
            jax.ShapeDtypeStruct((2, half, rows, columns), BF16),
            jax.ShapeDtypeStruct((lines, rows, columns), BF16),
        ]

    def load(self, pairs):
        copies = [
            pltpu.make_async_copy(source, target, self.sem.at[k])
            for k, (source, target) in enumerate(pairs)
        ]
        for copy in copies:
            copy.start()
        for copy in copies:
            copy.wait()

    def first_half(self):
        p, blocks, land = self.place, self.blocks, self.lands[0]
        half = p.lines // 2
        near, far = pl.ds(0, half), pl.ds(half, half)
        self.pairs = [
            p.exchange(blocks.at[near, :, 1 - p.low], land.at[0], land.at[0], p.low_peer()),
            p.exchange(blocks.at[far, 1 - p.high], land.at[1], land.at[1], p.high_peer()),
        ]

    def second_half(self):
        p, blocks, land, into, temp = self.place, self.blocks, *self.lands[:2], self.temp
        half = p.lines // 2
        near, far = pl.ds(0, half), pl.ds(half, half)
        finish(self.pairs)
        self.load([(land.at[k], temp.at[k]) for k in range(2)])

        @pl.loop(0, half)
        def _(line):
            for k in range(2):
                mine = blocks[line, k, p.low].astype(F32) + temp[0, line, k].astype(F32)
                blocks[line, k, p.low] = mine.astype(BF16)
                mine = blocks[half + line, p.high, k].astype(F32) + temp[1, line, k].astype(F32)
                blocks[half + line, p.high, k] = mine.astype(BF16)

        self.pairs = [
            p.exchange(blocks.at[near, 1 - p.high, p.low], into.at[0], into.at[0], p.high_peer()),
            p.exchange(blocks.at[far, p.high, 1 - p.low], into.at[1], into.at[1], p.low_peer()),
        ]

    def along_line(self):
        p, blocks, temp = self.place, self.blocks, self.temp
        into, land = self.lands[1:]
        half = p.lines // 2
        finish(self.pairs)
        self.load([(into.at[k], temp.at[k, :, 0]) for k in range(2)])

        @pl.loop(0, half)
        def _(line):
            for k in range(2):
                mine = blocks[k * half + line, p.high, p.low].astype(F32)
                mine += temp[k, line, 0].astype(F32)
                blocks[k * half + line, p.high, p.low] = mine.astype(BF16)

        self.pairs = p.swap_lines(
            lambda peer: blocks.at[peer, p.high, p.low], lambda line: land.at[line]
        )

    def end(self):
        p, land, temp = self.place, self.lands[2], self.temp
        half = p.lines // 2
        finish(self.pairs)
        peers = others(p.lines, p.line)
        self.load(
            [(land.at[peer], temp.at[k // half, k % half, 0]) for k, peer in enumerate(peers)]
        )
        total = self.blocks[p.line, p.high, p.low].astype(F32)
        for k in range(len(peers)):
            total += temp[k // half, k % half, 0].astype(F32)
        self.out[...] = total


class Move:
    def __init__(self, place, blocks, middle, out, sem):
        self.place, self.blocks, self.middle, self.out, self.sem = place, blocks, middle, out, sem

    def in_plane(self):
        p, blocks, middle = self.place, self.blocks, self.middle
        self.keep = pltpu.make_async_copy(
            blocks.at[:, p.high, p.low], middle.at[:, p.high, p.low], self.sem.at[0]
        )
        self.keep.start()
        self.pairs = []
        for device, high, low in (
            (p.low_peer(), p.high, 1 - p.low),
            (p.high_peer(), 1 - p.high, p.low),
            (p.across(), 1 - p.high, 1 - p.low),
        ):
            self.pairs.append(
                p.exchange(
                    blocks.at[:, high, low],
                    middle.at[:, p.high, p.low],
                    middle.at[:, high, low],
                    device,
                )
            )

    def along_line(self):
        p, middle, out = self.place, self.middle, self.out
        self.keep.wait()
        finish(self.pairs)
        self.keep = pltpu.make_async_copy(middle.at[p.line], out.at[p.line], self.sem.at[1])
        self.keep.start()
        self.pairs = p.swap_lines(lambda peer: middle.at[peer], lambda line: out.at[line])

    def end(self):
        self.keep.wait()
        finish(self.pairs)


class Total:
    def __init__(self, place, array, land, sums):
        self.place, self.array, self.land, self.sums = place, array, land, sums

    @staticmethod
    def scratch(lines, size, shape):
        return [pltpu.VMEM((size + 2 + lines,) + shape, F32), pltpu.VMEM((3,) + shape, F32)]

    def in_chip(self):
        self.pairs = self.place.swap_cores(lambda peer: self.array, lambda core: self.land.at[core])

    def low(self):
        p = self.place
        finish(self.pairs)
        total = self.array[...]
        for peer in others(p.size, p.me):
            total += self.land[peer]
        self.sums[0] = total
        land = self.land.at[p.size]
        self.pairs = [p.exchange(self.sums.at[0], land, land, p.low_peer())]

    def high(self):
        p = self.place
        finish(self.pairs)
        self.sums[1] = self.sums[0] + self.land[p.size]
        land = self.land.at[p.size + 1]
        self.pairs = [p.exchange(self.sums.at[1], land, land, p.high_peer())]

    def along_line(self):
        p = self.place
        finish(self.pairs)
        self.sums[2] = self.sums[1] + self.land[p.size + 1]
        self.pairs = p.swap_lines(
            lambda peer: self.sums.at[2], lambda line: self.land.at[p.size + 2 + line]
        )

    def end(self, out):
        p = self.place
        finish(self.pairs)
        total = self.sums[2]
        for peer in others(p.lines, p.line):
            total += self.land[p.size + 2 + peer]
        out[...] = total


ROWS = 64


def in_order(first_full, pair):
    return jnp.where(first_full, pair[0], pair[1]), jnp.where(first_full, pair[1], pair[0])


def forward_kernel(
    frames,
    lines,
    size,
    counts,
    media,
    latents,
    cotangent,
    gain_media,
    shift_media,
    gain_latent,
    shift_latent,
    time_embed,
    query_hbm,
    kv_hbm,
    norm_full_out,
    norm_image_out,
    weight_full_out,
    weight_image_out,
    absorbed_out,
    mixed_out,
    value_out,
    peak_out,
    latent_norm,
    queries,
    cotangent_all,
    cotangent_rows,
    own,
    latent_all,
    norm_full,
    norm_image,
    weight_full,
    weight_image,
    absorbed,
    mixed,
    query_weight,
    kv_weight,
    buffer,
    times,
    media_sem,
    load_sem,
    store_sem,
    gather_sem,
    send_sem,
    recv_sem,
):
    inner = HEADS * HEAD_DIM
    place = Place(lines, size, send_sem, recv_sem)
    me = place.me
    local = latents.shape[1]
    rows = 2 * local
    lat_all = local * size
    first_full = counts[0] > counts[1]
    image_alive = me * frames < jnp.minimum(counts[0], counts[1])

    def fetch(frame, slot):
        return pltpu.make_async_copy(
            media.at[:, pl.ds(frame * PATCH, PATCH)], buffer.at[slot], media_sem.at[slot]
        )

    load_query = pltpu.make_async_copy(query_hbm, query_weight, load_sem.at[0])
    load_kv = pltpu.make_async_copy(kv_hbm, kv_weight, load_sem.at[1])
    times[...] = time_embed[...].astype(F32)
    fetch(0, 0).start()
    load_query.start()
    load_kv.start()
    place.greet()
    for k, array in ((0, latents), (1, cotangent)):
        pair = in_order(first_full, (array[0].astype(F32), array[1].astype(F32)))
        own[k] = jnp.concatenate(pair, 0).astype(BF16)
    latent_swap = place.swap_cores(lambda p: own.at[0], lambda c: latent_all.at[c])
    cotangent_swap = place.swap_cores(lambda p: own.at[1], lambda c: cotangent_all.at[c])
    gather = Gather(place, own.at[1], cotangent_rows, gather_sem.at[0])
    gather.along_line()
    latent_all[me] = own[0]
    cotangent_all[me] = own[1]

    gain_m, shift_m = vector(gain_media), vector(shift_media)
    gain_l, shift_l = vector(gain_latent), vector(shift_latent)

    def normalize_frame(frame, slot, pick_first, target, base):
        time_row = times[pl.ds(me * frames + frame, 1)]

        @pl.loop(0, PATCH // ROWS)
        def _(part):
            at = pl.multiple_of(part * ROWS, ROWS)
            values = jnp.where(
                pick_first,
                buffer[slot, 0, pl.ds(at, ROWS)].astype(F32),
                buffer[slot, 1, pl.ds(at, ROWS)].astype(F32),
            )
            unit, _ = normalize(values + time_row)
            target[pl.ds(pl.multiple_of(base + at, ROWS), ROWS)] = (unit * gain_m + shift_m).astype(
                BF16
            )

    @pl.loop(0, frames)
    def _(frame):
        slot = lax.rem(frame, 2)
        fetch(frame, slot).wait()

        @pl.when(frame + 1 < frames)
        def _():
            fetch(frame + 1, 1 - slot).start()

        normalize_frame(frame, slot, first_full, norm_full, frame * PATCH)

        @pl.when(frame == 0)
        def _():
            normalize_frame(frame, slot, jnp.logical_not(first_full), norm_image, 0)

    unit, _ = normalize(own[0].astype(F32))
    low = (unit * gain_l + shift_l).astype(BF16)
    norm_full[frames * PATCH : frames * PATCH + local] = low[:local]
    norm_image[PATCH : PATCH + local] = low[local:]
    finish(latent_swap)
    for item in range(2):
        for core in range(size):
            unit, _ = normalize(latent_all[core, item * local : (item + 1) * local].astype(F32))
            at = item * lat_all + core * local
            latent_norm[at : at + local] = (unit * gain_l + shift_l).astype(BF16)
    stores = []

    def store(source, target):
        copy = pltpu.make_async_copy(source, target, store_sem.at[len(stores)])
        copy.start()
        stores.append(copy)

    store(norm_full, norm_full_out)
    store(norm_image, norm_image_out)
    load_query.wait()

    @pl.loop(0, GROUPS)
    def _(group):
        span = pl.ds(pl.multiple_of(group * SPAN, SPAN), SPAN)
        queries[:, span] = dot(latent_norm[...], query_weight[:, span], 1, 0).astype(BF16)

    gather.first_half()
    load_kv.wait()
    step = GROUP * lat_all
    lane = lax.broadcasted_iota(jnp.int32, (lat_all, 128), 1)
    outer_lane = lax.broadcasted_iota(jnp.int32, (rows, 128), 1)
    for core in range(size):
        peak_out[core, 0] = jnp.zeros((rows, 128), F32)
        peak_out[core, 1] = jnp.where(outer_lane < HEADS, 0.0, 1.0)
    for item, keys, weights, weights_out in (
        (0, norm_full, weight_full, weight_full_out),
        (1, norm_image, weight_image, weight_image_out),
    ):
        count = keys.shape[0]
        row = lax.broadcasted_iota(jnp.int32, (count, 1), 0)
        live = (row >= count - local) | image_alive

        @pl.loop(0, GROUPS)
        def _(group, item=item, keys=keys, weights=weights, live=live):
            span = pl.ds(pl.multiple_of(group * SPAN, SPAN), SPAN)
            value_span = pl.ds(pl.multiple_of(inner + group * SPAN, SPAN), SPAN)
            at = pl.ds(pl.multiple_of(group * step, step), step)
            spread = spread_heads(queries[item * lat_all : (item + 1) * lat_all, span])
            key_rows = (dot(spread, kv_weight[:, span], 1, 1) * SCALE).astype(BF16)
            absorbed[item, at] = key_rows
            scores = dot(keys[...], key_rows, 1, 1)
            if item == 1:
                scores = jnp.where(live, scores, -1e30)
            peak = jnp.max(scores, 0, keepdims=True)
            weight = jnp.exp(scores - peak)
            if item == 1:
                weight = jnp.where(live, weight, 0.0)
            total = jnp.sum(weight, 0, keepdims=True)
            low = weight.astype(BF16)
            weights[:, at] = low
            mix = dot(low, keys[...], 0, 0).astype(BF16)
            mixed[item, at] = mix
            values = fold_heads(dot(mix, kv_weight[:, value_span], 1, 0))
            statistics = []
            for row_values in (peak, total):
                down = down_rows(row_values)
                picked = jnp.zeros((lat_all, 128), F32)
                for h in range(GROUP):
                    rows_of_head = down[h * lat_all : (h + 1) * lat_all]
                    picked += jnp.where(lane == group * GROUP + h, rows_of_head, 0.0)
                statistics.append(picked)
            for core in range(size):
                mine = slice(core * local, (core + 1) * local)
                into = slice(item * local, (item + 1) * local)
                value_out[core, into, span] = values[mine]
                for k in range(2):
                    peak_out[core, k, into] += statistics[k][mine]

        store(weights, weights_out)
        store(absorbed.at[item], absorbed_out.at[item])
        store(mixed.at[item], mixed_out.at[item])
        if item == 0:
            gather.second_half()
    for copy in stores:
        copy.wait()
    finish(cotangent_swap)
    gather.end()


def attend_forward(
    chips,
    size,
    counts,
    media,
    latents,
    cotangent,
    gain_media,
    shift_media,
    gain_latent,
    shift_latent,
    time_embed,
    query_weight,
    kv_weight,
):
    width = media.shape[-1]
    inner = HEADS * HEAD_DIM
    lines = chips // 4
    frames = media.shape[1] // PATCH
    local = latents.shape[1]
    rows = 2 * local
    lat_all = local * size
    keys = (frames * PATCH + local, PATCH + local)
    slots = HEADS * lat_all
    shape = jax.ShapeDtypeStruct
    copies = lines + 2 * size + 8
    return pl.pallas_call(
        functools.partial(forward_kernel, frames, lines, size),
        out_shape=[
            shape((keys[0], width), BF16),
            shape((keys[1], width), BF16),
            shape((keys[0], slots), BF16),
            shape((keys[1], slots), BF16),
            shape((2, slots, width), BF16),
            shape((2, slots, width), BF16),
            shape((size, rows, inner), F32),
            shape((size, 2, rows, 128), F32),
            shape((2 * lat_all, width), BF16),
            shape((2 * lat_all, inner), BF16),
            shape((size, rows, width), BF16),
            shape((lines, 2, 2, rows, width), BF16),
        ],
        in_specs=[SMEM, ANY] + [VMEM] * 7 + [ANY] * 2,
        out_specs=[ANY] * 6 + [VMEM] * 5 + [ANY],
        scratch_shapes=[
            pltpu.VMEM((2, rows, width), BF16),
            pltpu.VMEM((size, rows, width), BF16),
            pltpu.VMEM((keys[0], width), BF16),
            pltpu.VMEM((keys[1], width), BF16),
            pltpu.VMEM((keys[0], slots), BF16),
            pltpu.VMEM((keys[1], slots), BF16),
            pltpu.VMEM((2, slots, width), BF16),
            pltpu.VMEM((2, slots, width), BF16),
            pltpu.VMEM(query_weight.shape, BF16),
            pltpu.VMEM(kv_weight.shape, BF16),
            pltpu.VMEM((2, 2, PATCH, width), BF16),
            pltpu.VMEM(time_embed.shape, F32),
            pltpu.SemaphoreType.DMA((2,)),
            pltpu.SemaphoreType.DMA((2,)),
            pltpu.SemaphoreType.DMA((8,)),
            pltpu.SemaphoreType.DMA((1,)),
            pltpu.SemaphoreType.DMA((copies,)),
            pltpu.SemaphoreType.DMA((copies,)),
        ],
        compiler_params=params(collective_id=0, has_side_effects=True),
    )(
        counts,
        media,
        latents,
        cotangent,
        gain_media,
        shift_media,
        gain_latent,
        shift_latent,
        time_embed,
        query_weight,
        kv_weight,
    )


DEPTH = 3


def latent_kernel(
    lines,
    size,
    chunk,
    counts,
    value_parts,
    peaks,
    latents,
    cotangent_all,
    gain_ffn,
    shift_ffn,
    out_hbm,
    in_hbm,
    down_hbm,
    kv_hbm,
    mixed_hbm,
    cotangent_rows,
    latent_out,
    state_grad,
    gains,
    into_out,
    shifted,
    value_sum,
    out_half,
    ffn_rows,
    cotangent_other,
    value_wait,
    out_weight,
    in_weight,
    down_weight,
    value_weight,
    mixed,
    value_land,
    peak_land,
    ffn_norm,
    partial,
    partial_land,
    kept,
    kept_log,
    attended_all,
    update_all,
    grad_all,
    log_all,
    grad_items,
    stage,
    temp,
    load_sem,
    weight_sem,
    store_sem,
    gather_sem,
    send_sem,
    recv_sem,
):
    inner = HEADS * HEAD_DIM
    place = Place(lines, size, send_sem, recv_sem)
    me = place.me
    first_full = counts[0] > counts[1]
    local, width = latents.shape[1:]
    rows = 2 * local
    lat_all = local * size
    step = GROUP * lat_all
    chunks = in_hbm.shape[1] // chunk
    cores = others(size, me)

    def weights(c):
        at = pl.ds(pl.multiple_of(c * chunk, chunk), chunk)
        slot = lax.rem(c, DEPTH)
        return (
            pltpu.make_async_copy(in_hbm.at[:, at], in_weight.at[slot], weight_sem.at[0, slot]),
            pltpu.make_async_copy(down_hbm.at[at, :], down_weight.at[slot], weight_sem.at[1, slot]),
        )

    loads = [
        pltpu.make_async_copy(out_hbm, out_weight, load_sem.at[0]),
        pltpu.make_async_copy(kv_hbm.at[:, pl.ds(inner, inner)], value_weight, load_sem.at[1]),
        pltpu.make_async_copy(mixed_hbm, mixed, load_sem.at[2]),
    ]
    loads[0].start()
    for c in range(min(DEPTH, chunks)):
        for copy in weights(c):
            copy.start()
    loads[1].start()
    loads[2].start()
    place.greet()
    values_swap = place.swap_cores(lambda p: value_parts.at[p], lambda c: value_land.at[c])
    peaks_swap = place.swap_cores(lambda p: peaks.at[p], lambda c: peak_land.at[c])
    cotangent_swap = place.swap_cores(
        lambda p: cotangent_rows, lambda c: cotangent_other.at[c]
    )
    value_land[me] = value_parts[me]
    peak_land[me] = peaks[me]
    selector = head_selector()
    finish(values_swap)
    finish(peaks_swap)
    peak = peak_land[0, 0]
    for s in range(1, size):
        peak = jnp.maximum(peak, peak_land[s, 0])
    factors = [jnp.exp(peak_land[s, 0] - peak) for s in range(size)]
    total = factors[0] * peak_land[0, 1]
    for s in range(1, size):
        total += factors[s] * peak_land[s, 1]
    kept_log[...] = peak + jnp.log(total)
    attended = jnp.zeros((rows, width), F32)
    for s in range(size):
        attended += value_land[s] * dot_exact(factors[s] / total, selector)
    kept[0] = attended
    attended_low = attended.astype(BF16)
    attended_all[me] = attended_low
    loads[0].wait()
    hidden = dot(attended_low, out_weight[...], 1, 0)
    hidden += jnp.concatenate(
        in_order(first_full, (latents[0].astype(F32), latents[1].astype(F32))), 0
    )
    kept[1] = hidden
    gain, shift = vector(gain_ffn), vector(shift_ffn)
    unit, _ = normalize(hidden)
    ffn_norm[me] = (unit * gain + shift).astype(BF16)
    norm_swap = place.swap_cores(lambda p: ffn_norm.at[me], lambda c: ffn_norm.at[c])
    gather = Gather(place, ffn_norm.at[me], ffn_rows, gather_sem.at[0])
    gather.along_line()
    attended_swap = place.swap_cores(lambda p: attended_all.at[me], lambda c: attended_all.at[c])
    partial[...] = jnp.zeros_like(partial)
    finish(norm_swap)

    @pl.loop(0, chunks)
    def _(c):
        for copy in weights(c):
            copy.wait()
        slot = lax.rem(c, DEPTH)
        all_rows = ffn_norm[...].reshape(size * rows, width)
        cotangents = cotangent_all[...].reshape(size * rows, width)
        activated, slope = gelu_parts(dot(all_rows, in_weight[slot], 1, 0))
        activated = activated.astype(BF16)
        act_grad = dot(cotangents, down_weight[slot], 1, 1)
        pre_grad = (act_grad * slope).astype(BF16)
        partial[0] += dot(activated, down_weight[slot], 1, 0).reshape(size, rows, width)
        partial[1] += dot(pre_grad, in_weight[slot], 1, 1).reshape(size, rows, width)

        @pl.when(c + DEPTH < chunks)
        def _():
            for copy in weights(c + DEPTH):
                copy.start()

    sums_swap = place.swap_cores(lambda p: partial.at[:, p], lambda c: partial_land.at[c])
    gather.first_half()
    finish(sums_swap)
    ffn_sum, norm_grad = partial[0, me], partial[1, me]
    for origin in cores:
        ffn_sum += partial_land[origin, 0]
        norm_grad += partial_land[origin, 1]
    hidden = kept[1]
    unit, inverse = normalize(hidden)
    result = hidden + ffn_sum
    for k, value in enumerate(in_order(first_full, (result[:local], result[local:]))):
        latent_out[k] = value.astype(BF16)
    gains[0:1] = jnp.sum(norm_grad * unit, 0, keepdims=True)
    gains[1:2] = jnp.sum(norm_grad, 0, keepdims=True)
    state = cotangent_all[me].astype(F32) + norm_back(unit, inverse, gain, norm_grad)
    state_grad[...] = state
    update = state.astype(BF16)
    update_all[me] = update
    grad = dot(update, out_weight[...], 1, 1).astype(BF16)
    grad_all[me] = grad
    log_all[me, 0] = kept_log[...]
    log_all[me, 1] = head_sums(grad.astype(F32) * kept[0])
    grad_swap = place.swap_cores(lambda p: grad_all.at[me], lambda c: grad_all.at[c])
    log_swap = place.swap_cores(lambda p: log_all.at[me], lambda c: log_all.at[c])
    update_swap = place.swap_cores(lambda p: update_all.at[me], lambda c: update_all.at[c])
    finish(grad_swap)
    finish(log_swap)

    def by_item(item, of_core):
        part = slice(item * local, (item + 1) * local)
        return jnp.concatenate([of_core(core)[part] for core in range(size)], 0)

    factor, factor_delta = [], []
    for item in range(2):
        grad_items[item] = by_item(item, lambda c: grad_all[c])
        scale = jnp.exp(
            by_item(item, lambda c: peaks[c, 0]) - by_item(item, lambda c: log_all[c, 0])
        )
        factor.append(scale)
        factor_delta.append(scale * by_item(item, lambda c: log_all[c, 1]))
    loads[1].wait()
    loads[2].wait()
    block_rows = width // (lines * 4 * size)
    value_sends = []
    stores = []
    for group in range(GROUPS):
        span = slice(group * SPAN, (group + 1) * SPAN)
        at = slice(group * step, (group + 1) * step)
        weight = None
        for item in range(2):
            spread = spread_heads(grad_items[item, :, span])
            heads = range(group * GROUP, (group + 1) * GROUP)
            column = jnp.concatenate([own_columns(factor[item], h) for h in heads], 0)
            shifted[item : item + 1, at] = across_lanes(
                jnp.concatenate([own_columns(factor_delta[item], h) for h in heads], 0)
            )
            spread = (spread.astype(F32) * column).astype(BF16)
            part = dot(mixed[item, at], spread, 0, 0)
            weight = part if weight is None else weight + part
            mixed[item, at] = dot(spread, value_weight[:, span], 1, 1).astype(BF16)
            copy = pltpu.make_async_copy(
                mixed.at[item, pl.ds(group * step, step)],
                into_out.at[item, pl.ds(group * step, step)],
                store_sem.at[group, item],
            )
            copy.start()
            stores.append(copy)
        slot = group % 2
        if group >= 2:
            finish_sends(value_sends[group - 2])
        low = weight.astype(BF16)
        for k in range(lines * 4):
            for core in range(size):
                base = (k * size + core) * block_rows
                stage[slot, k // 4, (k // 2) % 2, k % 2, core] = low[base : base + block_rows]
        value_sends.append(
            place.swap_cores(
                lambda p, slot=slot: stage.at[slot, :, :, :, p],
                lambda c, group=group: value_wait.at[
                    c, :, :, :, :, pl.ds(group * SPAN, SPAN)
                ],
            )
        )

        @pl.loop(0, lines)
        def _(line, slot=slot, span=span):
            for high in range(2):
                for low_at in range(2):
                    value_sum[line, high, low_at, :, span] = stage[slot, line, high, low_at, me]

    gather.second_half()
    finish(attended_swap)
    finish(update_swap)
    updates = update_all[...].reshape(size * rows, width)
    for group in range(GROUPS):
        span = slice(group * SPAN, (group + 1) * SPAN)
        attends = attended_all[:, :, span].reshape(size * rows, SPAN)
        low = dot(updates, attends, 0, 0)
        for k in range(lines * 4):
            base = k * size * block_rows
            mine = low[base : base + block_rows]
            for core in range(1, size):
                base += block_rows
                mine = jnp.where(me == core, low[base : base + block_rows], mine)
            out_half[k // 4, (k // 2) % 2, k % 2, :, span] = mine.astype(BF16)
    for sends in value_sends[2:]:
        finish_sends(sends)
    for sends in value_sends:
        finish_arrivals(sends)
    for origin in cores:
        load = pltpu.make_async_copy(value_wait.at[origin], temp, load_sem.at[0])
        load.start()
        load.wait()

        @pl.loop(0, lines)
        def _(line):
            for high in range(2):
                for low_at in range(2):
                    mine = value_sum[line, high, low_at].astype(F32)
                    mine += temp[line, high, low_at].astype(F32)
                    value_sum[line, high, low_at] = mine.astype(BF16)

    finish(cotangent_swap)
    for copy in stores:
        copy.wait()
    gather.end()


def latent_pass(
    chips,
    size,
    counts,
    value_parts,
    peaks,
    latents,
    cotangent_all,
    gain_ffn,
    shift_ffn,
    out_weight,
    in_weight,
    down_weight,
    kv_weight,
    mixed,
    cotangent_rows,
):
    lines = chips // 4
    local, width = latents.shape[1:]
    inner = HEADS * HEAD_DIM
    rows = 2 * local
    lat_all = local * size
    hidden_units = in_weight.shape[1]
    chunk = 512 if hidden_units % 512 == 0 else 256
    block_rows = width // (chips * size)
    blocks = (lines, 2, 2, block_rows, inner)
    gathered = (lines, 2, 2, rows, width)
    shape = jax.ShapeDtypeStruct
    copies = lines + 16 * size + 8
    return pl.pallas_call(
        functools.partial(latent_kernel, lines, size, chunk),
        out_shape=[
            shape(latents.shape, BF16),
            shape((rows, width), F32),
            shape((2, width), F32),
            shape(mixed.shape, BF16),
            shape((2, HEADS * lat_all), F32),
            shape(blocks, BF16),
            shape(blocks, BF16),
            shape(gathered, BF16),
            shape((size,) + gathered, BF16),
            shape((size,) + blocks, BF16),
        ],
        in_specs=[SMEM] + [VMEM] * 6 + [ANY] * 6,
        out_specs=[VMEM] * 3 + [ANY] + [VMEM] * 3 + [ANY] * 3,
        scratch_shapes=[
            pltpu.VMEM(out_weight.shape, BF16),
            pltpu.VMEM((DEPTH, width, chunk), BF16),
            pltpu.VMEM((DEPTH, chunk, width), BF16),
            pltpu.VMEM((width, inner), BF16),
            pltpu.VMEM(mixed.shape, BF16),
            pltpu.VMEM((size, rows, width), F32),
            pltpu.VMEM((size, 2, rows, 128), F32),
            pltpu.VMEM((size, rows, width), BF16),
            pltpu.VMEM((2, size, rows, width), F32),
            pltpu.VMEM((size, 2, rows, width), F32),
            pltpu.VMEM((2, rows, width), F32),
            pltpu.VMEM((rows, 128), F32),
            pltpu.VMEM((size, rows, inner), BF16),
            pltpu.VMEM((size, rows, width), BF16),
            pltpu.VMEM((size, rows, inner), BF16),
            pltpu.VMEM((size, 2, rows, 128), F32),
            pltpu.VMEM((2, lat_all, inner), BF16),
            pltpu.VMEM((2, lines, 2, 2, size, block_rows, SPAN), BF16),
            pltpu.VMEM(blocks, BF16),
            pltpu.SemaphoreType.DMA((3,)),
            pltpu.SemaphoreType.DMA((2, DEPTH)),
            pltpu.SemaphoreType.DMA((GROUPS, 2)),
            pltpu.SemaphoreType.DMA((1,)),
            pltpu.SemaphoreType.DMA((copies,)),
            pltpu.SemaphoreType.DMA((copies,)),
        ],
        compiler_params=params(collective_id=1, has_side_effects=True),
    )(
        counts,
        value_parts,
        peaks,
        latents,
        cotangent_all,
        gain_ffn,
        shift_ffn,
        out_weight,
        in_weight,
        down_weight,
        kv_weight,
        mixed,
        cotangent_rows,
    )


def backward_kernel(
    frames,
    lines,
    size,
    counts,
    media,
    latents,
    gain_media,
    gain_latent,
    shift_latent,
    time_embed,
    query_hbm,
    kv_hbm,
    norm_full_hbm,
    norm_image_hbm,
    weight_full_hbm,
    weight_image_hbm,
    absorbed_hbm,
    into_hbm,
    value_sum,
    out_half,
    ffn_rows,
    cotangent_rows,
    cotangent_other,
    shifted,
    queries,
    latent_norm,
    state_grad,
    ffn_gains,
    in_share,
    down_share,
    slot_grad,
    latent_grad,
    value_out_sum,
    key_sum,
    query_sum,
    units_out,
    small_out,
    ffn_other,
    units_middle,
    key_wait,
    vo_first,
    vo_second,
    vo_line,
    key_first,
    key_second,
    key_line,
    query_first,
    query_second,
    query_line,
    vo_blocks,
    key_blocks,
    query_blocks,
    temp,
    column_weight,
    norm_full,
    norm_image,
    weight_full,
    weight_image,
    score_full,
    score_image,
    absorbed,
    into,
    stage,
    query_part,
    query_land,
    query_all,
    buffer,
    share_sum,
    units,
    block,
    result,
    times,
    small,
    small_land,
    small_sums,
    load_sem,
    column_sem,
    buffer_sem,
    result_sem,
    scatter_sem,
    move_sem,
    send_sem,
    recv_sem,
):
    inner = HEADS * HEAD_DIM
    width = media.shape[-1]
    place = Place(lines, size, send_sem, recv_sem)
    me = place.me
    cores = others(size, me)
    first_full = counts[0] > counts[1]
    local = latents.shape[1]
    lat_all = local * size
    step = GROUP * lat_all
    block_rows = width // (lines * 4 * size)

    early = [
        pltpu.make_async_copy(value_sum, vo_blocks.at[..., pl.ds(0, inner)], load_sem.at[0]),
        pltpu.make_async_copy(out_half, vo_blocks.at[..., pl.ds(inner, inner)], load_sem.at[1]),
    ]
    late = [
        pltpu.make_async_copy(source, target, load_sem.at[2 + k])
        for k, (source, target) in enumerate(
            (
                (norm_full_hbm, norm_full),
                (norm_image_hbm, norm_image),
                (weight_full_hbm, weight_full),
                (weight_image_hbm, weight_image),
                (into_hbm, into),
                (absorbed_hbm, absorbed),
            )
        )
    ]

    def column(source, group):
        return pltpu.make_async_copy(
            source.at[:, pl.ds(group * SPAN, SPAN)],
            column_weight.at[group % 2],
            column_sem.at[group % 2],
        )

    own_pieces = [(ffn_rows, cotangent_rows, line) for line in range(lines)]
    pieces = own_pieces + [
        (ffn_other.at[core], cotangent_other.at[core], line) for core in cores for line in range(lines)
    ]
    device_rows = ffn_rows.shape[3]
    piece_rows = 4 * device_rows

    def piece(k):
        ffn_source, cotangent_source, line = pieces[k]
        return [
            pltpu.make_async_copy(
                source.at[line, n // 2, n % 2],
                buffer.at[k % 2, j, pl.ds(n * device_rows, device_rows)],
                buffer_sem.at[k % 2, j, n],
            )
            for j, source in ((0, ffn_source), (1, cotangent_source))
            for n in range(4)
        ]

    for copy in early + piece(0):
        copy.start()
    place.greet()
    for copy in late:
        copy.start()
    column(kv_hbm, 0).start()
    for copy in early:
        copy.wait()
    vo = Scatter(place, vo_blocks, (vo_first, vo_second, vo_line), temp, scatter_sem, value_out_sum)
    narrow = temp.at[:, :, :, :, pl.ds(0, inner)]
    keys_scatter = Scatter(
        place, key_blocks, (key_first, key_second, key_line), narrow, scatter_sem, key_sum
    )
    query_scatter = Scatter(
        place, query_blocks, (query_first, query_second, query_line), narrow, scatter_sem, query_sum
    )
    vo.first_half()
    ffn_swap = place.swap_cores(lambda p: ffn_rows, lambda c: ffn_other.at[c])
    small[...] = jnp.zeros_like(small)
    times[...] = time_embed[...].astype(F32)

    share = in_share.shape[1]
    for k in range(len(pieces)):
        if k + 1 == len(own_pieces):
            finish(ffn_swap)
        if k + 1 < len(pieces):
            for copy in piece(k + 1):
                copy.start()
        for copy in piece(k):
            copy.wait()
        ffn_piece = buffer[k % 2, 0, :piece_rows]
        cotangent_piece = buffer[k % 2, 1, :piece_rows]
        activated, slope = gelu_parts(dot(ffn_piece, in_share[...], 1, 0))
        pre_grad = (dot(cotangent_piece, down_share[...], 1, 1) * slope).astype(BF16)
        up = dot(ffn_piece, pre_grad, 0, 0)
        down = dot(cotangent_piece, activated.astype(BF16), 0, 0)
        if k == 0:
            share_sum[0], share_sum[1] = up, down
        else:
            share_sum[0] += up
            share_sum[1] += down
    unit_rows = width // (lines * 4)
    for k in range(lines * 4):
        at = slice(k * unit_rows, (k + 1) * unit_rows)
        both = jnp.concatenate([share_sum[0, at], share_sum[1, at]], 1)
        units[k // 4, (k // 2) % 2, k % 2] = both.astype(BF16)
    moved = Move(place, units, units_middle, units_out, move_sem)
    moved.in_plane()

    def fetch(frame):
        return pltpu.make_async_copy(
            media.at[:, pl.ds(frame * PATCH, PATCH)], buffer.at[frame % 2], buffer_sem.at[frame % 2, 0, 0]
        )

    fetch(0).start()
    for copy in late[:5]:
        copy.wait()
    key_sends = []
    for group in range(GROUPS):
        span = slice(group * SPAN, (group + 1) * SPAN)
        at = slice(group * step, (group + 1) * step)
        if group + 1 < GROUPS:
            column(kv_hbm, group + 1).start()
        column(kv_hbm, group).wait()
        weight = None
        for item, keys, weights, scores in (
            (0, norm_full, weight_full, score_full),
            (1, norm_image, weight_image, score_image),
        ):
            item_rows = slice(item * lat_all, (item + 1) * lat_all)
            prob_grad = dot(keys[...], into[item, at], 1, 1)
            score = weights[:, at].astype(F32) * (prob_grad - shifted[item : item + 1, at])
            score = score.astype(BF16)
            scores[:, at] = score
            pulled = dot(score, keys[...], 0, 0).astype(BF16)
            query_part[item_rows, span] = (
                fold_heads(dot(pulled, column_weight[group % 2], 1, 0)) * SCALE
            )
            part = dot(pulled, spread_heads(queries[item_rows, span]), 0, 0)
            weight = part if weight is None else weight + part
        if group >= 1:
            finish_sends(key_sends[group - 1])
        low = (weight * SCALE).astype(BF16)
        for k in range(lines * 4):
            for core in range(size):
                base = (k * size + core) * block_rows
                stage[k // 4, (k // 2) % 2, k % 2, core] = low[base : base + block_rows]
        key_sends.append(
            place.swap_cores(
                lambda p: stage.at[:, :, :, p],
                lambda c, group=group: key_wait.at[c, :, :, :, :, pl.ds(group * SPAN, SPAN)],
            )
        )

        @pl.loop(0, lines)
        def _(line, span=span):
            for high in range(2):
                for low_at in range(2):
                    key_blocks[line, high, low_at, :, span] = stage[line, high, low_at, me]

        if group == 2:
            vo.second_half()
    column(query_hbm, 0).start()
    query_swap = place.swap_cores(lambda p: query_part, lambda c: query_land.at[c])
    finish_sends(key_sends[-1])
    for sends in key_sends:
        finish_arrivals(sends)
    half = lines // 2
    for origin in cores:
        loads = [
            pltpu.make_async_copy(
                key_wait.at[origin, pl.ds(k * half, half), :, low_at],
                temp.at[k, :, :, :, pl.ds(low_at * inner, inner)],
                scatter_sem.at[2 * k + low_at],
            )
            for k in range(2)
            for low_at in range(2)
        ]
        for load in loads:
            load.start()
        for load in loads:
            load.wait()

        @pl.loop(0, half)
        def _(line):
            for k in range(2):
                for high in range(2):
                    for low_at in range(2):
                        mine = key_blocks[k * half + line, high, low_at].astype(F32)
                        mine += temp[
                            k, line, high, :, low_at * inner : (low_at + 1) * inner
                        ].astype(F32)
                        key_blocks[k * half + line, high, low_at] = mine.astype(BF16)

    keys_scatter.first_half()
    finish(query_swap)
    total_query = query_part[...]
    for origin in cores:
        total_query += query_land[origin]
    query_all[...] = total_query.astype(BF16)
    for group in range(GROUPS):
        span = slice(group * SPAN, (group + 1) * SPAN)
        low = dot(latent_norm[...], query_all[:, span], 0, 0)
        for k in range(lines * 4):
            base = k * size * block_rows
            mine = low[base : base + block_rows]
            for core in range(1, size):
                base += block_rows
                mine = jnp.where(me == core, low[base : base + block_rows], mine)
            query_blocks[k // 4, (k // 2) % 2, k % 2, :, span] = mine.astype(BF16)
    query_scatter.first_half()
    for copy in late[5:]:
        copy.wait()

    def back(scores, weights, item, at, count):
        rows = slice(at, at + count)
        return dot(scores[rows], absorbed[item], 1, 0) + dot(weights[rows], into[item], 1, 0)

    row_grad = [
        back(score_full, weight_full, 0, frames * PATCH, local),
        back(score_image, weight_image, 1, PATCH, local),
    ]
    row_grad = jnp.concatenate(row_grad, 0)
    mine = [
        query_all[pl.ds(pl.multiple_of(item * lat_all + me * local, local), local)]
        for item in range(2)
    ]
    mine = jnp.concatenate(mine, 0)
    for group in range(GROUPS):
        if group + 1 < GROUPS:
            column(query_hbm, group + 1).start()
        column(query_hbm, group).wait()
        span = slice(group * SPAN, (group + 1) * SPAN)
        row_grad += dot(mine[:, span], column_weight[group % 2], 1, 1)
    own = jnp.concatenate(
        in_order(first_full, (latents[0].astype(F32), latents[1].astype(F32))), 0
    )
    unit, inverse = normalize(own)
    small[2:3] = jnp.sum(row_grad * unit, 0, keepdims=True)
    small[3:4] = jnp.sum(row_grad, 0, keepdims=True)
    small[4:6] = ffn_gains[...]
    row_grad = state_grad[...] + norm_back(unit, inverse, vector(gain_latent), row_grad)
    for k, value in enumerate(in_order(first_full, (row_grad[:local], row_grad[local:]))):
        latent_grad[k] = value

    gain = vector(gain_media)
    total = Total(place, small, small_land, small_sums)

    def norm_frame(frame, slot, pick_first, target):
        at_time = 6 + me * frames + frame
        time_row = times[pl.ds(me * frames + frame, 1)]

        @pl.loop(0, PATCH // ROWS)
        def _(part):
            at = pl.ds(pl.multiple_of(part * ROWS, ROWS), ROWS)
            values = jnp.where(
                pick_first, buffer[slot, 0, at].astype(F32), buffer[slot, 1, at].astype(F32)
            )
            unit, inverse = normalize(values + time_row)
            grad = block[at]
            rows_grad = norm_back(unit, inverse, gain, grad)
            target[at] = rows_grad.astype(BF16)
            small[0:1] += jnp.sum(grad * unit, 0, keepdims=True)
            small[1:2] += jnp.sum(grad, 0, keepdims=True)
            small[pl.ds(at_time, 1)] += jnp.sum(rows_grad, 0, keepdims=True)

    puts = []
    for k in range(frames + 1):
        frame = max(0, k - 1)
        if k != 1:
            fetch(frame).wait()
        if k >= 1 and frame + 1 < frames:
            fetch(frame + 1).start()
        if k == 0:
            block[...] = back(score_image, weight_image, 1, 0, PATCH)
        else:
            block[...] = back(score_full, weight_full, 0, frame * PATCH, PATCH)
        if k >= 2:
            puts[k - 2].wait()
        picked = jnp.logical_not(first_full) if k == 0 else first_full
        norm_frame(frame, frame % 2, picked, result.at[k % 2])
        puts.append(
            pltpu.make_async_copy(
                result.at[k % 2], slot_grad.at[pl.ds(k * PATCH, PATCH)], result_sem.at[k % 2]
            )
        )
        puts[k].start()
        if k == 0:
            vo.along_line()
        if k == frames // 2:
            keys_scatter.second_half()
    total.in_chip()
    query_scatter.second_half()
    total.low()
    moved.along_line()
    total.high()
    keys_scatter.along_line()
    total.along_line()
    query_scatter.along_line()
    total.end(small_out)
    vo.end()
    moved.end()
    keys_scatter.end()
    query_scatter.end()
    for put in puts[max(0, frames - 1) :]:
        put.wait()


def attend_backward(
    chips,
    size,
    counts,
    media,
    latents,
    gain_media,
    gain_latent,
    shift_latent,
    time_embed,
    query_weight,
    kv_weight,
    norm_full,
    norm_image,
    weight_full,
    weight_image,
    absorbed,
    into,
    value_sum,
    out_half,
    ffn_rows,
    cotangent_rows,
    cotangent_other,
    shifted,
    queries,
    latent_norm,
    state_grad,
    ffn_gains,
    in_share,
    down_share,
):
    width = media.shape[-1]
    inner = HEADS * HEAD_DIM
    lines = chips // 4
    frames = media.shape[1] // PATCH
    local = latents.shape[1]
    block_rows = width // (chips * size)
    blocks = (lines, 2, 2, block_rows, inner)
    share = in_share.shape[1]
    unit = (lines, 2, 2, width // chips, 2 * share)
    small = (6 + time_embed.shape[0] + 7) // 8 * 8
    rows = queries.shape[0]
    shape = jax.ShapeDtypeStruct
    copies = 5 * lines + 10 * size + 24
    return pl.pallas_call(
        functools.partial(backward_kernel, frames, lines, size),
        out_shape=[
            shape(((frames + 1) * PATCH, width), BF16),
            shape(latents.shape, F32),
            shape((block_rows, 2 * inner), F32),
            shape((block_rows, inner), F32),
            shape((block_rows, inner), F32),
            shape(unit, BF16),
            shape((small, width), F32),
            shape((size,) + ffn_rows.shape, BF16),
            shape(unit, BF16),
            shape((size,) + blocks, BF16),
            *Scatter.lands(lines, block_rows, 2 * inner),
            *Scatter.lands(lines, block_rows, inner),
            *Scatter.lands(lines, block_rows, inner),
        ],
        in_specs=[SMEM, ANY] + [VMEM] * 5 + [ANY] * 13 + [VMEM] * 7,
        out_specs=[ANY] + [VMEM] * 4 + [ANY, VMEM] + [ANY] * 12,
        scratch_shapes=[
            pltpu.VMEM((lines, 2, 2, block_rows, 2 * inner), BF16),
            pltpu.VMEM(blocks, BF16),
            pltpu.VMEM(blocks, BF16),
            pltpu.VMEM((2, lines // 2, 2, block_rows, 2 * inner), BF16),
            pltpu.VMEM((2, width, SPAN), BF16),
            pltpu.VMEM(norm_full.shape, BF16),
            pltpu.VMEM(norm_image.shape, BF16),
            pltpu.VMEM(weight_full.shape, BF16),
            pltpu.VMEM(weight_image.shape, BF16),
            pltpu.VMEM(weight_full.shape, BF16),
            pltpu.VMEM(weight_image.shape, BF16),
            pltpu.VMEM(absorbed.shape, BF16),
            pltpu.VMEM(into.shape, BF16),
            pltpu.VMEM((lines, 2, 2, size, block_rows, SPAN), BF16),
            pltpu.VMEM((rows, inner), F32),
            pltpu.VMEM((size, rows, inner), F32),
            pltpu.VMEM((rows, inner), BF16),
            pltpu.VMEM((2, 2, PATCH, width), BF16),
            pltpu.VMEM((2, width, share), F32),
            pltpu.VMEM(unit, BF16),
            pltpu.VMEM((PATCH, width), F32),
            pltpu.VMEM((2, PATCH, width), BF16),
            pltpu.VMEM(time_embed.shape, F32),
            pltpu.VMEM((small, width), F32),
            *Total.scratch(lines, size, (small, width)),
            pltpu.SemaphoreType.DMA((8,)),
            pltpu.SemaphoreType.DMA((2,)),
            pltpu.SemaphoreType.DMA((2, 2, 4)),
            pltpu.SemaphoreType.DMA((2,)),
            pltpu.SemaphoreType.DMA((max(4, lines),)),
            pltpu.SemaphoreType.DMA((2,)),
            pltpu.SemaphoreType.DMA((copies,)),
            pltpu.SemaphoreType.DMA((copies,)),
        ],
        compiler_params=params(collective_id=2, has_side_effects=True),
    )(
        counts,
        media,
        latents,
        gain_media,
        gain_latent,
        shift_latent,
        time_embed,
        query_weight,
        kv_weight,
        norm_full,
        norm_image,
        weight_full,
        weight_image,
        absorbed,
        into,
        value_sum,
        out_half,
        ffn_rows,
        cotangent_rows,
        cotangent_other,
        shifted,
        queries,
        latent_norm,
        state_grad,
        ffn_gains,
        in_share,
        down_share,
    )


def per_device(
    chips,
    size,
    media,
    frame_counts,
    latents,
    norm_media_gain,
    norm_media_shift,
    norm_latent_gain,
    norm_latent_shift,
    time_embed,
    query_weight,
    key_value_weight,
    out_weight,
    ffn_norm_gain,
    ffn_norm_shift,
    ffn_in_weight,
    ffn_out_weight,
    out_cotangent,
):
    dp, me = lax.axis_index("dp"), lax.axis_index("mp")
    width = media.shape[-1]
    share = ffn_in_weight.shape[1] // chips
    in_share = lax.dynamic_slice_in_dim(ffn_in_weight, dp * share, share, 1)
    down_share = lax.dynamic_slice_in_dim(ffn_out_weight, dp * share, share, 0)
    (
        norm_full,
        norm_image,
        weight_full,
        weight_image,
        absorbed,
        mixed,
        value_parts,
        peaks,
        latent_norm,
        queries,
        cotangent_all,
        cotangent_rows,
    ) = attend_forward(
        chips,
        size,
        frame_counts,
        media,
        latents,
        out_cotangent,
        norm_media_gain,
        norm_media_shift,
        norm_latent_gain,
        norm_latent_shift,
        time_embed,
        query_weight,
        key_value_weight,
    )
    (
        latent_out,
        state_grad,
        ffn_gains,
        into,
        shifted,
        value_sum,
        out_half,
        ffn_rows,
        cotangent_other,
        _,
    ) = latent_pass(
        chips,
        size,
        frame_counts,
        value_parts,
        peaks,
        latents,
        cotangent_all,
        ffn_norm_gain,
        ffn_norm_shift,
        out_weight,
        ffn_in_weight,
        ffn_out_weight,
        key_value_weight,
        mixed,
        cotangent_rows,
    )
    slot_grad, latent_grad, value_out_sum, key_sum, query_sum, units, small, *_ = attend_backward(
        chips,
        size,
        frame_counts,
        media,
        latents,
        norm_media_gain,
        norm_latent_gain,
        norm_latent_shift,
        time_embed,
        query_weight,
        key_value_weight,
        norm_full,
        norm_image,
        weight_full,
        weight_image,
        absorbed,
        into,
        value_sum,
        out_half,
        ffn_rows,
        cotangent_rows,
        cotangent_other,
        shifted,
        queries,
        latent_norm,
        state_grad,
        ffn_gains,
        in_share,
        down_share,
    )
    first_full = frame_counts[0] > frame_counts[1]
    full = slot_grad[PATCH:].astype(F32)
    image = jnp.pad(slot_grad[:PATCH].astype(F32), ((0, full.shape[0] - PATCH), (0, 0)))
    media_grad = jnp.stack(
        [jnp.where(first_full, full, image), jnp.where(first_full, image, full)]
    )
    inner = HEADS * HEAD_DIM
    value_weight_sum, out_sum = value_out_sum[:, :inner], value_out_sum[:, inner:].T
    units = units.reshape(chips, width // chips, 2, share).astype(F32)
    up_sum = units[:, :, 0].transpose(1, 0, 2).reshape(width // chips, chips * share)
    down_sum = units[:, :, 1].transpose(0, 2, 1).reshape(chips * share, width // chips)
    place = (dp * size + me) * (width // (chips * size))
    small = lax.dynamic_slice_in_dim(small, place, width // (chips * size), 1)
    return (
        latent_out,
        latent_grad,
        media_grad,
        small[0],
        small[1],
        small[2],
        small[3],
        small[6 : 6 + time_embed.shape[0]],
        query_sum,
        jnp.concatenate([key_sum, value_weight_sum], 1),
        out_sum,
        small[4],
        small[5],
        up_sum,
        down_sum,
    )


def layer_norm(values_in, gain, shift):
    row_mean = jnp.mean(values_in, -1, keepdims=True)
    centered = values_in - row_mean
    variance = jnp.mean(centered * centered, -1, keepdims=True)
    return centered * lax.rsqrt(variance + EPSILON) * gain + shift


def plain_norm_back(values_in, gain, shift, gradient):
    result, pullback = jax.vjp(layer_norm, values_in, gain, shift)
    return pullback(gradient)


def gelu_exact(values_in):
    return jax.nn.gelu(values_in, approximate=False)


def rescale_heads(values_in, factor):
    shaped = values_in.reshape(values_in.shape[:-1] + (factor.shape[-1], -1))
    return (shaped * factor[..., None]).reshape(values_in.shape)


def plain_device(
    media,
    frame_counts,
    latents,
    norm_media_gain,
    norm_media_shift,
    norm_latent_gain,
    norm_latent_shift,
    time_embed,
    query_weight,
    key_value_weight,
    out_weight,
    ffn_norm_gain,
    ffn_norm_shift,
    ffn_in_weight,
    ffn_out_weight,
    out_cotangent,
):
    item_count, local_keys, model_width = media.shape
    latent_local = latents.shape[1]
    inner = HEADS * HEAD_DIM
    frames_local = local_keys // PATCH
    key_count = local_keys + latent_local
    mp_index = lax.axis_index("mp")
    latent_start = mp_index * latent_local
    score_scale = HEAD_DIM ** (-0.5)
    gain_m = norm_media_gain.astype(jnp.float32)
    shift_m = norm_media_shift.astype(jnp.float32)
    gain_l = norm_latent_gain.astype(jnp.float32)
    shift_l = norm_latent_shift.astype(jnp.float32)
    gain_f = ffn_norm_gain.astype(jnp.float32)
    shift_f = ffn_norm_shift.astype(jnp.float32)
    frame_ids = mp_index * frames_local + jnp.arange(frames_local)
    frame_live = frame_ids[None, :] < frame_counts[:, None]
    key_alive = jnp.concatenate(
        [jnp.repeat(frame_live, PATCH, axis=1), jnp.ones((item_count, latent_local), bool)], axis=1
    )
    alive_mask = key_alive[:, None, None, :]
    time_rows = lax.dynamic_slice_in_dim(
        time_embed, mp_index * frames_local, frames_local, 0
    ).astype(jnp.float32)
    with_time = (
        media.astype(jnp.float32).reshape(item_count, frames_local, PATCH, model_width)
        + time_rows[None, :, None, :]
    )
    with_time = with_time.reshape(item_count * local_keys, model_width)
    media_norm = layer_norm(with_time, gain_m, shift_m).astype(jnp.bfloat16)
    latent_in = latents.astype(jnp.float32)
    latent_norm = layer_norm(latent_in, gain_l, shift_l).astype(jnp.bfloat16)
    media_kv = jnp.dot(media_norm, key_value_weight, preferred_element_type=jnp.float32).astype(
        jnp.bfloat16
    )
    latent_kv = jnp.einsum(
        "ild,de->ile", latent_norm, key_value_weight, preferred_element_type=jnp.float32
    ).astype(jnp.bfloat16)
    keys_values = jnp.concatenate(
        [media_kv.reshape(item_count, local_keys, 2 * inner), latent_kv], axis=1
    )
    key_heads = keys_values[..., :inner].reshape(item_count, key_count, HEADS, HEAD_DIM)
    value_heads = keys_values[..., inner:].reshape(item_count, key_count, HEADS, HEAD_DIM)
    query_own = jnp.einsum(
        "ild,de->ile", latent_norm, query_weight, preferred_element_type=jnp.float32
    ).astype(jnp.bfloat16)
    queries = lax.all_gather(query_own, "mp", axis=1, tiled=True)
    lat_all = queries.shape[1]
    query_heads = queries.reshape(item_count, lat_all, HEADS, HEAD_DIM)
    scores = (
        jnp.einsum("iqhd,ikhd->ihqk", query_heads, key_heads, preferred_element_type=jnp.float32)
        * score_scale
    )
    masked = jnp.where(alive_mask, scores, -1e30)
    peak_score = jnp.max(masked, -1)
    weights = jnp.where(alive_mask, jnp.exp(masked - peak_score[..., None]), 0.0)
    weight_sum = jnp.sum(weights, -1).transpose(0, 2, 1)
    peak_score = peak_score.transpose(0, 2, 1)
    numerator = jnp.einsum(
        "ihqk,ikhd->iqhd",
        weights.astype(jnp.bfloat16),
        value_heads,
        preferred_element_type=jnp.float32,
    ).reshape(item_count, lat_all, inner)
    peak_all = lax.pmax(peak_score, "mp")
    factor = jnp.exp(peak_score - peak_all)
    weight_own, numerator_own = (
        lax.psum_scatter(weight_sum * factor, "mp", scatter_dimension=1, tiled=True),
        lax.psum_scatter(rescale_heads(numerator, factor), "mp", scatter_dimension=1, tiled=True),
    )
    peak_own = lax.dynamic_slice_in_dim(peak_all, latent_start, latent_local, 1)
    log_sum_own = peak_own + jnp.log(weight_own)
    attended_exact = rescale_heads(numerator_own, 1.0 / weight_own)
    attended_low = attended_exact.astype(jnp.bfloat16)
    update = jnp.einsum("ile,ed->ild", attended_low, out_weight, preferred_element_type=jnp.float32)
    hidden_state = latent_in + update
    ffn_norm = layer_norm(hidden_state, gain_f, shift_f).astype(jnp.bfloat16)
    ffn_norm_rows = ffn_norm.transpose(1, 0, 2)
    gathered = lax.all_gather(ffn_norm_rows, "mp", axis=0, tiled=True)
    pre_act = jnp.einsum("lid,df->lif", gathered, ffn_in_weight, preferred_element_type=jnp.float32)
    activated = gelu_exact(pre_act).astype(jnp.bfloat16)
    ffn_norm_all = gathered
    block = activated
    ffn_result = lax.psum_scatter(
        jnp.einsum("lif,fd->lid", block, ffn_out_weight, preferred_element_type=jnp.float32),
        "mp",
        scatter_dimension=0,
        tiled=True,
    )
    latent_out = (hidden_state + ffn_result.transpose(1, 0, 2)).astype(jnp.bfloat16)
    cotangent_rows = out_cotangent.transpose(1, 0, 2)
    gathered = lax.all_gather(cotangent_rows, "mp", axis=0, tiled=True)
    act_grad = jnp.einsum(
        "lid,fd->lif", gathered, ffn_out_weight, preferred_element_type=jnp.float32
    )
    result, pullback = jax.vjp(gelu_exact, pre_act)
    pre_grad = pullback(act_grad)[0].astype(jnp.bfloat16)
    ffn_down_grad = jnp.einsum(
        "lif,lid->fd", activated, gathered, preferred_element_type=jnp.float32
    )
    ffn_up_grad = jnp.einsum(
        "lid,lif->df", ffn_norm_all, pre_grad, preferred_element_type=jnp.float32
    )
    block = pre_grad
    ffn_norm_grad = lax.psum_scatter(
        jnp.einsum("lif,df->lid", block, ffn_in_weight, preferred_element_type=jnp.float32),
        "mp",
        scatter_dimension=0,
        tiled=True,
    ).transpose(1, 0, 2)
    state_part, gain_f_grad, shift_f_grad = plain_norm_back(hidden_state, gain_f, shift_f, ffn_norm_grad)
    state_grad = out_cotangent.astype(jnp.float32) + state_part
    update_grad = state_grad.astype(jnp.bfloat16)
    out_grad_local = jnp.einsum(
        "ile,ild->ed", attended_low, update_grad, preferred_element_type=jnp.float32
    )
    attended_grad = jnp.einsum(
        "ild,ed->ile", update_grad, out_weight, preferred_element_type=jnp.float32
    ).astype(jnp.bfloat16)
    row_delta = jnp.sum(
        (attended_grad.astype(jnp.float32) * attended_exact).reshape(
            item_count, latent_local, HEADS, HEAD_DIM
        ),
        -1,
    )
    grad_all, delta_all, log_sum_all = (
        lax.all_gather(attended_grad.astype(jnp.float32), "mp", axis=1, tiled=True),
        lax.all_gather(row_delta, "mp", axis=1, tiled=True),
        lax.all_gather(log_sum_own, "mp", axis=1, tiled=True),
    )
    grad_heads = grad_all.astype(jnp.bfloat16).reshape(item_count, lat_all, HEADS, HEAD_DIM)
    scores_again = (
        jnp.einsum("iqhd,ikhd->ihqk", query_heads, key_heads, preferred_element_type=jnp.float32)
        * score_scale
    )
    probability = jnp.where(
        alive_mask, jnp.exp(scores_again - log_sum_all.transpose(0, 2, 1)[..., None]), 0.0
    )
    prob_grad = jnp.einsum(
        "iqhd,ikhd->ihqk", grad_heads, value_heads, preferred_element_type=jnp.float32
    )
    score_grad = (probability * (prob_grad - delta_all.transpose(0, 2, 1)[..., None])).astype(
        jnp.bfloat16
    )
    query_part_grad = (
        jnp.einsum("ihqk,ikhd->iqhd", score_grad, key_heads, preferred_element_type=jnp.float32)
        * score_scale
    ).reshape(item_count, lat_all, inner)
    key_grad = (
        jnp.einsum("ihqk,iqhd->ikhd", score_grad, query_heads, preferred_element_type=jnp.float32)
        * score_scale
    )
    value_grad = jnp.einsum(
        "ihqk,iqhd->ikhd",
        probability.astype(jnp.bfloat16),
        grad_heads,
        preferred_element_type=jnp.float32,
    )
    kv_grad = jnp.concatenate(
        [
            key_grad.reshape(item_count, key_count, inner),
            value_grad.reshape(item_count, key_count, inner),
        ],
        -1,
    ).astype(jnp.bfloat16)
    query_grad = lax.psum_scatter(query_part_grad, "mp", scatter_dimension=1, tiled=True).astype(
        jnp.bfloat16
    )
    media_kv_grad = kv_grad[:, :local_keys].reshape(item_count * local_keys, 2 * inner)
    latent_kv_grad = kv_grad[:, local_keys:]
    kv_weight_local = jnp.einsum(
        "rd,re->de", media_norm, media_kv_grad, preferred_element_type=jnp.float32
    ) + jnp.einsum("ild,ile->de", latent_norm, latent_kv_grad, preferred_element_type=jnp.float32)
    query_weight_local = jnp.einsum(
        "ild,ile->de", latent_norm, query_grad, preferred_element_type=jnp.float32
    )
    media_norm_grad = jnp.einsum(
        "re,de->rd", media_kv_grad, key_value_weight, preferred_element_type=jnp.float32
    )
    latent_norm_grad = jnp.einsum(
        "ile,de->ild", latent_kv_grad, key_value_weight, preferred_element_type=jnp.float32
    ) + jnp.einsum("ile,de->ild", query_grad, query_weight, preferred_element_type=jnp.float32)
    media_pre_grad, gain_m_grad, shift_m_grad = plain_norm_back(
        with_time, gain_m, shift_m, media_norm_grad
    )
    latent_part, gain_l_grad, shift_l_grad = plain_norm_back(latent_in, gain_l, shift_l, latent_norm_grad)
    latent_grad = state_grad + latent_part
    media_grad = media_pre_grad.reshape(item_count, local_keys, model_width)
    time_local = jnp.sum(
        media_pre_grad.reshape(item_count, frames_local, PATCH, model_width), (0, 2)
    )
    time_grad = lax.dynamic_update_slice_in_dim(
        jnp.zeros((time_embed.shape[0], model_width), jnp.float32),
        time_local,
        mp_index * frames_local,
        0,
    )
    small_grads = jnp.concatenate(
        [
            jnp.stack(
                [gain_m_grad, shift_m_grad, gain_l_grad, shift_l_grad, gain_f_grad, shift_f_grad], 1
            ),
            time_grad.T,
        ],
        1,
    )
    query_sum, kv_sum, out_sum, small_sum = (
        lax.psum_scatter(query_weight_local, ("dp", "mp"), scatter_dimension=0, tiled=True),
        lax.psum_scatter(kv_weight_local, ("dp", "mp"), scatter_dimension=0, tiled=True),
        lax.psum_scatter(out_grad_local.T, ("dp", "mp"), scatter_dimension=0, tiled=True),
        lax.psum_scatter(small_grads, ("dp", "mp"), scatter_dimension=0, tiled=True),
    )
    ffn_up_sum, ffn_down_sum = (
        lax.psum_scatter(ffn_up_grad, "dp", scatter_dimension=0, tiled=True),
        lax.psum_scatter(ffn_down_grad.T, "dp", scatter_dimension=0, tiled=True),
    )
    return (
        latent_out,
        latent_grad,
        media_grad,
        small_sum[:, 0],
        small_sum[:, 1],
        small_sum[:, 2],
        small_sum[:, 3],
        small_sum[:, 6:].T,
        query_sum,
        kv_sum,
        out_sum.T,
        small_sum[:, 4],
        small_sum[:, 5],
        ffn_up_sum,
        ffn_down_sum.T,
    )


def solution(mesh):
    placed = (
        P("dp", "mp", None),
        P("dp"),
        P("dp", "mp", None),
        P(),
        P(),
        P(),
        P(),
        P(),
        P(),
        P(),
        P(),
        P(),
        P(),
        P(None, "mp"),
        P("mp", None),
        P("dp", "mp", None),
    )
    chips, size = mesh.shape["dp"], mesh.shape["mp"]

    def device(*arrays):
        tiled = arrays[0].shape[-1] % (chips * size * 16) == 0 and arrays[2].shape[1] % 16 == 0
        if tiled and chips % 8 == 0:
            return per_device(chips, size, *arrays)
        return plain_device(*arrays)

    return jax.shard_map(
        device,
        mesh=mesh,
        in_specs=placed,
        out_specs=(
            P("dp", "mp", None),
            P("dp", "mp", None),
            P("dp", "mp", None),
            P(("dp", "mp")),
            P(("dp", "mp")),
            P(("dp", "mp")),
            P(("dp", "mp")),
            P(None, ("dp", "mp")),
            P(("dp", "mp"), None),
            P(("dp", "mp"), None),
            P(None, ("dp", "mp")),
            P(("dp", "mp")),
            P(("dp", "mp")),
            P("dp", "mp"),
            P("mp", "dp"),
        ),
        check_vma=False,
    )
```

```python
import functools

import jax
import jax.numpy as jnp
from jax import lax
from jax.experimental import pallas as pl
from jax.experimental.pallas import tpu as pltpu
from jax.sharding import PartitionSpec as P

HEADS = 16
HEAD_DIM = 96
PATCH = 256
GROUP = 4
SPAN = GROUP * HEAD_DIM
GROUPS = HEADS // GROUP
LATENT_PAD = 32
EPSILON = 1e-05
SCALE = HEAD_DIM ** (-0.5)
F32 = jnp.float32
BF16 = jnp.bfloat16
MESH = pl.DeviceIdType.MESH
VMEM_LIMIT = 60 * 1024 * 1024

VMEM = pl.BlockSpec(memory_space=pltpu.VMEM)
SMEM = pl.BlockSpec(memory_space=pltpu.SMEM)
ANY = pl.BlockSpec(memory_space=pl.ANY)


def dot(left, right, left_axis, right_axis):
    return lax.dot_general(
        left,
        right,
        (((left_axis,), (right_axis,)), ((), ())),
        preferred_element_type=F32,
    )


def normalize(rows):
    mean = jnp.mean(rows, -1, keepdims=True)
    centered = rows - mean
    variance = jnp.mean(centered * centered, -1, keepdims=True)
    inverse = lax.rsqrt(variance + EPSILON)
    return centered * inverse, inverse


def norm_back(unit, inverse, gain, gradient):
    scaled = gradient * gain
    return inverse * (
        scaled
        - jnp.mean(scaled, -1, keepdims=True)
        - unit * jnp.mean(scaled * unit, -1, keepdims=True)
    )


def lane_head(rows):
    column = lax.broadcasted_iota(jnp.int32, (rows, SPAN), 1)
    head = jnp.zeros((rows, SPAN), jnp.int32)
    for h in range(1, GROUP):
        head += (column >= h * HEAD_DIM).astype(jnp.int32)
    return head


def spread_heads(rows):
    head = lane_head(rows.shape[0])
    zero = jnp.zeros_like(rows)
    return jnp.concatenate([jnp.where(head == h, rows, zero) for h in range(GROUP)], 0)


def fold_heads(rows):
    count = rows.shape[0] // GROUP
    head = lane_head(count)
    total = jnp.zeros((count, SPAN), F32)
    for h in range(GROUP):
        total += jnp.where(head == h, rows[h * count : (h + 1) * count], 0.0)
    return total


def dot_exact(left, selector):
    total = None
    for _ in range(3):
        term = left.astype(BF16)
        left = left - term.astype(F32)
        part = dot(term, selector, 1, 0)
        total = part if total is None else total + part
    return total


def head_selector():
    low = lax.broadcasted_iota(jnp.int32, (128, HEADS * HEAD_DIM), 0) * HEAD_DIM
    column = lax.broadcasted_iota(jnp.int32, (128, HEADS * HEAD_DIM), 1)
    return ((column >= low) & (column < low + HEAD_DIM)).astype(F32).astype(BF16)


def head_sums(rows):
    count = rows.shape[0]
    head = lane_head(count)
    lane = lax.broadcasted_iota(jnp.int32, (count, 128), 1)
    result = jnp.zeros((count, 128), F32)
    for group in range(GROUPS):
        span = rows[:, group * SPAN : (group + 1) * SPAN]
        for h in range(GROUP):
            total = jnp.sum(jnp.where(head == h, span, 0.0), 1, keepdims=True)
            result += jnp.where(lane == group * GROUP + h, total, 0.0)
    return result


def own_columns(rows, head):
    lane = lax.broadcasted_iota(jnp.int32, rows.shape, 1)
    return jnp.sum(jnp.where(lane == head, rows, 0.0), 1, keepdims=True)


def across_lanes(column):
    return jnp.transpose(jnp.broadcast_to(column, (column.shape[0], 128)))[0:1]


def down_rows(row):
    return jnp.transpose(jnp.broadcast_to(row, (128, row.shape[1])))


def vector(ref):
    return ref[...].astype(F32).reshape(1, ref.shape[-1])


def gelu_parts(pre):
    cdf = 0.5 * (1.0 + lax.erf(pre * (0.5**0.5)))
    return pre * cdf, cdf + pre * (jnp.exp(-0.5 * pre * pre) * 0.3989422804014327)


def params(**more):
    return pltpu.CompilerParams(vmem_limit_bytes=VMEM_LIMIT, **more)


def greet(devices):
    barrier = pltpu.get_barrier_semaphore()
    for device in devices:
        pl.semaphore_signal(barrier, inc=1, device_id=device, device_id_type=MESH)
    pl.semaphore_wait(barrier, len(devices))


def others(axis_size, me):
    return [lax.rem(me + k, axis_size) for k in range(1, axis_size)]


class Place:
    def __init__(self, lines, size, send_sem, recv_sem):
        self.lines, self.size = lines, size
        self.dp, self.me = lax.axis_index("dp"), lax.axis_index("mp")
        self.line = self.dp // 4
        self.high = lax.rem(self.dp // 2, 2)
        self.low = lax.rem(self.dp, 2)
        self.send_sem, self.recv_sem = send_sem, recv_sem
        self.used = 0

    def at(self, line, high, low):
        return (line * 4 + high * 2 + low, self.me)

    def low_peer(self):
        return self.at(self.line, self.high, 1 - self.low)

    def high_peer(self):
        return self.at(self.line, 1 - self.high, self.low)

    def across(self):
        return self.at(self.line, 1 - self.high, 1 - self.low)

    def greet(self):
        greet(
            [self.low_peer(), self.high_peer(), self.across()]
            + [self.at(peer, self.high, self.low) for peer in others(self.lines, self.line)]
            + [(self.dp, peer) for peer in others(self.size, self.me)]
        )

    def exchange(self, source, target, land, device):
        index = self.used
        self.used += 1

        def copy(destination):
            return pltpu.make_async_remote_copy(
                src_ref=source,
                dst_ref=destination,
                send_sem=self.send_sem.at[index],
                recv_sem=self.recv_sem.at[index],
                device_id=device,
                device_id_type=MESH,
            )

        pair = (copy(target), copy(land))
        pair[0].start()
        return pair

    def swap(self, me, count, device_of, source_of, land_of):
        pairs = []
        for k in range(1, count):
            peer, origin = lax.rem(me + k, count), lax.rem(me + count - k, count)
            pairs.append(
                self.exchange(source_of(peer), land_of(me), land_of(origin), device_of(peer))
            )
        return pairs

    def swap_cores(self, source_of, land_of):
        return self.swap(self.me, self.size, lambda p: (self.dp, p), source_of, land_of)

    def swap_lines(self, source_of, land_of):
        return self.swap(
            self.line, self.lines, lambda p: self.at(p, self.high, self.low), source_of, land_of
        )


def finish_sends(pairs):
    for copy, _ in pairs:
        copy.wait_send()


def finish_arrivals(pairs):
    for _, arrival in pairs:
        arrival.wait_recv()


def finish(pairs):
    finish_arrivals(pairs)
    finish_sends(pairs)


class Gather:
    def __init__(self, place, rows, out, sem):
        self.place, self.rows, self.out, self.sem = place, rows, out, sem

    def along_line(self):
        p, out = self.place, self.out
        self.keep = pltpu.make_async_copy(
            self.rows, out.at[p.line, p.high, p.low], self.sem
        )
        self.keep.start()
        self.pairs = p.swap_lines(
            lambda peer: self.rows, lambda line: out.at[line, p.high, p.low]
        )

    def first_half(self):
        p, out = self.place, self.out
        self.keep.wait()
        finish(self.pairs)
        half = p.lines // 2
        near, far = pl.ds(0, half), pl.ds(half, p.lines - half)
        self.pairs = [
            p.exchange(
                out.at[near, p.high, p.low],
                out.at[near, p.high, p.low],
                out.at[near, p.high, 1 - p.low],
                p.low_peer(),
            ),
            p.exchange(
                out.at[far, p.high, p.low],
                out.at[far, p.high, p.low],
                out.at[far, 1 - p.high, p.low],
                p.high_peer(),
            ),
        ]

    def second_half(self):
        p, out = self.place, self.out
        finish(self.pairs)
        half = p.lines // 2
        near, far = pl.ds(0, half), pl.ds(half, p.lines - half)
        self.pairs = [
            p.exchange(
                out.at[near, p.high],
                out.at[near, p.high],
                out.at[near, 1 - p.high],
                p.high_peer(),
            ),
            p.exchange(
                out.at[far, :, p.low],
                out.at[far, :, p.low],
                out.at[far, :, 1 - p.low],
                p.low_peer(),
            ),
        ]

    def end(self):
        finish(self.pairs)


class Scatter:
    def __init__(self, place, blocks, lands, temp, sem, out):
        self.place, self.blocks, self.lands, self.out = place, blocks, lands, out
        self.temp, self.sem = temp, sem

    @staticmethod
    def lands(lines, rows, columns):
        half = lines // 2
        return [
            jax.ShapeDtypeStruct((2, half, 2, rows, columns), BF16),
            jax.ShapeDtypeStruct((2, half, rows, columns), BF16),
            jax.ShapeDtypeStruct((lines, rows, columns), BF16),
        ]

    def load(self, pairs):
        copies = [
            pltpu.make_async_copy(source, target, self.sem.at[k])
            for k, (source, target) in enumerate(pairs)
        ]
        for copy in copies:
            copy.start()
        for copy in copies:
            copy.wait()

    def first_half(self):
        p, blocks, land = self.place, self.blocks, self.lands[0]
        half = p.lines // 2
        near, far = pl.ds(0, half), pl.ds(half, half)
        self.pairs = [
            p.exchange(blocks.at[near, :, 1 - p.low], land.at[0], land.at[0], p.low_peer()),
            p.exchange(blocks.at[far, 1 - p.high], land.at[1], land.at[1], p.high_peer()),
        ]

    def second_half(self):
        p, blocks, land, into, temp = self.place, self.blocks, *self.lands[:2], self.temp
        half = p.lines // 2
        near, far = pl.ds(0, half), pl.ds(half, half)
        finish(self.pairs)
        self.load([(land.at[k], temp.at[k, :, :, 0]) for k in range(2)])

        @pl.loop(0, half)
        def _(line):
            for k in range(2):
                mine = blocks[line, k, p.low].astype(F32) + temp[0, line, k, 0].astype(F32)
                blocks[line, k, p.low] = mine.astype(BF16)
                mine = blocks[half + line, p.high, k].astype(F32) + temp[1, line, k, 0].astype(F32)
                blocks[half + line, p.high, k] = mine.astype(BF16)

        self.pairs = [
            p.exchange(blocks.at[near, 1 - p.high, p.low], into.at[0], into.at[0], p.high_peer()),
            p.exchange(blocks.at[far, p.high, 1 - p.low], into.at[1], into.at[1], p.low_peer()),
        ]

    def mine(self, line):
        return self.blocks.at[line, self.place.high, self.place.low]

    def plane_sum(self):
        p, blocks, temp, into = self.place, self.blocks, self.temp, self.lands[1]
        half = p.lines // 2
        finish(self.pairs)
        self.load([(into.at[k], temp.at[k, :, 0, 0]) for k in range(2)])

        @pl.loop(0, half)
        def _(line):
            for k in range(2):
                mine = blocks[k * half + line, p.high, p.low].astype(F32)
                mine += temp[k, line, 0, 0].astype(F32)
                blocks[k * half + line, p.high, p.low] = mine.astype(BF16)

    def send_line(self):
        land = self.lands[2]
        self.pairs = self.place.swap_lines(self.mine, lambda line: land.at[line])

    def end(self):
        p, land, temp = self.place, self.lands[2], self.temp
        half = p.lines // 2
        finish(self.pairs)
        peers = others(p.lines, p.line)
        self.load(
            [(land.at[peer], temp.at[k // half, k % half, 0, 0]) for k, peer in enumerate(peers)]
        )
        total = self.mine(p.line)[...].astype(F32)
        for k in range(len(peers)):
            total += temp[k // half, k % half, 0, 0].astype(F32)
        self.out[...] = total


class LineSum(Scatter):
    def mine(self, line):
        return self.blocks.at[line]


class Move:
    def __init__(self, place, blocks, middle, out, sem):
        self.place, self.blocks, self.middle, self.out, self.sem = place, blocks, middle, out, sem

    def along_line(self):
        p, blocks, middle = self.place, self.blocks, self.middle
        self.keep = pltpu.make_async_copy(blocks.at[p.line], middle.at[p.line], self.sem.at[0])
        self.keep.start()
        self.pairs = p.swap_lines(lambda peer: blocks.at[peer], lambda line: middle.at[line])

    def in_plane(self):
        p, middle, out = self.place, self.middle, self.out
        self.keep.wait()
        finish(self.pairs)
        self.keep = pltpu.make_async_copy(
            middle.at[:, p.high, p.low], out.at[:, p.high, p.low], self.sem.at[1]
        )
        self.keep.start()
        self.pairs = []
        for device, high, low in (
            (p.low_peer(), p.high, 1 - p.low),
            (p.high_peer(), 1 - p.high, p.low),
            (p.across(), 1 - p.high, 1 - p.low),
        ):
            self.pairs.append(
                p.exchange(
                    middle.at[:, high, low],
                    out.at[:, p.high, p.low],
                    out.at[:, high, low],
                    device,
                )
            )

    def end(self):
        self.keep.wait()
        finish(self.pairs)


class Total:
    def __init__(self, place, array, land, sums):
        self.place, self.array, self.land, self.sums = place, array, land, sums

    @staticmethod
    def scratch(lines, size, shape):
        return [pltpu.VMEM((size + 2 + lines,) + shape, F32), pltpu.VMEM((3,) + shape, F32)]

    def in_chip(self):
        self.pairs = self.place.swap_cores(lambda peer: self.array, lambda core: self.land.at[core])

    def low(self):
        p = self.place
        finish(self.pairs)
        total = self.array[...]
        for peer in others(p.size, p.me):
            total += self.land[peer]
        self.sums[0] = total
        land = self.land.at[p.size]
        self.pairs = [p.exchange(self.sums.at[0], land, land, p.low_peer())]

    def high(self):
        p = self.place
        finish(self.pairs)
        self.sums[1] = self.sums[0] + self.land[p.size]
        land = self.land.at[p.size + 1]
        self.pairs = [p.exchange(self.sums.at[1], land, land, p.high_peer())]

    def along_line(self):
        p = self.place
        finish(self.pairs)
        self.sums[2] = self.sums[1] + self.land[p.size + 1]
        self.pairs = p.swap_lines(
            lambda peer: self.sums.at[2], lambda line: self.land.at[p.size + 2 + line]
        )

    def end(self, out):
        p = self.place
        finish(self.pairs)
        total = self.sums[2]
        for peer in others(p.lines, p.line):
            total += self.land[p.size + 2 + peer]
        out[...] = total


ROWS = 64


def in_order(first_full, pair):
    return jnp.where(first_full, pair[0], pair[1]), jnp.where(first_full, pair[1], pair[0])


def forward_kernel(
    frames,
    lines,
    size,
    counts,
    media,
    latents,
    cotangent,
    gain_media,
    shift_media,
    gain_latent,
    shift_latent,
    time_embed,
    query_hbm,
    kv_hbm,
    norm_full_out,
    norm_image_out,
    weight_full_out,
    weight_image_out,
    absorbed_out,
    mixed_out,
    value_out,
    peak_out,
    latent_norm,
    queries,
    cotangent_all,
    cotangent_rows,
    own,
    latent_all,
    norm_full,
    norm_image,
    weight_full,
    weight_image,
    absorbed,
    mixed,
    query_weight,
    kv_weight,
    buffer,
    times,
    media_sem,
    load_sem,
    store_sem,
    gather_sem,
    send_sem,
    recv_sem,
):
    inner = HEADS * HEAD_DIM
    place = Place(lines, size, send_sem, recv_sem)
    me = place.me
    local = latents.shape[1]
    rows = 2 * local
    lat_all = local * size
    first_full = counts[0] > counts[1]
    image_alive = me * frames < jnp.minimum(counts[0], counts[1])

    def fetch(frame, slot):
        return pltpu.make_async_copy(
            media.at[:, pl.ds(frame * PATCH, PATCH)], buffer.at[slot], media_sem.at[slot]
        )

    load_query = pltpu.make_async_copy(query_hbm, query_weight, load_sem.at[0])
    load_kv = pltpu.make_async_copy(kv_hbm, kv_weight, load_sem.at[1])
    times[...] = time_embed[...].astype(F32)
    fetch(0, 0).start()
    load_query.start()
    load_kv.start()
    place.greet()
    for k, array in ((0, latents), (1, cotangent)):
        pair = in_order(first_full, (array[0].astype(F32), array[1].astype(F32)))
        own[k] = jnp.concatenate(pair, 0).astype(BF16)
    latent_swap = place.swap_cores(lambda p: own.at[0], lambda c: latent_all.at[c])
    cotangent_swap = place.swap_cores(lambda p: own.at[1], lambda c: cotangent_all.at[c])
    gather = Gather(place, own.at[1], cotangent_rows, gather_sem.at[0])
    gather.along_line()
    latent_all[me] = own[0]
    cotangent_all[me] = own[1]

    gain_m, shift_m = vector(gain_media), vector(shift_media)
    gain_l, shift_l = vector(gain_latent), vector(shift_latent)

    def normalize_frame(frame, slot, pick_first, target, base):
        time_row = times[pl.ds(me * frames + frame, 1)]

        @pl.loop(0, PATCH // ROWS)
        def _(part):
            at = pl.multiple_of(part * ROWS, ROWS)
            values = jnp.where(
                pick_first,
                buffer[slot, 0, pl.ds(at, ROWS)].astype(F32),
                buffer[slot, 1, pl.ds(at, ROWS)].astype(F32),
            )
            unit, _ = normalize(values + time_row)
            target[pl.ds(pl.multiple_of(base + at, ROWS), ROWS)] = (unit * gain_m + shift_m).astype(
                BF16
            )

    @pl.loop(0, frames)
    def _(frame):
        slot = lax.rem(frame, 2)
        fetch(frame, slot).wait()

        @pl.when(frame + 1 < frames)
        def _():
            fetch(frame + 1, 1 - slot).start()

        normalize_frame(frame, slot, first_full, norm_full, frame * PATCH)

        @pl.when(frame == 0)
        def _():
            normalize_frame(frame, slot, jnp.logical_not(first_full), norm_image, 0)

    unit, _ = normalize(own[0].astype(F32))
    low = (unit * gain_l + shift_l).astype(BF16)
    norm_full[frames * PATCH : frames * PATCH + local] = low[:local]
    norm_image[PATCH : PATCH + local] = low[local:]
    finish(latent_swap)
    for item in range(2):
        for core in range(size):
            unit, _ = normalize(latent_all[core, item * local : (item + 1) * local].astype(F32))
            at = item * lat_all + core * local
            latent_norm[at : at + local] = (unit * gain_l + shift_l).astype(BF16)
    stores = []

    def store(source, target):
        copy = pltpu.make_async_copy(source, target, store_sem.at[len(stores)])
        copy.start()
        stores.append(copy)

    store(norm_full, norm_full_out)
    store(norm_image, norm_image_out)
    load_query.wait()

    @pl.loop(0, GROUPS)
    def _(group):
        span = pl.ds(pl.multiple_of(group * SPAN, SPAN), SPAN)
        queries[:, span] = dot(latent_norm[...], query_weight[:, span], 1, 0).astype(BF16)

    load_kv.wait()
    step = GROUP * lat_all
    lane = lax.broadcasted_iota(jnp.int32, (lat_all, 128), 1)
    outer_lane = lax.broadcasted_iota(jnp.int32, (rows, 128), 1)
    for core in range(size):
        peak_out[core, 0] = jnp.zeros((rows, 128), F32)
        peak_out[core, 1] = jnp.where(outer_lane < HEADS, 0.0, 1.0)
    for item, keys, weights, weights_out in (
        (0, norm_full, weight_full, weight_full_out),
        (1, norm_image, weight_image, weight_image_out),
    ):
        count = keys.shape[0]
        row = lax.broadcasted_iota(jnp.int32, (count, 1), 0)
        live = (row >= count - local) | image_alive

        def attend_group(group, item=item, keys=keys, weights=weights, live=live):
            span = pl.ds(pl.multiple_of(group * SPAN, SPAN), SPAN)
            value_span = pl.ds(pl.multiple_of(inner + group * SPAN, SPAN), SPAN)
            at = pl.ds(pl.multiple_of(group * step, step), step)
            spread = spread_heads(queries[item * lat_all : (item + 1) * lat_all, span])
            key_rows = (dot(spread, kv_weight[:, span], 1, 1) * SCALE).astype(BF16)
            absorbed[item, at] = key_rows
            scores = dot(keys[...], key_rows, 1, 1)
            if item == 1:
                scores = jnp.where(live, scores, -1e30)
            peak = jnp.max(scores, 0, keepdims=True)
            weight = jnp.exp(scores - peak)
            if item == 1:
                weight = jnp.where(live, weight, 0.0)
            total = jnp.sum(weight, 0, keepdims=True)
            low = weight.astype(BF16)
            weights[:, at] = low
            mix = dot(low, keys[...], 0, 0).astype(BF16)
            mixed[item, at] = mix
            values = fold_heads(dot(mix, kv_weight[:, value_span], 1, 0))
            statistics = []
            for row_values in (peak, total):
                down = down_rows(row_values)
                picked = jnp.zeros((lat_all, 128), F32)
                for h in range(GROUP):
                    rows_of_head = down[h * lat_all : (h + 1) * lat_all]
                    picked += jnp.where(lane == group * GROUP + h, rows_of_head, 0.0)
                statistics.append(picked)
            for core in range(size):
                mine = slice(core * local, (core + 1) * local)
                into = slice(item * local, (item + 1) * local)
                value_out[core, into, span] = values[mine]
                for k in range(2):
                    peak_out[core, k, into] += statistics[k][mine]

        if item == 0:
            pl.loop(0, 1)(attend_group)
            gather.first_half()
            pl.loop(1, GROUPS - 1)(attend_group)
            gather.second_half()
            pl.loop(GROUPS - 1, GROUPS)(attend_group)
        else:
            pl.loop(0, GROUPS)(attend_group)
        store(weights, weights_out)
        store(absorbed.at[item], absorbed_out.at[item])
        store(mixed.at[item], mixed_out.at[item])
    for copy in stores:
        copy.wait()
    finish(cotangent_swap)
    gather.end()


def attend_forward(
    chips,
    size,
    counts,
    media,
    latents,
    cotangent,
    gain_media,
    shift_media,
    gain_latent,
    shift_latent,
    time_embed,
    query_weight,
    kv_weight,
):
    width = media.shape[-1]
    inner = HEADS * HEAD_DIM
    lines = chips // 4
    frames = media.shape[1] // PATCH
    local = latents.shape[1]
    rows = 2 * local
    lat_all = local * size
    keys = (frames * PATCH + local, PATCH + local)
    slots = HEADS * lat_all
    shape = jax.ShapeDtypeStruct
    copies = lines + 2 * size + 8
    return pl.pallas_call(
        functools.partial(forward_kernel, frames, lines, size),
        out_shape=[
            shape((keys[0], width), BF16),
            shape((keys[1], width), BF16),
            shape((keys[0], slots), BF16),
            shape((keys[1], slots), BF16),
            shape((2, slots, width), BF16),
            shape((2, slots, width), BF16),
            shape((size, rows, inner), F32),
            shape((size, 2, rows, 128), F32),
            shape((2 * lat_all, width), BF16),
            shape((2 * lat_all, inner), BF16),
            shape((size, rows, width), BF16),
            shape((lines, 2, 2, rows, width), BF16),
        ],
        in_specs=[SMEM, ANY] + [VMEM] * 7 + [ANY] * 2,
        out_specs=[ANY] * 6 + [VMEM] * 5 + [ANY],
        scratch_shapes=[
            pltpu.VMEM((2, rows, width), BF16),
            pltpu.VMEM((size, rows, width), BF16),
            pltpu.VMEM((keys[0], width), BF16),
            pltpu.VMEM((keys[1], width), BF16),
            pltpu.VMEM((keys[0], slots), BF16),
            pltpu.VMEM((keys[1], slots), BF16),
            pltpu.VMEM((2, slots, width), BF16),
            pltpu.VMEM((2, slots, width), BF16),
            pltpu.VMEM(query_weight.shape, BF16),
            pltpu.VMEM(kv_weight.shape, BF16),
            pltpu.VMEM((2, 2, PATCH, width), BF16),
            pltpu.VMEM(time_embed.shape, F32),
            pltpu.SemaphoreType.DMA((2,)),
            pltpu.SemaphoreType.DMA((2,)),
            pltpu.SemaphoreType.DMA((8,)),
            pltpu.SemaphoreType.DMA((1,)),
            pltpu.SemaphoreType.DMA((copies,)),
            pltpu.SemaphoreType.DMA((copies,)),
        ],
        compiler_params=params(collective_id=0, has_side_effects=True),
    )(
        counts,
        media,
        latents,
        cotangent,
        gain_media,
        shift_media,
        gain_latent,
        shift_latent,
        time_embed,
        query_weight,
        kv_weight,
    )


DEPTH = 2


def latent_kernel(
    lines,
    size,
    chunk,
    counts,
    value_parts,
    peaks,
    latents,
    cotangent_all,
    gain_ffn,
    shift_ffn,
    out_hbm,
    in_hbm,
    down_hbm,
    kv_hbm,
    mixed_hbm,
    norm_full_hbm,
    norm_image_hbm,
    weight_full_hbm,
    weight_image_hbm,
    cotangent_rows,
    queries,
    latent_norm,
    latent_out,
    state_grad,
    gains,
    into_out,
    score_full_out,
    score_image_out,
    query_all,
    out_plane,
    query_half,
    key_half,
    value_half,
    ffn_rows,
    cotangent_other,
    key_wait,
    value_wait,
    out_first,
    out_second,
    out_weight,
    in_weight,
    down_weight,
    column_weight,
    norm_full,
    norm_image,
    weight_full,
    weight_image,
    score_full,
    score_image,
    mixed,
    value_land,
    peak_land,
    ffn_norm,
    partial,
    partial_land,
    kept,
    kept_log,
    attended_all,
    update_all,
    grad_all,
    log_all,
    grad_items,
    stage,
    query_part,
    query_land,
    out_blocks,
    temp,
    load_sem,
    weight_sem,
    column_sem,
    half_sem,
    store_sem,
    scatter_sem,
    gather_sem,
    send_sem,
    recv_sem,
):
    inner = HEADS * HEAD_DIM
    place = Place(lines, size, send_sem, recv_sem)
    me = place.me
    first_full = counts[0] > counts[1]
    local, width = latents.shape[1:]
    rows = 2 * local
    lat_all = local * size
    step = GROUP * lat_all
    chunks = in_hbm.shape[1] // chunk
    cores = others(size, me)

    def weights(c):
        at = pl.ds(pl.multiple_of(c * chunk, chunk), chunk)
        slot = lax.rem(c, DEPTH)
        return (
            pltpu.make_async_copy(in_hbm.at[:, at], in_weight.at[slot], weight_sem.at[0, slot]),
            pltpu.make_async_copy(down_hbm.at[at, :], down_weight.at[slot], weight_sem.at[1, slot]),
        )

    loads = [
        pltpu.make_async_copy(out_hbm, out_weight, load_sem.at[0]),
        pltpu.make_async_copy(mixed_hbm, mixed, load_sem.at[1]),
        pltpu.make_async_copy(norm_full_hbm, norm_full, load_sem.at[2]),
        pltpu.make_async_copy(norm_image_hbm, norm_image, load_sem.at[3]),
        pltpu.make_async_copy(weight_full_hbm, weight_full, load_sem.at[4]),
        pltpu.make_async_copy(weight_image_hbm, weight_image, load_sem.at[5]),
    ]

    def column(n):
        first = inner + n * SPAN if n < GROUPS else (n - GROUPS) * SPAN
        return pltpu.make_async_copy(
            kv_hbm.at[:, pl.ds(first, SPAN)], column_weight.at[n % 2], column_sem.at[n % 2]
        )

    loads[0].start()
    for c in range(min(DEPTH, chunks)):
        for copy in weights(c):
            copy.start()
    for copy in loads[1:]:
        copy.start()
    column(0).start()
    place.greet()
    values_swap = place.swap_cores(lambda p: value_parts.at[p], lambda c: value_land.at[c])
    peaks_swap = place.swap_cores(lambda p: peaks.at[p], lambda c: peak_land.at[c])
    cotangent_swap = place.swap_cores(
        lambda p: cotangent_rows, lambda c: cotangent_other.at[c]
    )
    value_land[me] = value_parts[me]
    peak_land[me] = peaks[me]
    selector = head_selector()
    finish(values_swap)
    finish(peaks_swap)
    peak = peak_land[0, 0]
    for s in range(1, size):
        peak = jnp.maximum(peak, peak_land[s, 0])
    factors = [jnp.exp(peak_land[s, 0] - peak) for s in range(size)]
    total = factors[0] * peak_land[0, 1]
    for s in range(1, size):
        total += factors[s] * peak_land[s, 1]
    kept_log[...] = peak + jnp.log(total)
    attended = jnp.zeros((rows, width), F32)
    for s in range(size):
        attended += value_land[s] * dot_exact(factors[s] / total, selector)
    kept[0] = attended
    attended_low = attended.astype(BF16)
    attended_all[me] = attended_low
    loads[0].wait()
    hidden = dot(attended_low, out_weight[...], 1, 0)
    hidden += jnp.concatenate(
        in_order(first_full, (latents[0].astype(F32), latents[1].astype(F32))), 0
    )
    kept[1] = hidden
    gain, shift = vector(gain_ffn), vector(shift_ffn)
    unit, _ = normalize(hidden)
    ffn_norm[me] = (unit * gain + shift).astype(BF16)
    norm_swap = place.swap_cores(lambda p: ffn_norm.at[me], lambda c: ffn_norm.at[c])
    gather = Gather(place, ffn_norm.at[me], ffn_rows, gather_sem.at[0])
    gather.along_line()
    attended_swap = place.swap_cores(lambda p: attended_all.at[me], lambda c: attended_all.at[c])
    partial[...] = jnp.zeros_like(partial)
    finish(norm_swap)

    @pl.loop(0, chunks)
    def _(c):
        for copy in weights(c):
            copy.wait()
        slot = lax.rem(c, DEPTH)
        all_rows = ffn_norm[...].reshape(size * rows, width)
        cotangents = cotangent_all[...].reshape(size * rows, width)
        activated, slope = gelu_parts(dot(all_rows, in_weight[slot], 1, 0))
        activated = activated.astype(BF16)
        act_grad = dot(cotangents, down_weight[slot], 1, 1)
        pre_grad = (act_grad * slope).astype(BF16)
        partial[0] += dot(activated, down_weight[slot], 1, 0).reshape(size, rows, width)
        partial[1] += dot(pre_grad, in_weight[slot], 1, 1).reshape(size, rows, width)

        @pl.when(c + DEPTH < chunks)
        def _():
            for copy in weights(c + DEPTH):
                copy.start()

    sums_swap = place.swap_cores(lambda p: partial.at[:, p], lambda c: partial_land.at[c])
    gather.first_half()
    finish(sums_swap)
    ffn_sum, norm_grad = partial[0, me], partial[1, me]
    for origin in cores:
        ffn_sum += partial_land[origin, 0]
        norm_grad += partial_land[origin, 1]
    hidden = kept[1]
    unit, inverse = normalize(hidden)
    result = hidden + ffn_sum
    for k, value in enumerate(in_order(first_full, (result[:local], result[local:]))):
        latent_out[k] = value.astype(BF16)
    gains[0:1] = jnp.sum(norm_grad * unit, 0, keepdims=True)
    gains[1:2] = jnp.sum(norm_grad, 0, keepdims=True)
    state = cotangent_all[me].astype(F32) + norm_back(unit, inverse, gain, norm_grad)
    state_grad[...] = state
    update = state.astype(BF16)
    update_all[me] = update
    grad = dot(update, out_weight[...], 1, 1).astype(BF16)
    grad_all[me] = grad
    log_all[me, 0] = kept_log[...]
    log_all[me, 1] = head_sums(grad.astype(F32) * kept[0])
    grad_swap = place.swap_cores(lambda p: grad_all.at[me], lambda c: grad_all.at[c])
    log_swap = place.swap_cores(lambda p: log_all.at[me], lambda c: log_all.at[c])
    update_swap = place.swap_cores(lambda p: update_all.at[me], lambda c: update_all.at[c])
    finish(grad_swap)
    finish(log_swap)

    def by_item(item, of_core):
        part = slice(item * local, (item + 1) * local)
        return jnp.concatenate([of_core(core)[part] for core in range(size)], 0)

    factor, factor_delta = [], []
    for item in range(2):
        grad_items[item] = by_item(item, lambda c: grad_all[c])
        scale = jnp.exp(
            by_item(item, lambda c: peaks[c, 0]) - by_item(item, lambda c: log_all[c, 0])
        )
        factor.append(scale)
        factor_delta.append(scale * by_item(item, lambda c: log_all[c, 1]))
    block_rows = width // (lines * 4 * size)
    uses = []

    def stage_blocks(low):
        slot = len(uses) % 2
        if len(uses) >= 2:
            sends, copy = uses[len(uses) - 2]
            finish_sends(sends)
            copy.wait()
        for k in range(lines * 4):
            for core in range(size):
                base = (k * size + core) * block_rows
                stage[slot, k // 4, (k // 2) % 2, k % 2, core] = low[base : base + block_rows]
        return slot

    def split_cores(low, group, half, wait):
        slot = stage_blocks(low)
        columns = pl.ds(group * SPAN, SPAN)
        sends = place.swap_cores(
            lambda p: stage.at[slot, :, :, :, p], lambda c: wait.at[c, :, :, :, :, columns]
        )
        keep_half(slot, columns, half, sends)

    def keep_half(slot, columns, half, sends):
        copy = pltpu.make_async_copy(
            stage.at[slot, :, :, :, me], half.at[:, :, :, :, columns], half_sem.at[slot]
        )
        copy.start()
        uses.append((sends, copy))

    stores = []

    def store(source, target):
        copy = pltpu.make_async_copy(source, target, store_sem.at[len(stores)])
        copy.start()
        stores.append(copy)

    outs = Scatter(place, out_blocks, (out_first, out_second, None), temp, scatter_sem, None)
    finish(attended_swap)
    finish(update_swap)
    updates = update_all[...].reshape(size * rows, width)
    for group in range(GROUPS):
        span = slice(group * SPAN, (group + 1) * SPAN)
        attends = attended_all[:, :, span].reshape(size * rows, SPAN)
        low = dot(updates, attends, 0, 0)
        for k in range(lines * 4):
            base = k * size * block_rows
            mine = low[base : base + block_rows]
            for core in range(1, size):
                base += block_rows
                mine = jnp.where(me == core, low[base : base + block_rows], mine)
            out_blocks[k // 4, (k // 2) % 2, k % 2, :, span] = mine.astype(BF16)
    for copy in loads[1:]:
        copy.wait()
    shifts = []
    for group in range(GROUPS):
        span = slice(group * SPAN, (group + 1) * SPAN)
        at = slice(group * step, (group + 1) * step)
        column(group + 1).start()
        column(group).wait()
        weight = None
        for item in range(2):
            spread = spread_heads(grad_items[item, :, span])
            heads = range(group * GROUP, (group + 1) * GROUP)
            scale = jnp.concatenate([own_columns(factor[item], h) for h in heads], 0)
            shifts.append(
                across_lanes(
                    jnp.concatenate([own_columns(factor_delta[item], h) for h in heads], 0)
                )
            )
            spread = (spread.astype(F32) * scale).astype(BF16)
            part = dot(mixed[item, at], spread, 0, 0)
            weight = part if weight is None else weight + part
            mixed[item, at] = dot(spread, column_weight[group % 2], 1, 1).astype(BF16)
        split_cores(weight.astype(BF16), group, value_half, value_wait)
        if group == 1:
            gather.second_half()
    for item in range(2):
        store(mixed.at[item], into_out.at[item])
    outs.first_half()
    for group in range(GROUPS):
        span = slice(group * SPAN, (group + 1) * SPAN)
        at = slice(group * step, (group + 1) * step)
        if group + 1 < GROUPS:
            column(GROUPS + group + 1).start()
        column(GROUPS + group).wait()
        weight = None
        for item, keys, weights, scores in (
            (0, norm_full, weight_full, score_full),
            (1, norm_image, weight_image, score_image),
        ):
            item_rows = slice(item * lat_all, (item + 1) * lat_all)
            prob_grad = dot(keys[...], mixed[item, at], 1, 1)
            score = weights[:, at].astype(F32) * (prob_grad - shifts[2 * group + item])
            score = score.astype(BF16)
            scores[:, at] = score
            pulled = dot(score, keys[...], 0, 0).astype(BF16)
            query_part[item_rows, span] = (
                fold_heads(dot(pulled, column_weight[group % 2], 1, 0)) * SCALE
            )
            part = dot(pulled, spread_heads(queries[item_rows, span]), 0, 0)
            weight = part if weight is None else weight + part
        split_cores((weight * SCALE).astype(BF16), group, key_half, key_wait)
    store(score_full, score_full_out)
    store(score_image, score_image_out)
    query_swap = place.swap_cores(lambda p: query_part, lambda c: query_land.at[c])
    outs.second_half()
    finish(query_swap)
    total_query = query_part[...]
    for origin in cores:
        total_query += query_land[origin]
    query_all[...] = total_query.astype(BF16)
    for group in range(GROUPS):
        span = slice(group * SPAN, (group + 1) * SPAN)
        slot = stage_blocks(dot(latent_norm[...], query_all[:, span], 0, 0).astype(BF16))
        keep_half(slot, pl.ds(group * SPAN, SPAN), query_half, [])
    for sends, copy in uses[-2:]:
        finish_sends(sends)
        copy.wait()
    for sends, _ in uses:
        finish_arrivals(sends)
    finish(cotangent_swap)
    gather.end()
    outs.plane_sum()
    store(out_blocks.at[:, place.high, place.low], out_plane)
    for copy in stores:
        copy.wait()


def latent_pass(
    chips,
    size,
    counts,
    value_parts,
    peaks,
    latents,
    cotangent_all,
    gain_ffn,
    shift_ffn,
    out_weight,
    in_weight,
    down_weight,
    kv_weight,
    mixed,
    norm_full,
    norm_image,
    weight_full,
    weight_image,
    cotangent_rows,
    queries,
    latent_norm,
):
    lines = chips // 4
    local, width = latents.shape[1:]
    inner = HEADS * HEAD_DIM
    rows = 2 * local
    lat_all = local * size
    hidden_units = in_weight.shape[1]
    chunk = 512 if hidden_units % 512 == 0 else 256
    block_rows = width // (chips * size)
    blocks = (lines, 2, 2, block_rows, inner)
    gathered = (lines, 2, 2, rows, width)
    shape = jax.ShapeDtypeStruct
    copies = 2 * lines + 24 * size + 12
    return pl.pallas_call(
        functools.partial(latent_kernel, lines, size, chunk),
        out_shape=[
            shape(latents.shape, BF16),
            shape((rows, width), F32),
            shape((2, width), F32),
            shape(mixed.shape, BF16),
            shape(weight_full.shape, BF16),
            shape(weight_image.shape, BF16),
            shape((2 * lat_all, inner), BF16),
            shape((lines, block_rows, inner), BF16),
            shape(blocks, BF16),
            shape(blocks, BF16),
            shape(blocks, BF16),
            shape(gathered, BF16),
            shape((size,) + gathered, BF16),
            shape((size,) + blocks, BF16),
            shape((size,) + blocks, BF16),
            *Scatter.lands(lines, block_rows, inner)[:2],
        ],
        in_specs=[SMEM] + [VMEM] * 6 + [ANY] * 10 + [VMEM] * 2,
        out_specs=[VMEM] * 3 + [ANY] * 3 + [VMEM] + [ANY] * 10,
        scratch_shapes=[
            pltpu.VMEM(out_weight.shape, BF16),
            pltpu.VMEM((DEPTH, width, chunk), BF16),
            pltpu.VMEM((DEPTH, chunk, width), BF16),
            pltpu.VMEM((2, width, SPAN), BF16),
            pltpu.VMEM(norm_full.shape, BF16),
            pltpu.VMEM(norm_image.shape, BF16),
            pltpu.VMEM(weight_full.shape, BF16),
            pltpu.VMEM(weight_image.shape, BF16),
            pltpu.VMEM(weight_full.shape, BF16),
            pltpu.VMEM(weight_image.shape, BF16),
            pltpu.VMEM(mixed.shape, BF16),
            pltpu.VMEM((size, rows, width), F32),
            pltpu.VMEM((size, 2, rows, 128), F32),
            pltpu.VMEM((size, rows, width), BF16),
            pltpu.VMEM((2, size, rows, width), F32),
            pltpu.VMEM((size, 2, rows, width), F32),
            pltpu.VMEM((2, rows, width), F32),
            pltpu.VMEM((rows, 128), F32),
            pltpu.VMEM((size, rows, inner), BF16),
            pltpu.VMEM((size, rows, width), BF16),
            pltpu.VMEM((size, rows, inner), BF16),
            pltpu.VMEM((size, 2, rows, 128), F32),
            pltpu.VMEM((2, lat_all, inner), BF16),
            pltpu.VMEM((2, lines, 2, 2, size, block_rows, SPAN), BF16),
            pltpu.VMEM((2 * lat_all, inner), F32),
            pltpu.VMEM((size, 2 * lat_all, inner), F32),
            pltpu.VMEM(blocks, BF16),
            pltpu.VMEM((2, lines // 2, 2, 1, block_rows, inner), BF16),
            pltpu.SemaphoreType.DMA((6,)),
            pltpu.SemaphoreType.DMA((2, DEPTH)),
            pltpu.SemaphoreType.DMA((2,)),
            pltpu.SemaphoreType.DMA((2,)),
            pltpu.SemaphoreType.DMA((5,)),
            pltpu.SemaphoreType.DMA((max(2, lines),)),
            pltpu.SemaphoreType.DMA((1,)),
            pltpu.SemaphoreType.DMA((copies,)),
            pltpu.SemaphoreType.DMA((copies,)),
        ],
        compiler_params=params(collective_id=1, has_side_effects=True),
    )(
        counts,
        value_parts,
        peaks,
        latents,
        cotangent_all,
        gain_ffn,
        shift_ffn,
        out_weight,
        in_weight,
        down_weight,
        kv_weight,
        mixed,
        norm_full,
        norm_image,
        weight_full,
        weight_image,
        cotangent_rows,
        queries,
        latent_norm,
    )


def backward_kernel(
    frames,
    lines,
    size,
    counts,
    media,
    latents,
    gain_media,
    gain_latent,
    shift_latent,
    time_embed,
    query_hbm,
    weight_full_hbm,
    weight_image_hbm,
    score_full_hbm,
    score_image_hbm,
    absorbed_hbm,
    into_hbm,
    out_plane,
    query_half,
    key_half,
    value_half,
    key_wait,
    value_wait,
    ffn_rows,
    cotangent_rows,
    cotangent_other,
    query_all,
    state_grad,
    ffn_gains,
    in_hbm,
    down_hbm,
    slot_grad,
    latent_grad,
    out_sum,
    query_sum,
    key_sum,
    value_sum,
    units_out,
    small_out,
    ffn_other,
    units_middle,
    out_line,
    query_first,
    query_second,
    query_line,
    key_first,
    key_second,
    key_line,
    value_first,
    value_second,
    value_line,
    out_blocks,
    query_blocks,
    key_blocks,
    value_blocks,
    temp,
    column_weight,
    weight_full,
    weight_image,
    score_full,
    score_image,
    absorbed,
    into,
    in_share,
    down_share,
    buffer,
    share_sum,
    units,
    block,
    result,
    times,
    small,
    small_land,
    small_sums,
    load_sem,
    column_sem,
    buffer_sem,
    result_sem,
    scatter_sem,
    move_sem,
    send_sem,
    recv_sem,
):
    inner = HEADS * HEAD_DIM
    width = media.shape[-1]
    place = Place(lines, size, send_sem, recv_sem)
    me = place.me
    cores = others(size, me)
    first_full = counts[0] > counts[1]
    local = latents.shape[1]
    lat_all = local * size
    half = lines // 2
    share = down_share.shape[0]
    down_first = pl.multiple_of(place.dp * share, share)
    offset = lax.rem(place.dp * share, 128)
    in_first = pl.multiple_of(place.dp * share - offset, 128)

    loads = [
        pltpu.make_async_copy(source, target, load_sem.at[k])
        for k, (source, target) in enumerate(
            (
                (out_plane, out_blocks),
                (query_half, query_blocks),
                (key_half, key_blocks),
                (value_half, value_blocks),
                (weight_full_hbm, weight_full),
                (weight_image_hbm, weight_image),
                (score_full_hbm, score_full),
                (score_image_hbm, score_image),
                (into_hbm, into),
                (absorbed_hbm, absorbed),
                (in_hbm.at[:, pl.ds(in_first, in_share.shape[1])], in_share),
                (down_hbm.at[pl.ds(down_first, share), :], down_share),
            )
        )
    ]

    def column(group):
        return pltpu.make_async_copy(
            query_hbm.at[:, pl.ds(group * SPAN, SPAN)],
            column_weight.at[group % 2],
            column_sem.at[group % 2],
        )

    own_pieces = [(ffn_rows, cotangent_rows, line) for line in range(lines)]
    pieces = own_pieces + [
        (ffn_other.at[core], cotangent_other.at[core], line) for core in cores for line in range(lines)
    ]
    device_rows = ffn_rows.shape[3]
    piece_rows = 4 * device_rows

    def piece(k):
        ffn_source, cotangent_source, line = pieces[k]
        return [
            pltpu.make_async_copy(
                source.at[line, n // 2, n % 2],
                buffer.at[k % 2, j, pl.ds(n * device_rows, device_rows)],
                buffer_sem.at[k % 2, j, n],
            )
            for j, source in ((0, ffn_source), (1, cotangent_source))
            for n in range(4)
        ]

    for copy in loads[:2] + piece(0) + loads[10:] + loads[2:10]:
        copy.start()
    column(0).start()
    place.greet()

    def scatter(blocks, lands, out):
        return Scatter(place, blocks, lands, temp, scatter_sem, out)

    quer = scatter(query_blocks, (query_first, query_second, query_line), query_sum)
    keys = scatter(key_blocks, (key_first, key_second, key_line), key_sum)
    vals = scatter(value_blocks, (value_first, value_second, value_line), value_sum)

    def add_cores(blocks, wait):
        for origin in cores:
            for k in range(2):
                load = pltpu.make_async_copy(
                    wait.at[origin, pl.ds(k * half, half)], temp.at[k], scatter_sem.at[k]
                )
                load.start()
            for k in range(2):
                pltpu.make_async_copy(
                    wait.at[origin, pl.ds(k * half, half)], temp.at[k], scatter_sem.at[k]
                ).wait()

            @pl.loop(0, half)
            def _(line):
                for k in range(2):
                    for high in range(2):
                        for low in range(2):
                            mine = blocks[k * half + line, high, low].astype(F32)
                            mine += temp[k, line, high, low].astype(F32)
                            blocks[k * half + line, high, low] = mine.astype(BF16)

    outs = LineSum(place, out_blocks, (None, None, out_line), temp, scatter_sem, out_sum)
    for copy in loads[:2]:
        copy.wait()
    outs.send_line()
    quer.first_half()
    ffn_swap = place.swap_cores(lambda p: ffn_rows, lambda c: ffn_other.at[c])
    small[...] = jnp.zeros_like(small)
    times[...] = time_embed[...].astype(F32)

    for copy in loads[10:]:
        copy.wait()
    in_part = in_share[:, :share]
    for first in range(64, in_share.shape[1] - share + 1, 64):
        in_part = jnp.where(offset == first, in_share[:, first : first + share], in_part)
    in_share[:, :share] = in_part
    for k in range(len(pieces)):
        if k + 1 == len(own_pieces):
            finish(ffn_swap)
            loads[2].wait()
            add_cores(key_blocks, key_wait)
            quer.second_half()
            keys.first_half()
        if k + 1 < len(pieces):
            for copy in piece(k + 1):
                copy.start()
        for copy in piece(k):
            copy.wait()
        ffn_piece = buffer[k % 2, 0, :piece_rows]
        cotangent_piece = buffer[k % 2, 1, :piece_rows]
        activated, slope = gelu_parts(dot(ffn_piece, in_share[:, :share], 1, 0))
        pre_grad = (dot(cotangent_piece, down_share[...], 1, 1) * slope).astype(BF16)
        up = dot(ffn_piece, pre_grad, 0, 0)
        down = dot(cotangent_piece, activated.astype(BF16), 0, 0)
        if k == 0:
            share_sum[0], share_sum[1] = up, down
        else:
            share_sum[0] += up
            share_sum[1] += down
    unit_rows = width // (lines * 4)
    for k in range(lines * 4):
        at = slice(k * unit_rows, (k + 1) * unit_rows)
        both = jnp.concatenate([share_sum[0, at], share_sum[1, at]], 1)
        units[k // 4, (k // 2) % 2, k % 2] = both.astype(BF16)
    moved = Move(place, units, units_middle, units_out, move_sem)
    moved.along_line()

    def fetch(frame):
        return pltpu.make_async_copy(
            media.at[:, pl.ds(frame * PATCH, PATCH)], buffer.at[frame % 2], buffer_sem.at[frame % 2, 0, 0]
        )

    fetch(0).start()
    loads[3].wait()
    add_cores(value_blocks, value_wait)
    quer.plane_sum()
    quer.send_line()
    vals.first_half()
    keys.second_half()
    outs.end()
    for copy in loads[4:10]:
        copy.wait()

    def back(scores, weights, item, at, count):
        rows = slice(at, at + count)
        return dot(scores[rows], absorbed[item], 1, 0) + dot(weights[rows], into[item], 1, 0)

    row_grad = [
        back(score_full, weight_full, 0, frames * PATCH, local),
        back(score_image, weight_image, 1, PATCH, local),
    ]
    row_grad = jnp.concatenate(row_grad, 0)
    mine = [
        query_all[pl.ds(pl.multiple_of(item * lat_all + me * local, local), local)]
        for item in range(2)
    ]
    mine = jnp.concatenate(mine, 0)
    for group in range(GROUPS):
        if group + 1 < GROUPS:
            column(group + 1).start()
        column(group).wait()
        span = slice(group * SPAN, (group + 1) * SPAN)
        row_grad += dot(mine[:, span], column_weight[group % 2], 1, 1)
    own = jnp.concatenate(
        in_order(first_full, (latents[0].astype(F32), latents[1].astype(F32))), 0
    )
    unit, inverse = normalize(own)
    small[2:3] = jnp.sum(row_grad * unit, 0, keepdims=True)
    small[3:4] = jnp.sum(row_grad, 0, keepdims=True)
    small[4:6] = ffn_gains[...]
    row_grad = state_grad[...] + norm_back(unit, inverse, vector(gain_latent), row_grad)
    for k, value in enumerate(in_order(first_full, (row_grad[:local], row_grad[local:]))):
        latent_grad[k] = value

    gain = vector(gain_media)
    total = Total(place, small, small_land, small_sums)

    def norm_frame(frame, slot, pick_first, target):
        at_time = 6 + me * frames + frame
        time_row = times[pl.ds(me * frames + frame, 1)]

        @pl.loop(0, PATCH // ROWS)
        def _(part):
            at = pl.ds(pl.multiple_of(part * ROWS, ROWS), ROWS)
            values = jnp.where(
                pick_first, buffer[slot, 0, at].astype(F32), buffer[slot, 1, at].astype(F32)
            )
            unit, inverse = normalize(values + time_row)
            grad = block[at]
            rows_grad = norm_back(unit, inverse, gain, grad)
            target[at] = rows_grad.astype(BF16)
            small[0:1] += jnp.sum(grad * unit, 0, keepdims=True)
            small[1:2] += jnp.sum(grad, 0, keepdims=True)
            small[pl.ds(at_time, 1)] += jnp.sum(rows_grad, 0, keepdims=True)

    puts = []
    for k in range(frames + 1):
        frame = max(0, k - 1)
        if k != 1:
            fetch(frame).wait()
        if k >= 1 and frame + 1 < frames:
            fetch(frame + 1).start()
        if k == 0:
            block[...] = back(score_image, weight_image, 1, 0, PATCH)
        else:
            block[...] = back(score_full, weight_full, 0, frame * PATCH, PATCH)
        if k >= 2:
            puts[k - 2].wait()
        picked = jnp.logical_not(first_full) if k == 0 else first_full
        norm_frame(frame, frame % 2, picked, result.at[k % 2])
        puts.append(
            pltpu.make_async_copy(
                result.at[k % 2], slot_grad.at[pl.ds(k * PATCH, PATCH)], result_sem.at[k % 2]
            )
        )
        puts[k].start()
        if k == 1:
            vals.second_half()
            keys.plane_sum()
            keys.send_line()
            moved.in_plane()
        if k == frames // 2 + 1:
            quer.end()
    total.in_chip()
    vals.plane_sum()
    vals.send_line()
    total.low()
    total.high()
    total.along_line()
    keys.end()
    total.end(small_out)
    moved.end()
    vals.end()
    for put in puts[max(0, frames - 1) :]:
        put.wait()


def attend_backward(
    chips,
    size,
    counts,
    media,
    latents,
    gain_media,
    gain_latent,
    shift_latent,
    time_embed,
    query_weight,
    weight_full,
    weight_image,
    score_full,
    score_image,
    absorbed,
    into,
    out_plane,
    query_half,
    key_half,
    value_half,
    key_wait,
    value_wait,
    ffn_rows,
    cotangent_rows,
    cotangent_other,
    query_all,
    state_grad,
    ffn_gains,
    in_weight,
    down_weight,
):
    width = media.shape[-1]
    inner = HEADS * HEAD_DIM
    lines = chips // 4
    frames = media.shape[1] // PATCH
    block_rows = width // (chips * size)
    blocks = (lines, 2, 2, block_rows, inner)
    share = in_weight.shape[1] // chips
    unit = (lines, 2, 2, width // chips, 2 * share)
    small = (6 + time_embed.shape[0] + 7) // 8 * 8
    shape = jax.ShapeDtypeStruct
    copies = 6 * lines + 10 * size + 24
    lands = Scatter.lands(lines, block_rows, inner)
    return pl.pallas_call(
        functools.partial(backward_kernel, frames, lines, size),
        out_shape=[
            shape(((frames + 1) * PATCH, width), BF16),
            shape(latents.shape, F32),
            *[shape((block_rows, inner), F32)] * 4,
            shape(unit, BF16),
            shape((small, width), F32),
            shape((size,) + ffn_rows.shape, BF16),
            shape(unit, BF16),
            lands[2],
            *lands * 3,
        ],
        in_specs=[SMEM, ANY] + [VMEM] * 5 + [ANY] * 16 + [VMEM] * 3 + [ANY] * 2,
        out_specs=[ANY] + [VMEM] * 5 + [ANY, VMEM] + [ANY] * 12,
        scratch_shapes=[
            pltpu.VMEM((lines, block_rows, inner), BF16),
            *[pltpu.VMEM(blocks, BF16)] * 3,
            pltpu.VMEM((2, lines // 2, 2, 2, block_rows, inner), BF16),
            pltpu.VMEM((2, width, SPAN), BF16),
            pltpu.VMEM(weight_full.shape, BF16),
            pltpu.VMEM(weight_image.shape, BF16),
            pltpu.VMEM(weight_full.shape, BF16),
            pltpu.VMEM(weight_image.shape, BF16),
            pltpu.VMEM(absorbed.shape, BF16),
            pltpu.VMEM(into.shape, BF16),
            pltpu.VMEM((width, (share + 64 + 127) // 128 * 128), BF16),
            pltpu.VMEM((share, width), BF16),
            pltpu.VMEM((2, 2, PATCH, width), BF16),
            pltpu.VMEM((2, width, share), F32),
            pltpu.VMEM(unit, BF16),
            pltpu.VMEM((PATCH, width), F32),
            pltpu.VMEM((2, PATCH, width), BF16),
            pltpu.VMEM(time_embed.shape, F32),
            pltpu.VMEM((small, width), F32),
            *Total.scratch(lines, size, (small, width)),
            pltpu.SemaphoreType.DMA((12,)),
            pltpu.SemaphoreType.DMA((2,)),
            pltpu.SemaphoreType.DMA((2, 2, 4)),
            pltpu.SemaphoreType.DMA((2,)),
            pltpu.SemaphoreType.DMA((max(4, lines),)),
            pltpu.SemaphoreType.DMA((2,)),
            pltpu.SemaphoreType.DMA((copies,)),
            pltpu.SemaphoreType.DMA((copies,)),
        ],
        compiler_params=params(collective_id=2, has_side_effects=True),
    )(
        counts,
        media,
        latents,
        gain_media,
        gain_latent,
        shift_latent,
        time_embed,
        query_weight,
        weight_full,
        weight_image,
        score_full,
        score_image,
        absorbed,
        into,
        out_plane,
        query_half,
        key_half,
        value_half,
        key_wait,
        value_wait,
        ffn_rows,
        cotangent_rows,
        cotangent_other,
        query_all,
        state_grad,
        ffn_gains,
        in_weight,
        down_weight,
    )


def result_kernel(
    chips,
    flags,
    slots,
    units,
    latent_in,
    latent_grad_in,
    key_in,
    value_in,
    query_in,
    out_in,
    media_grad,
    up,
    down,
    latent_out,
    latent_grad,
    key_value,
    query,
    out,
):
    item, frame = pl.program_id(0), pl.program_id(1)
    alive = (item == flags[0]) | (frame == 0)
    media_grad[0] = jnp.where(alive, slots[...].astype(F32), 0.0)

    @pl.when((item == 0) & (frame == 0))
    def _():
        share = units.shape[-1] // 2
        for pair in range(chips // 2):
            at = slice(pair * 2 * share, (pair + 1) * 2 * share)
            left, right = units[2 * pair].astype(F32), units[2 * pair + 1].astype(F32)
            up[:, at] = jnp.concatenate([left[:, :share], right[:, :share]], 1)
            down[:, at] = jnp.concatenate([left[:, share:], right[:, share:]], 1)
        latent_out[...] = latent_in[...]
        latent_grad[...] = latent_grad_in[...]
        inner = key_in.shape[-1]
        key_value[:, :inner] = key_in[...]
        key_value[:, inner:] = value_in[...]
        query[...] = query_in[...]
        out[...] = out_in[...]


def final_form(counts, slots, units, latent_out, latent_grad, sums, frames):
    chips, rows, columns = units.shape
    width = slots.shape[-1]
    block_rows = sums[0].shape[0]
    full = jnp.where(counts[0] > counts[1], 0, 1).astype(jnp.int32).reshape(1)
    shape = jax.ShapeDtypeStruct

    def whole(array_shape):
        return pl.BlockSpec(array_shape, lambda i, f, flags: (0,) * len(array_shape))

    outs = [
        ((rows, chips * columns // 2), F32),
        ((rows, chips * columns // 2), F32),
        (latent_out.shape, BF16),
        (latent_grad.shape, F32),
        ((block_rows, 2 * width), F32),
        ((block_rows, width), F32),
        ((block_rows, width), F32),
    ]
    return pl.pallas_call(
        functools.partial(result_kernel, chips),
        out_shape=[shape((2, frames * PATCH, width), F32)] + [shape(*out) for out in outs],
        grid_spec=pltpu.PrefetchScalarGridSpec(
            num_scalar_prefetch=1,
            grid=(2, frames),
            in_specs=[
                pl.BlockSpec(
                    (PATCH, width), lambda i, f, flags: (jnp.where(i == flags[0], f + 1, 0), 0)
                ),
                whole(units.shape),
                whole(latent_out.shape),
                whole(latent_grad.shape),
                *[whole(part.shape) for part in sums],
            ],
            out_specs=[pl.BlockSpec((1, PATCH, width), lambda i, f, flags: (i, f, 0))]
            + [whole(out[0]) for out in outs],
        ),
        compiler_params=params(),
    )(full, slots, units, latent_out, latent_grad, *sums)


def per_device(
    chips,
    size,
    media,
    frame_counts,
    latents,
    norm_media_gain,
    norm_media_shift,
    norm_latent_gain,
    norm_latent_shift,
    time_embed,
    query_weight,
    key_value_weight,
    out_weight,
    ffn_norm_gain,
    ffn_norm_shift,
    ffn_in_weight,
    ffn_out_weight,
    out_cotangent,
):
    dp, me = lax.axis_index("dp"), lax.axis_index("mp")
    width = media.shape[-1]
    share = ffn_in_weight.shape[1] // chips
    (
        norm_full,
        norm_image,
        weight_full,
        weight_image,
        absorbed,
        mixed,
        value_parts,
        peaks,
        latent_norm,
        queries,
        cotangent_all,
        cotangent_rows,
    ) = attend_forward(
        chips,
        size,
        frame_counts,
        media,
        latents,
        out_cotangent,
        norm_media_gain,
        norm_media_shift,
        norm_latent_gain,
        norm_latent_shift,
        time_embed,
        query_weight,
        key_value_weight,
    )
    (
        latent_out,
        state_grad,
        ffn_gains,
        into,
        score_full,
        score_image,
        query_all,
        out_plane,
        query_half,
        key_half,
        value_half,
        ffn_rows,
        cotangent_other,
        key_wait,
        value_wait,
        *_,
    ) = latent_pass(
        chips,
        size,
        frame_counts,
        value_parts,
        peaks,
        latents,
        cotangent_all,
        ffn_norm_gain,
        ffn_norm_shift,
        out_weight,
        ffn_in_weight,
        ffn_out_weight,
        key_value_weight,
        mixed,
        norm_full,
        norm_image,
        weight_full,
        weight_image,
        cotangent_rows,
        queries,
        latent_norm,
    )
    slot_grad, latent_grad, out_sum, query_sum, key_sum, value_sum, units, small, *_ = (
        attend_backward(
            chips,
            size,
            frame_counts,
            media,
            latents,
            norm_media_gain,
            norm_latent_gain,
            norm_latent_shift,
            time_embed,
            query_weight,
            weight_full,
            weight_image,
            score_full,
            score_image,
            absorbed,
            into,
            out_plane,
            query_half,
            key_half,
            value_half,
            key_wait,
            value_wait,
            ffn_rows,
            cotangent_rows,
            cotangent_other,
            query_all,
            state_grad,
            ffn_gains,
            ffn_in_weight,
            ffn_out_weight,
        )
    )
    units = units.reshape(chips, width // chips, 2 * share)
    sums = (key_sum, value_sum, query_sum, out_sum)
    media_grad, up_sum, down_sum, latent_out, latent_grad, key_value_sum, query_sum, out_sum = (
        final_form(
            frame_counts, slot_grad, units, latent_out, latent_grad, sums, media.shape[1] // PATCH
        )
    )
    place = (dp * size + me) * (width // (chips * size))
    small = lax.dynamic_slice_in_dim(small, place, width // (chips * size), 1)
    return (
        latent_out,
        latent_grad,
        media_grad,
        small[0],
        small[1],
        small[2],
        small[3],
        small[6 : 6 + time_embed.shape[0]],
        query_sum,
        key_value_sum,
        out_sum.T,
        small[4],
        small[5],
        up_sum,
        down_sum.T,
    )


def layer_norm(values_in, gain, shift):
    row_mean = jnp.mean(values_in, -1, keepdims=True)
    centered = values_in - row_mean
    variance = jnp.mean(centered * centered, -1, keepdims=True)
    return centered * lax.rsqrt(variance + EPSILON) * gain + shift


def plain_norm_back(values_in, gain, shift, gradient):
    result, pullback = jax.vjp(layer_norm, values_in, gain, shift)
    return pullback(gradient)


def gelu_exact(values_in):
    return jax.nn.gelu(values_in, approximate=False)


def rescale_heads(values_in, factor):
    shaped = values_in.reshape(values_in.shape[:-1] + (factor.shape[-1], -1))
    return (shaped * factor[..., None]).reshape(values_in.shape)


def plain_device(
    media,
    frame_counts,
    latents,
    norm_media_gain,
    norm_media_shift,
    norm_latent_gain,
    norm_latent_shift,
    time_embed,
    query_weight,
    key_value_weight,
    out_weight,
    ffn_norm_gain,
    ffn_norm_shift,
    ffn_in_weight,
    ffn_out_weight,
    out_cotangent,
):
    item_count, local_keys, model_width = media.shape
    latent_local = latents.shape[1]
    inner = HEADS * HEAD_DIM
    frames_local = local_keys // PATCH
    key_count = local_keys + latent_local
    mp_index = lax.axis_index("mp")
    latent_start = mp_index * latent_local
    score_scale = HEAD_DIM ** (-0.5)
    gain_m = norm_media_gain.astype(jnp.float32)
    shift_m = norm_media_shift.astype(jnp.float32)
    gain_l = norm_latent_gain.astype(jnp.float32)
    shift_l = norm_latent_shift.astype(jnp.float32)
    gain_f = ffn_norm_gain.astype(jnp.float32)
    shift_f = ffn_norm_shift.astype(jnp.float32)
    frame_ids = mp_index * frames_local + jnp.arange(frames_local)
    frame_live = frame_ids[None, :] < frame_counts[:, None]
    key_alive = jnp.concatenate(
        [jnp.repeat(frame_live, PATCH, axis=1), jnp.ones((item_count, latent_local), bool)], axis=1
    )
    alive_mask = key_alive[:, None, None, :]
    time_rows = lax.dynamic_slice_in_dim(
        time_embed, mp_index * frames_local, frames_local, 0
    ).astype(jnp.float32)
    with_time = (
        media.astype(jnp.float32).reshape(item_count, frames_local, PATCH, model_width)
        + time_rows[None, :, None, :]
    )
    with_time = with_time.reshape(item_count * local_keys, model_width)
    media_norm = layer_norm(with_time, gain_m, shift_m).astype(jnp.bfloat16)
    latent_in = latents.astype(jnp.float32)
    latent_norm = layer_norm(latent_in, gain_l, shift_l).astype(jnp.bfloat16)
    media_kv = jnp.dot(media_norm, key_value_weight, preferred_element_type=jnp.float32).astype(
        jnp.bfloat16
    )
    latent_kv = jnp.einsum(
        "ild,de->ile", latent_norm, key_value_weight, preferred_element_type=jnp.float32
    ).astype(jnp.bfloat16)
    keys_values = jnp.concatenate(
        [media_kv.reshape(item_count, local_keys, 2 * inner), latent_kv], axis=1
    )
    key_heads = keys_values[..., :inner].reshape(item_count, key_count, HEADS, HEAD_DIM)
    value_heads = keys_values[..., inner:].reshape(item_count, key_count, HEADS, HEAD_DIM)
    query_own = jnp.einsum(
        "ild,de->ile", latent_norm, query_weight, preferred_element_type=jnp.float32
    ).astype(jnp.bfloat16)
    queries = lax.all_gather(query_own, "mp", axis=1, tiled=True)
    lat_all = queries.shape[1]
    query_heads = queries.reshape(item_count, lat_all, HEADS, HEAD_DIM)
    scores = (
        jnp.einsum("iqhd,ikhd->ihqk", query_heads, key_heads, preferred_element_type=jnp.float32)
        * score_scale
    )
    masked = jnp.where(alive_mask, scores, -1e30)
    peak_score = jnp.max(masked, -1)
    weights = jnp.where(alive_mask, jnp.exp(masked - peak_score[..., None]), 0.0)
    weight_sum = jnp.sum(weights, -1).transpose(0, 2, 1)
    peak_score = peak_score.transpose(0, 2, 1)
    numerator = jnp.einsum(
        "ihqk,ikhd->iqhd",
        weights.astype(jnp.bfloat16),
        value_heads,
        preferred_element_type=jnp.float32,
    ).reshape(item_count, lat_all, inner)
    peak_all = lax.pmax(peak_score, "mp")
    factor = jnp.exp(peak_score - peak_all)
    weight_own, numerator_own = (
        lax.psum_scatter(weight_sum * factor, "mp", scatter_dimension=1, tiled=True),
        lax.psum_scatter(rescale_heads(numerator, factor), "mp", scatter_dimension=1, tiled=True),
    )
    peak_own = lax.dynamic_slice_in_dim(peak_all, latent_start, latent_local, 1)
    log_sum_own = peak_own + jnp.log(weight_own)
    attended_exact = rescale_heads(numerator_own, 1.0 / weight_own)
    attended_low = attended_exact.astype(jnp.bfloat16)
    update = jnp.einsum("ile,ed->ild", attended_low, out_weight, preferred_element_type=jnp.float32)
    hidden_state = latent_in + update
    ffn_norm = layer_norm(hidden_state, gain_f, shift_f).astype(jnp.bfloat16)
    ffn_norm_rows = ffn_norm.transpose(1, 0, 2)
    gathered = lax.all_gather(ffn_norm_rows, "mp", axis=0, tiled=True)
    pre_act = jnp.einsum("lid,df->lif", gathered, ffn_in_weight, preferred_element_type=jnp.float32)
    activated = gelu_exact(pre_act).astype(jnp.bfloat16)
    ffn_norm_all = gathered
    block = activated
    ffn_result = lax.psum_scatter(
        jnp.einsum("lif,fd->lid", block, ffn_out_weight, preferred_element_type=jnp.float32),
        "mp",
        scatter_dimension=0,
        tiled=True,
    )
    latent_out = (hidden_state + ffn_result.transpose(1, 0, 2)).astype(jnp.bfloat16)
    cotangent_rows = out_cotangent.transpose(1, 0, 2)
    gathered = lax.all_gather(cotangent_rows, "mp", axis=0, tiled=True)
    act_grad = jnp.einsum(
        "lid,fd->lif", gathered, ffn_out_weight, preferred_element_type=jnp.float32
    )
    result, pullback = jax.vjp(gelu_exact, pre_act)
    pre_grad = pullback(act_grad)[0].astype(jnp.bfloat16)
    ffn_down_grad = jnp.einsum(
        "lif,lid->fd", activated, gathered, preferred_element_type=jnp.float32
    )
    ffn_up_grad = jnp.einsum(
        "lid,lif->df", ffn_norm_all, pre_grad, preferred_element_type=jnp.float32
    )
    block = pre_grad
    ffn_norm_grad = lax.psum_scatter(
        jnp.einsum("lif,df->lid", block, ffn_in_weight, preferred_element_type=jnp.float32),
        "mp",
        scatter_dimension=0,
        tiled=True,
    ).transpose(1, 0, 2)
    state_part, gain_f_grad, shift_f_grad = plain_norm_back(hidden_state, gain_f, shift_f, ffn_norm_grad)
    state_grad = out_cotangent.astype(jnp.float32) + state_part
    update_grad = state_grad.astype(jnp.bfloat16)
    out_grad_local = jnp.einsum(
        "ile,ild->ed", attended_low, update_grad, preferred_element_type=jnp.float32
    )
    attended_grad = jnp.einsum(
        "ild,ed->ile", update_grad, out_weight, preferred_element_type=jnp.float32
    ).astype(jnp.bfloat16)
    row_delta = jnp.sum(
        (attended_grad.astype(jnp.float32) * attended_exact).reshape(
            item_count, latent_local, HEADS, HEAD_DIM
        ),
        -1,
    )
    grad_all, delta_all, log_sum_all = (
        lax.all_gather(attended_grad.astype(jnp.float32), "mp", axis=1, tiled=True),
        lax.all_gather(row_delta, "mp", axis=1, tiled=True),
        lax.all_gather(log_sum_own, "mp", axis=1, tiled=True),
    )
    grad_heads = grad_all.astype(jnp.bfloat16).reshape(item_count, lat_all, HEADS, HEAD_DIM)
    scores_again = (
        jnp.einsum("iqhd,ikhd->ihqk", query_heads, key_heads, preferred_element_type=jnp.float32)
        * score_scale
    )
    probability = jnp.where(
        alive_mask, jnp.exp(scores_again - log_sum_all.transpose(0, 2, 1)[..., None]), 0.0
    )
    prob_grad = jnp.einsum(
        "iqhd,ikhd->ihqk", grad_heads, value_heads, preferred_element_type=jnp.float32
    )
    score_grad = (probability * (prob_grad - delta_all.transpose(0, 2, 1)[..., None])).astype(
        jnp.bfloat16
    )
    query_part_grad = (
        jnp.einsum("ihqk,ikhd->iqhd", score_grad, key_heads, preferred_element_type=jnp.float32)
        * score_scale
    ).reshape(item_count, lat_all, inner)
    key_grad = (
        jnp.einsum("ihqk,iqhd->ikhd", score_grad, query_heads, preferred_element_type=jnp.float32)
        * score_scale
    )
    value_grad = jnp.einsum(
        "ihqk,iqhd->ikhd",
        probability.astype(jnp.bfloat16),
        grad_heads,
        preferred_element_type=jnp.float32,
    )
    kv_grad = jnp.concatenate(
        [
            key_grad.reshape(item_count, key_count, inner),
            value_grad.reshape(item_count, key_count, inner),
        ],
        -1,
    ).astype(jnp.bfloat16)
    query_grad = lax.psum_scatter(query_part_grad, "mp", scatter_dimension=1, tiled=True).astype(
        jnp.bfloat16
    )
    media_kv_grad = kv_grad[:, :local_keys].reshape(item_count * local_keys, 2 * inner)
    latent_kv_grad = kv_grad[:, local_keys:]
    kv_weight_local = jnp.einsum(
        "rd,re->de", media_norm, media_kv_grad, preferred_element_type=jnp.float32
    ) + jnp.einsum("ild,ile->de", latent_norm, latent_kv_grad, preferred_element_type=jnp.float32)
    query_weight_local = jnp.einsum(
        "ild,ile->de", latent_norm, query_grad, preferred_element_type=jnp.float32
    )
    media_norm_grad = jnp.einsum(
        "re,de->rd", media_kv_grad, key_value_weight, preferred_element_type=jnp.float32
    )
    latent_norm_grad = jnp.einsum(
        "ile,de->ild", latent_kv_grad, key_value_weight, preferred_element_type=jnp.float32
    ) + jnp.einsum("ile,de->ild", query_grad, query_weight, preferred_element_type=jnp.float32)
    media_pre_grad, gain_m_grad, shift_m_grad = plain_norm_back(
        with_time, gain_m, shift_m, media_norm_grad
    )
    latent_part, gain_l_grad, shift_l_grad = plain_norm_back(latent_in, gain_l, shift_l, latent_norm_grad)
    latent_grad = state_grad + latent_part
    media_grad = media_pre_grad.reshape(item_count, local_keys, model_width)
    time_local = jnp.sum(
        media_pre_grad.reshape(item_count, frames_local, PATCH, model_width), (0, 2)
    )
    time_grad = lax.dynamic_update_slice_in_dim(
        jnp.zeros((time_embed.shape[0], model_width), jnp.float32),
        time_local,
        mp_index * frames_local,
        0,
    )
    small_grads = jnp.concatenate(
        [
            jnp.stack(
                [gain_m_grad, shift_m_grad, gain_l_grad, shift_l_grad, gain_f_grad, shift_f_grad], 1
            ),
            time_grad.T,
        ],
        1,
    )
    query_sum, kv_sum, out_sum, small_sum = (
        lax.psum_scatter(query_weight_local, ("dp", "mp"), scatter_dimension=0, tiled=True),
        lax.psum_scatter(kv_weight_local, ("dp", "mp"), scatter_dimension=0, tiled=True),
        lax.psum_scatter(out_grad_local.T, ("dp", "mp"), scatter_dimension=0, tiled=True),
        lax.psum_scatter(small_grads, ("dp", "mp"), scatter_dimension=0, tiled=True),
    )
    ffn_up_sum, ffn_down_sum = (
        lax.psum_scatter(ffn_up_grad, "dp", scatter_dimension=0, tiled=True),
        lax.psum_scatter(ffn_down_grad.T, "dp", scatter_dimension=0, tiled=True),
    )
    return (
        latent_out,
        latent_grad,
        media_grad,
        small_sum[:, 0],
        small_sum[:, 1],
        small_sum[:, 2],
        small_sum[:, 3],
        small_sum[:, 6:].T,
        query_sum,
        kv_sum,
        out_sum.T,
        small_sum[:, 4],
        small_sum[:, 5],
        ffn_up_sum,
        ffn_down_sum.T,
    )


def solution(mesh):
    placed = (
        P("dp", "mp", None),
        P("dp"),
        P("dp", "mp", None),
        P(),
        P(),
        P(),
        P(),
        P(),
        P(),
        P(),
        P(),
        P(),
        P(),
        P(None, "mp"),
        P("mp", None),
        P("dp", "mp", None),
    )
    chips, size = mesh.shape["dp"], mesh.shape["mp"]

    def device(*arrays):
        tiled = arrays[0].shape[-1] % (chips * size * 16) == 0 and arrays[2].shape[1] % 16 == 0
        if tiled and chips == 16:
            return per_device(chips, size, *arrays)
        return plain_device(*arrays)

    return jax.shard_map(
        device,
        mesh=mesh,
        in_specs=placed,
        out_specs=(
            P("dp", "mp", None),
            P("dp", "mp", None),
            P("dp", "mp", None),
            P(("dp", "mp")),
            P(("dp", "mp")),
            P(("dp", "mp")),
            P(("dp", "mp")),
            P(None, ("dp", "mp")),
            P(("dp", "mp"), None),
            P(("dp", "mp"), None),
            P(None, ("dp", "mp")),
            P(("dp", "mp")),
            P(("dp", "mp")),
            P("dp", "mp"),
            P("mp", "dp"),
        ),
        check_vma=False,
    )
```

```python
import functools

import jax
import jax.numpy as jnp
from jax import lax
from jax.experimental import pallas as pl
from jax.experimental.pallas import tpu as pltpu
from jax.sharding import PartitionSpec as P

HEADS = 16
HEAD_DIM = 96
PATCH = 256
GROUP = 4
SPAN = GROUP * HEAD_DIM
GROUPS = HEADS // GROUP
LATENT_PAD = 32
EPSILON = 1e-05
SCALE = HEAD_DIM ** (-0.5)
F32 = jnp.float32
BF16 = jnp.bfloat16
MESH = pl.DeviceIdType.MESH
VMEM_LIMIT = 60 * 1024 * 1024

VMEM = pl.BlockSpec(memory_space=pltpu.VMEM)
SMEM = pl.BlockSpec(memory_space=pltpu.SMEM)
ANY = pl.BlockSpec(memory_space=pl.ANY)


def dot(left, right, left_axis, right_axis):
    return lax.dot_general(
        left,
        right,
        (((left_axis,), (right_axis,)), ((), ())),
        preferred_element_type=F32,
    )


def normalize(rows):
    mean = jnp.mean(rows, -1, keepdims=True)
    centered = rows - mean
    variance = jnp.mean(centered * centered, -1, keepdims=True)
    inverse = lax.rsqrt(variance + EPSILON)
    return centered * inverse, inverse


def norm_back(unit, inverse, gain, gradient):
    scaled = gradient * gain
    return inverse * (
        scaled
        - jnp.mean(scaled, -1, keepdims=True)
        - unit * jnp.mean(scaled * unit, -1, keepdims=True)
    )


def lane_head(rows):
    column = lax.broadcasted_iota(jnp.int32, (rows, SPAN), 1)
    head = jnp.zeros((rows, SPAN), jnp.int32)
    for h in range(1, GROUP):
        head += (column >= h * HEAD_DIM).astype(jnp.int32)
    return head


def spread_heads(rows):
    head = lane_head(rows.shape[0])
    zero = jnp.zeros_like(rows)
    return jnp.concatenate([jnp.where(head == h, rows, zero) for h in range(GROUP)], 0)


def fold_heads(rows):
    count = rows.shape[0] // GROUP
    head = lane_head(count)
    total = jnp.zeros((count, SPAN), F32)
    for h in range(GROUP):
        total += jnp.where(head == h, rows[h * count : (h + 1) * count], 0.0)
    return total


def dot_exact(left, selector):
    total = None
    for _ in range(3):
        term = left.astype(BF16)
        left = left - term.astype(F32)
        part = dot(term, selector, 1, 0)
        total = part if total is None else total + part
    return total


def head_selector():
    low = lax.broadcasted_iota(jnp.int32, (128, HEADS * HEAD_DIM), 0) * HEAD_DIM
    column = lax.broadcasted_iota(jnp.int32, (128, HEADS * HEAD_DIM), 1)
    return ((column >= low) & (column < low + HEAD_DIM)).astype(F32).astype(BF16)


def head_sums(rows):
    count = rows.shape[0]
    head = lane_head(count)
    lane = lax.broadcasted_iota(jnp.int32, (count, 128), 1)
    result = jnp.zeros((count, 128), F32)
    for group in range(GROUPS):
        span = rows[:, group * SPAN : (group + 1) * SPAN]
        for h in range(GROUP):
            total = jnp.sum(jnp.where(head == h, span, 0.0), 1, keepdims=True)
            result += jnp.where(lane == group * GROUP + h, total, 0.0)
    return result


def own_columns(rows, head):
    lane = lax.broadcasted_iota(jnp.int32, rows.shape, 1)
    return jnp.sum(jnp.where(lane == head, rows, 0.0), 1, keepdims=True)


def across_lanes(column):
    return jnp.transpose(jnp.broadcast_to(column, (column.shape[0], 128)))[0:1]


def down_rows(row):
    return jnp.transpose(jnp.broadcast_to(row, (128, row.shape[1])))


def vector(ref):
    return ref[...].astype(F32).reshape(1, ref.shape[-1])


def gelu_parts(pre):
    cdf = 0.5 * (1.0 + lax.erf(pre * (0.5**0.5)))
    return pre * cdf, cdf + pre * (jnp.exp(-0.5 * pre * pre) * 0.3989422804014327)


def params(**more):
    return pltpu.CompilerParams(vmem_limit_bytes=VMEM_LIMIT, **more)


def greet(devices):
    barrier = pltpu.get_barrier_semaphore()
    for device in devices:
        pl.semaphore_signal(barrier, inc=1, device_id=device, device_id_type=MESH)
    pl.semaphore_wait(barrier, len(devices))


def others(axis_size, me):
    return [lax.rem(me + k, axis_size) for k in range(1, axis_size)]


class Place:
    def __init__(self, lines, size, send_sem, recv_sem):
        self.lines, self.size = lines, size
        self.dp, self.me = lax.axis_index("dp"), lax.axis_index("mp")
        self.line = self.dp // 4
        self.high = lax.rem(self.dp // 2, 2)
        self.low = lax.rem(self.dp, 2)
        self.send_sem, self.recv_sem = send_sem, recv_sem
        self.used = 0

    def at(self, line, high, low):
        return (line * 4 + high * 2 + low, self.me)

    def low_peer(self):
        return self.at(self.line, self.high, 1 - self.low)

    def high_peer(self):
        return self.at(self.line, 1 - self.high, self.low)

    def across(self):
        return self.at(self.line, 1 - self.high, 1 - self.low)

    def greet(self):
        greet(
            [self.low_peer(), self.high_peer(), self.across()]
            + [self.at(peer, self.high, self.low) for peer in others(self.lines, self.line)]
            + [(self.dp, peer) for peer in others(self.size, self.me)]
        )

    def exchange(self, source, target, land, device):
        index = self.used
        self.used += 1

        def copy(destination):
            return pltpu.make_async_remote_copy(
                src_ref=source,
                dst_ref=destination,
                send_sem=self.send_sem.at[index],
                recv_sem=self.recv_sem.at[index],
                device_id=device,
                device_id_type=MESH,
            )

        pair = (copy(target), copy(land))
        pair[0].start()
        return pair

    def swap(self, me, count, device_of, source_of, land_of):
        pairs = []
        for k in range(1, count):
            peer, origin = lax.rem(me + k, count), lax.rem(me + count - k, count)
            pairs.append(
                self.exchange(source_of(peer), land_of(me), land_of(origin), device_of(peer))
            )
        return pairs

    def swap_cores(self, source_of, land_of):
        return self.swap(self.me, self.size, lambda p: (self.dp, p), source_of, land_of)

    def swap_lines(self, source_of, land_of):
        return self.swap(
            self.line, self.lines, lambda p: self.at(p, self.high, self.low), source_of, land_of
        )


def finish_sends(pairs):
    for copy, _ in pairs:
        copy.wait_send()


def finish_arrivals(pairs):
    for _, arrival in pairs:
        arrival.wait_recv()


def finish(pairs):
    finish_arrivals(pairs)
    finish_sends(pairs)


class Gather:
    def __init__(self, place, rows, out, sem):
        self.place, self.rows, self.out, self.sem = place, rows, out, sem

    def along_line(self):
        p, out = self.place, self.out
        self.keep = pltpu.make_async_copy(
            self.rows, out.at[p.line, p.high, p.low], self.sem
        )
        self.keep.start()
        self.pairs = p.swap_lines(
            lambda peer: self.rows, lambda line: out.at[line, p.high, p.low]
        )

    def first_half(self):
        p, out = self.place, self.out
        self.keep.wait()
        finish(self.pairs)
        half = p.lines // 2
        near, far = pl.ds(0, half), pl.ds(half, p.lines - half)
        self.pairs = [
            p.exchange(
                out.at[near, p.high, p.low],
                out.at[near, p.high, p.low],
                out.at[near, p.high, 1 - p.low],
                p.low_peer(),
            ),
            p.exchange(
                out.at[far, p.high, p.low],
                out.at[far, p.high, p.low],
                out.at[far, 1 - p.high, p.low],
                p.high_peer(),
            ),
        ]

    def second_half(self):
        p, out = self.place, self.out
        finish(self.pairs)
        half = p.lines // 2
        near, far = pl.ds(0, half), pl.ds(half, p.lines - half)
        self.pairs = [
            p.exchange(
                out.at[near, p.high],
                out.at[near, p.high],
                out.at[near, 1 - p.high],
                p.high_peer(),
            ),
            p.exchange(
                out.at[far, :, p.low],
                out.at[far, :, p.low],
                out.at[far, :, 1 - p.low],
                p.low_peer(),
            ),
        ]

    def end(self):
        finish(self.pairs)


class Scatter:
    def __init__(self, place, blocks, lands, temp, sem, out):
        self.place, self.blocks, self.lands, self.out = place, blocks, lands, out
        self.temp, self.sem = temp, sem

    @staticmethod
    def lands(lines, rows, columns):
        half = lines // 2
        return [
            jax.ShapeDtypeStruct((2, half, 2, rows, columns), BF16),
            jax.ShapeDtypeStruct((2, half, rows, columns), BF16),
            jax.ShapeDtypeStruct((lines, rows, columns), BF16),
        ]

    def load(self, pairs):
        copies = [
            pltpu.make_async_copy(source, target, self.sem.at[k])
            for k, (source, target) in enumerate(pairs)
        ]
        for copy in copies:
            copy.start()
        for copy in copies:
            copy.wait()

    def first_half(self):
        p, blocks, land = self.place, self.blocks, self.lands[0]
        half = p.lines // 2
        near, far = pl.ds(0, half), pl.ds(half, half)
        self.pairs = [
            p.exchange(blocks.at[near, :, 1 - p.low], land.at[0], land.at[0], p.low_peer()),
            p.exchange(blocks.at[far, 1 - p.high], land.at[1], land.at[1], p.high_peer()),
        ]

    def second_half(self):
        p, blocks, land, into, temp = self.place, self.blocks, *self.lands[:2], self.temp
        half = p.lines // 2
        near, far = pl.ds(0, half), pl.ds(half, half)
        finish(self.pairs)
        self.load([(land.at[k], temp.at[k, :, :, 0]) for k in range(2)])

        @pl.loop(0, half)
        def _(line):
            for k in range(2):
                mine = blocks[line, k, p.low].astype(F32) + temp[0, line, k, 0].astype(F32)
                blocks[line, k, p.low] = mine.astype(BF16)
                mine = blocks[half + line, p.high, k].astype(F32) + temp[1, line, k, 0].astype(F32)
                blocks[half + line, p.high, k] = mine.astype(BF16)

        self.pairs = [
            p.exchange(blocks.at[near, 1 - p.high, p.low], into.at[0], into.at[0], p.high_peer()),
            p.exchange(blocks.at[far, p.high, 1 - p.low], into.at[1], into.at[1], p.low_peer()),
        ]

    def mine(self, line):
        return self.blocks.at[line, self.place.high, self.place.low]

    def plane_sum(self):
        p, blocks, temp, into = self.place, self.blocks, self.temp, self.lands[1]
        half = p.lines // 2
        finish(self.pairs)
        self.load([(into.at[k], temp.at[k, :, 0, 0]) for k in range(2)])

        @pl.loop(0, half)
        def _(line):
            for k in range(2):
                mine = blocks[k * half + line, p.high, p.low].astype(F32)
                mine += temp[k, line, 0, 0].astype(F32)
                blocks[k * half + line, p.high, p.low] = mine.astype(BF16)

    def line_low(self):
        p, land = self.place, self.lands[2]
        high, low = p.line // 2, lax.rem(p.line, 2)
        peer = p.at(2 * high + 1 - low, p.high, p.low)
        self.pairs = [
            p.exchange(self.mine(2 * k + 1 - low), land.at[k], land.at[k], peer) for k in range(2)
        ]

    def line_high(self):
        p, land, temp = self.place, self.lands[2], self.temp
        high, low = p.line // 2, lax.rem(p.line, 2)
        finish(self.pairs)
        self.load([(land.at[k], temp.at[k, 0, 0, 0]) for k in range(2)])
        for k in range(2):
            mine = self.mine(2 * k + low)
            mine[...] = (mine[...].astype(F32) + temp[k, 0, 0, 0].astype(F32)).astype(BF16)
        peer = 2 * (1 - high) + low
        self.pairs = [
            p.exchange(self.mine(peer), land.at[2], land.at[2], p.at(peer, p.high, p.low))
        ]

    def end(self):
        land, temp = self.lands[2], self.temp
        finish(self.pairs)
        self.load([(land.at[2], temp.at[0, 0, 0, 0])])
        mine = self.mine(self.place.line)
        self.out[...] = mine[...].astype(F32) + temp[0, 0, 0, 0].astype(F32)


class NearScatter(Scatter):
    def second_half(self):
        p, blocks, land, into = self.place, self.blocks, self.lands[0], self.lands[1]
        half = p.lines // 2
        near, far = pl.ds(0, half), pl.ds(half, half)
        finish(self.pairs)

        @pl.loop(0, half)
        def _(line):
            for k in range(2):
                mine = blocks[line, k, p.low].astype(F32) + land[0, line, k].astype(F32)
                blocks[line, k, p.low] = mine.astype(BF16)
                mine = blocks[half + line, p.high, k].astype(F32) + land[1, line, k].astype(F32)
                blocks[half + line, p.high, k] = mine.astype(BF16)

        self.pairs = [
            p.exchange(blocks.at[near, 1 - p.high, p.low], into.at[0], into.at[0], p.high_peer()),
            p.exchange(blocks.at[far, p.high, 1 - p.low], into.at[1], into.at[1], p.low_peer()),
        ]

    def plane_sum(self):
        p, blocks, into = self.place, self.blocks, self.lands[1]
        half = p.lines // 2
        finish(self.pairs)

        @pl.loop(0, half)
        def _(line):
            for k in range(2):
                mine = blocks[k * half + line, p.high, p.low].astype(F32)
                mine += into[k, line].astype(F32)
                blocks[k * half + line, p.high, p.low] = mine.astype(BF16)

    def send_line(self):
        land = self.lands[2]
        self.pairs = self.place.swap_lines(self.mine, lambda line: land.at[line])

    def end_line(self):
        p, land = self.place, self.lands[2]
        finish(self.pairs)
        total = self.mine(p.line)[...].astype(F32)
        for peer in others(p.lines, p.line):
            total += land[peer].astype(F32)
        self.out[...] = total


class LineSum(Scatter):
    def mine(self, line):
        return self.blocks.at[line]


class Move:
    def __init__(self, place, blocks, middle, out, sem):
        self.place, self.blocks, self.middle, self.out, self.sem = place, blocks, middle, out, sem

    def along_line(self):
        p, blocks, middle = self.place, self.blocks, self.middle
        self.keep = pltpu.make_async_copy(blocks.at[p.line], middle.at[p.line], self.sem.at[0])
        self.keep.start()
        self.pairs = p.swap_lines(lambda peer: blocks.at[peer], lambda line: middle.at[line])

    def in_plane(self):
        p, middle, out = self.place, self.middle, self.out
        self.keep.wait()
        finish(self.pairs)
        self.keep = pltpu.make_async_copy(
            middle.at[:, p.high, p.low], out.at[:, p.high, p.low], self.sem.at[1]
        )
        self.keep.start()
        self.pairs = []
        for device, high, low in (
            (p.low_peer(), p.high, 1 - p.low),
            (p.high_peer(), 1 - p.high, p.low),
            (p.across(), 1 - p.high, 1 - p.low),
        ):
            self.pairs.append(
                p.exchange(
                    middle.at[:, high, low],
                    out.at[:, p.high, p.low],
                    out.at[:, high, low],
                    device,
                )
            )

    def end(self):
        self.keep.wait()
        finish(self.pairs)


class Total:
    def __init__(self, place, array, land, sums):
        self.place, self.array, self.land, self.sums = place, array, land, sums

    @staticmethod
    def scratch(lines, size, shape):
        return [pltpu.VMEM((size + 2 + lines,) + shape, F32), pltpu.VMEM((3,) + shape, F32)]

    def in_chip(self):
        self.pairs = self.place.swap_cores(lambda peer: self.array, lambda core: self.land.at[core])

    def low(self):
        p = self.place
        finish(self.pairs)
        total = self.array[...]
        for peer in others(p.size, p.me):
            total += self.land[peer]
        self.sums[0] = total
        land = self.land.at[p.size]
        self.pairs = [p.exchange(self.sums.at[0], land, land, p.low_peer())]

    def high(self):
        p = self.place
        finish(self.pairs)
        self.sums[1] = self.sums[0] + self.land[p.size]
        land = self.land.at[p.size + 1]
        self.pairs = [p.exchange(self.sums.at[1], land, land, p.high_peer())]

    def along_line(self):
        p = self.place
        finish(self.pairs)
        self.sums[2] = self.sums[1] + self.land[p.size + 1]
        self.pairs = p.swap_lines(
            lambda peer: self.sums.at[2], lambda line: self.land.at[p.size + 2 + line]
        )

    def end(self, out):
        p = self.place
        finish(self.pairs)
        total = self.sums[2]
        for peer in others(p.lines, p.line):
            total += self.land[p.size + 2 + peer]
        out[...] = total


ROWS = 64


def in_order(first_full, pair):
    return jnp.where(first_full, pair[0], pair[1]), jnp.where(first_full, pair[1], pair[0])


def half_gathers(place, rows, out, sem):
    count = rows.shape[0] // 2
    return [
        Gather(
            place,
            rows.at[pl.ds(k * count, count)],
            out.at[:, :, :, pl.ds(k * count, count)],
            sem.at[k],
        )
        for k in range(2)
    ]


def forward_kernel(
    frames,
    lines,
    size,
    counts,
    media,
    latents,
    cotangent,
    gain_media,
    shift_media,
    gain_latent,
    shift_latent,
    time_embed,
    query_hbm,
    kv_hbm,
    norm_full_out,
    norm_image_out,
    weight_full_out,
    weight_image_out,
    absorbed_out,
    mixed_out,
    value_out,
    peak_out,
    latent_norm,
    queries,
    cotangent_all,
    cotangent_rows,
    own,
    latent_all,
    norm_full,
    norm_image,
    weight_full,
    weight_image,
    absorbed,
    mixed,
    query_weight,
    kv_weight,
    buffer,
    times,
    media_sem,
    load_sem,
    store_sem,
    gather_sem,
    send_sem,
    recv_sem,
):
    inner = HEADS * HEAD_DIM
    place = Place(lines, size, send_sem, recv_sem)
    me = place.me
    local = latents.shape[1]
    rows = 2 * local
    lat_all = local * size
    first_full = counts[0] > counts[1]
    image_alive = me * frames < jnp.minimum(counts[0], counts[1])

    def fetch(frame, slot):
        return pltpu.make_async_copy(
            media.at[:, pl.ds(frame * PATCH, PATCH)], buffer.at[slot], media_sem.at[slot]
        )

    load_query = pltpu.make_async_copy(query_hbm, query_weight, load_sem.at[0])
    load_kv = pltpu.make_async_copy(kv_hbm, kv_weight, load_sem.at[1])
    times[...] = time_embed[...].astype(F32)
    fetch(0, 0).start()
    load_query.start()
    load_kv.start()
    place.greet()
    for k, array in ((0, latents), (1, cotangent)):
        pair = in_order(first_full, (array[0].astype(F32), array[1].astype(F32)))
        own[k] = jnp.concatenate(pair, 0).astype(BF16)
    latent_swap = place.swap_cores(lambda p: own.at[0], lambda c: latent_all.at[c])
    cotangent_swap = place.swap_cores(lambda p: own.at[1], lambda c: cotangent_all.at[c])
    gathers = half_gathers(place, own.at[1], cotangent_rows, gather_sem)
    gathers[0].along_line()
    latent_all[me] = own[0]
    cotangent_all[me] = own[1]

    gain_m, shift_m = vector(gain_media), vector(shift_media)
    gain_l, shift_l = vector(gain_latent), vector(shift_latent)

    def normalize_frame(frame, slot, pick_first, target, base):
        time_row = times[pl.ds(me * frames + frame, 1)]

        @pl.loop(0, PATCH // ROWS)
        def _(part):
            at = pl.multiple_of(part * ROWS, ROWS)
            values = jnp.where(
                pick_first,
                buffer[slot, 0, pl.ds(at, ROWS)].astype(F32),
                buffer[slot, 1, pl.ds(at, ROWS)].astype(F32),
            )
            unit, _ = normalize(values + time_row)
            target[pl.ds(pl.multiple_of(base + at, ROWS), ROWS)] = (unit * gain_m + shift_m).astype(
                BF16
            )

    @pl.loop(0, frames)
    def _(frame):
        slot = lax.rem(frame, 2)
        fetch(frame, slot).wait()

        @pl.when(frame + 1 < frames)
        def _():
            fetch(frame + 1, 1 - slot).start()

        normalize_frame(frame, slot, first_full, norm_full, frame * PATCH)

        @pl.when(frame == 0)
        def _():
            normalize_frame(frame, slot, jnp.logical_not(first_full), norm_image, 0)

    unit, _ = normalize(own[0].astype(F32))
    low = (unit * gain_l + shift_l).astype(BF16)
    norm_full[frames * PATCH : frames * PATCH + local] = low[:local]
    norm_image[PATCH : PATCH + local] = low[local:]
    finish(latent_swap)
    for item in range(2):
        for core in range(size):
            unit, _ = normalize(latent_all[core, item * local : (item + 1) * local].astype(F32))
            at = item * lat_all + core * local
            latent_norm[at : at + local] = (unit * gain_l + shift_l).astype(BF16)
    stores = []

    def store(source, target):
        copy = pltpu.make_async_copy(source, target, store_sem.at[len(stores)])
        copy.start()
        stores.append(copy)

    store(norm_full, norm_full_out)
    store(norm_image, norm_image_out)
    load_query.wait()

    @pl.loop(0, GROUPS)
    def _(group):
        span = pl.ds(pl.multiple_of(group * SPAN, SPAN), SPAN)
        queries[:, span] = dot(latent_norm[...], query_weight[:, span], 1, 0).astype(BF16)

    load_kv.wait()
    step = GROUP * lat_all
    lane = lax.broadcasted_iota(jnp.int32, (lat_all, 128), 1)
    outer_lane = lax.broadcasted_iota(jnp.int32, (rows, 128), 1)
    for core in range(size):
        peak_out[core, 0] = jnp.zeros((rows, 128), F32)
        peak_out[core, 1] = jnp.where(outer_lane < HEADS, 0.0, 1.0)
    for item, keys, weights, weights_out in (
        (0, norm_full, weight_full, weight_full_out),
        (1, norm_image, weight_image, weight_image_out),
    ):
        count = keys.shape[0]
        row = lax.broadcasted_iota(jnp.int32, (count, 1), 0)
        live = (row >= count - local) | image_alive

        def attend_group(group, item=item, keys=keys, weights=weights, live=live):
            span = pl.ds(pl.multiple_of(group * SPAN, SPAN), SPAN)
            value_span = pl.ds(pl.multiple_of(inner + group * SPAN, SPAN), SPAN)
            at = pl.ds(pl.multiple_of(group * step, step), step)
            spread = spread_heads(queries[item * lat_all : (item + 1) * lat_all, span])
            key_rows = (dot(spread, kv_weight[:, span], 1, 1) * SCALE).astype(BF16)
            absorbed[item, at] = key_rows
            scores = dot(keys[...], key_rows, 1, 1)
            if item == 1:
                scores = jnp.where(live, scores, -1e30)
            peak = jnp.max(scores, 0, keepdims=True)
            weight = jnp.exp(scores - peak)
            if item == 1:
                weight = jnp.where(live, weight, 0.0)
            total = jnp.sum(weight, 0, keepdims=True)
            low = weight.astype(BF16)
            weights[:, at] = low
            mix = dot(low, keys[...], 0, 0).astype(BF16)
            mixed[item, at] = mix
            values = fold_heads(dot(mix, kv_weight[:, value_span], 1, 0))
            statistics = []
            for row_values in (peak, total):
                down = down_rows(row_values)
                picked = jnp.zeros((lat_all, 128), F32)
                for h in range(GROUP):
                    rows_of_head = down[h * lat_all : (h + 1) * lat_all]
                    picked += jnp.where(lane == group * GROUP + h, rows_of_head, 0.0)
                statistics.append(picked)
            for core in range(size):
                mine = slice(core * local, (core + 1) * local)
                into = slice(item * local, (item + 1) * local)
                value_out[core, into, span] = values[mine]
                for k in range(2):
                    peak_out[core, k, into] += statistics[k][mine]

        if item == 0:
            gathers[0].first_half()
            gathers[1].along_line()
            pl.loop(0, 1)(attend_group)
            gathers[0].second_half()
            pl.loop(1, 2)(attend_group)
            gathers[1].first_half()
            pl.loop(2, GROUPS)(attend_group)
            gathers[1].second_half()
        else:
            pl.loop(0, GROUPS)(attend_group)
        store(weights, weights_out)
        store(absorbed.at[item], absorbed_out.at[item])
        store(mixed.at[item], mixed_out.at[item])
    for copy in stores:
        copy.wait()
    finish(cotangent_swap)
    for gather in gathers:
        gather.end()


def attend_forward(
    chips,
    size,
    counts,
    media,
    latents,
    cotangent,
    gain_media,
    shift_media,
    gain_latent,
    shift_latent,
    time_embed,
    query_weight,
    kv_weight,
):
    width = media.shape[-1]
    inner = HEADS * HEAD_DIM
    lines = chips // 4
    frames = media.shape[1] // PATCH
    local = latents.shape[1]
    rows = 2 * local
    lat_all = local * size
    keys = (frames * PATCH + local, PATCH + local)
    slots = HEADS * lat_all
    shape = jax.ShapeDtypeStruct
    copies = 2 * lines + 2 * size + 16
    return pl.pallas_call(
        functools.partial(forward_kernel, frames, lines, size),
        out_shape=[
            shape((keys[0], width), BF16),
            shape((keys[1], width), BF16),
            shape((keys[0], slots), BF16),
            shape((keys[1], slots), BF16),
            shape((2, slots, width), BF16),
            shape((2, slots, width), BF16),
            shape((size, rows, inner), F32),
            shape((size, 2, rows, 128), F32),
            shape((2 * lat_all, width), BF16),
            shape((2 * lat_all, inner), BF16),
            shape((size, rows, width), BF16),
            shape((lines, 2, 2, rows, width), BF16),
        ],
        in_specs=[SMEM, ANY] + [VMEM] * 7 + [ANY] * 2,
        out_specs=[ANY] * 6 + [VMEM] * 5 + [ANY],
        scratch_shapes=[
            pltpu.VMEM((2, rows, width), BF16),
            pltpu.VMEM((size, rows, width), BF16),
            pltpu.VMEM((keys[0], width), BF16),
            pltpu.VMEM((keys[1], width), BF16),
            pltpu.VMEM((keys[0], slots), BF16),
            pltpu.VMEM((keys[1], slots), BF16),
            pltpu.VMEM((2, slots, width), BF16),
            pltpu.VMEM((2, slots, width), BF16),
            pltpu.VMEM(query_weight.shape, BF16),
            pltpu.VMEM(kv_weight.shape, BF16),
            pltpu.VMEM((2, 2, PATCH, width), BF16),
            pltpu.VMEM(time_embed.shape, F32),
            pltpu.SemaphoreType.DMA((2,)),
            pltpu.SemaphoreType.DMA((2,)),
            pltpu.SemaphoreType.DMA((8,)),
            pltpu.SemaphoreType.DMA((2,)),
            pltpu.SemaphoreType.DMA((copies,)),
            pltpu.SemaphoreType.DMA((copies,)),
        ],
        compiler_params=params(collective_id=0, has_side_effects=True),
    )(
        counts,
        media,
        latents,
        cotangent,
        gain_media,
        shift_media,
        gain_latent,
        shift_latent,
        time_embed,
        query_weight,
        kv_weight,
    )


DEPTH = 2


def latent_kernel(
    lines,
    size,
    chunk,
    counts,
    value_parts,
    peaks,
    latents,
    cotangent_all,
    gain_ffn,
    shift_ffn,
    out_hbm,
    in_hbm,
    down_hbm,
    kv_hbm,
    mixed_hbm,
    norm_full_hbm,
    norm_image_hbm,
    weight_full_hbm,
    weight_image_hbm,
    cotangent_rows,
    queries,
    latent_norm,
    latent_out,
    state_grad,
    gains,
    into_out,
    score_full_out,
    score_image_out,
    query_all,
    out_plane,
    query_half,
    key_half,
    value_half,
    ffn_rows,
    cotangent_other,
    key_wait,
    value_wait,
    out_first,
    out_second,
    out_weight,
    in_weight,
    down_weight,
    column_weight,
    norm_full,
    norm_image,
    weight_full,
    weight_image,
    score_full,
    score_image,
    mixed,
    value_land,
    peak_land,
    ffn_norm,
    partial,
    partial_land,
    kept,
    kept_log,
    attended_all,
    update_all,
    grad_all,
    log_all,
    grad_items,
    stage,
    query_part,
    query_land,
    out_blocks,
    temp,
    load_sem,
    weight_sem,
    column_sem,
    half_sem,
    store_sem,
    scatter_sem,
    gather_sem,
    send_sem,
    recv_sem,
):
    inner = HEADS * HEAD_DIM
    place = Place(lines, size, send_sem, recv_sem)
    me = place.me
    first_full = counts[0] > counts[1]
    local, width = latents.shape[1:]
    rows = 2 * local
    lat_all = local * size
    step = GROUP * lat_all
    chunks = in_hbm.shape[1] // chunk
    cores = others(size, me)

    def weights(c):
        at = pl.ds(pl.multiple_of(c * chunk, chunk), chunk)
        slot = lax.rem(c, DEPTH)
        return (
            pltpu.make_async_copy(in_hbm.at[:, at], in_weight.at[slot], weight_sem.at[0, slot]),
            pltpu.make_async_copy(down_hbm.at[at, :], down_weight.at[slot], weight_sem.at[1, slot]),
        )

    loads = [
        pltpu.make_async_copy(out_hbm, out_weight, load_sem.at[0]),
        pltpu.make_async_copy(mixed_hbm, mixed, load_sem.at[1]),
        pltpu.make_async_copy(norm_full_hbm, norm_full, load_sem.at[2]),
        pltpu.make_async_copy(norm_image_hbm, norm_image, load_sem.at[3]),
        pltpu.make_async_copy(weight_full_hbm, weight_full, load_sem.at[4]),
        pltpu.make_async_copy(weight_image_hbm, weight_image, load_sem.at[5]),
    ]

    def column(n):
        first = inner + n * SPAN if n < GROUPS else (n - GROUPS) * SPAN
        return pltpu.make_async_copy(
            kv_hbm.at[:, pl.ds(first, SPAN)], column_weight.at[n % 2], column_sem.at[n % 2]
        )

    loads[0].start()
    for c in range(min(DEPTH, chunks)):
        for copy in weights(c):
            copy.start()
    for copy in loads[1:]:
        copy.start()
    column(0).start()
    place.greet()
    values_swap = place.swap_cores(lambda p: value_parts.at[p], lambda c: value_land.at[c])
    peaks_swap = place.swap_cores(lambda p: peaks.at[p], lambda c: peak_land.at[c])
    cotangent_swap = place.swap_cores(
        lambda p: cotangent_rows, lambda c: cotangent_other.at[c]
    )
    value_land[me] = value_parts[me]
    peak_land[me] = peaks[me]
    selector = head_selector()
    finish(values_swap)
    finish(peaks_swap)
    peak = peak_land[0, 0]
    for s in range(1, size):
        peak = jnp.maximum(peak, peak_land[s, 0])
    factors = [jnp.exp(peak_land[s, 0] - peak) for s in range(size)]
    total = factors[0] * peak_land[0, 1]
    for s in range(1, size):
        total += factors[s] * peak_land[s, 1]
    kept_log[...] = peak + jnp.log(total)
    attended = jnp.zeros((rows, width), F32)
    for s in range(size):
        attended += value_land[s] * dot_exact(factors[s] / total, selector)
    kept[0] = attended
    attended_low = attended.astype(BF16)
    attended_all[me] = attended_low
    loads[0].wait()
    hidden = dot(attended_low, out_weight[...], 1, 0)
    hidden += jnp.concatenate(
        in_order(first_full, (latents[0].astype(F32), latents[1].astype(F32))), 0
    )
    kept[1] = hidden
    gain, shift = vector(gain_ffn), vector(shift_ffn)
    unit, _ = normalize(hidden)
    ffn_norm[me] = (unit * gain + shift).astype(BF16)
    norm_swap = place.swap_cores(lambda p: ffn_norm.at[me], lambda c: ffn_norm.at[c])
    gather = Gather(place, ffn_norm.at[me], ffn_rows, gather_sem.at[0])
    gather.along_line()
    attended_swap = place.swap_cores(lambda p: attended_all.at[me], lambda c: attended_all.at[c])
    partial[...] = jnp.zeros_like(partial)
    finish(norm_swap)

    def feed_forward(c):
        for copy in weights(c):
            copy.wait()
        slot = lax.rem(c, DEPTH)
        all_rows = ffn_norm[...].reshape(size * rows, width)
        cotangents = cotangent_all[...].reshape(size * rows, width)
        activated, slope = gelu_parts(dot(all_rows, in_weight[slot], 1, 0))
        activated = activated.astype(BF16)
        act_grad = dot(cotangents, down_weight[slot], 1, 1)
        pre_grad = (act_grad * slope).astype(BF16)
        partial[0] += dot(activated, down_weight[slot], 1, 0).reshape(size, rows, width)
        partial[1] += dot(pre_grad, in_weight[slot], 1, 1).reshape(size, rows, width)

        @pl.when(c + DEPTH < chunks)
        def _():
            for copy in weights(c + DEPTH):
                copy.start()

    pl.loop(0, chunks)(feed_forward)
    sums_swap = place.swap_cores(lambda p: partial.at[:, p], lambda c: partial_land.at[c])
    gather.first_half()
    finish(sums_swap)
    ffn_sum, norm_grad = partial[0, me], partial[1, me]
    for origin in cores:
        ffn_sum += partial_land[origin, 0]
        norm_grad += partial_land[origin, 1]
    hidden = kept[1]
    unit, inverse = normalize(hidden)
    result = hidden + ffn_sum
    for k, value in enumerate(in_order(first_full, (result[:local], result[local:]))):
        latent_out[k] = value.astype(BF16)
    gains[0:1] = jnp.sum(norm_grad * unit, 0, keepdims=True)
    gains[1:2] = jnp.sum(norm_grad, 0, keepdims=True)
    state = cotangent_all[me].astype(F32) + norm_back(unit, inverse, gain, norm_grad)
    state_grad[...] = state
    update = state.astype(BF16)
    update_all[me] = update
    grad = dot(update, out_weight[...], 1, 1).astype(BF16)
    grad_all[me] = grad
    log_all[me, 0] = kept_log[...]
    log_all[me, 1] = head_sums(grad.astype(F32) * kept[0])
    grad_swap = place.swap_cores(lambda p: grad_all.at[me], lambda c: grad_all.at[c])
    log_swap = place.swap_cores(lambda p: log_all.at[me], lambda c: log_all.at[c])
    update_swap = place.swap_cores(lambda p: update_all.at[me], lambda c: update_all.at[c])
    finish(grad_swap)
    finish(log_swap)

    def by_item(item, of_core):
        part = slice(item * local, (item + 1) * local)
        return jnp.concatenate([of_core(core)[part] for core in range(size)], 0)

    factor, factor_delta = [], []
    for item in range(2):
        grad_items[item] = by_item(item, lambda c: grad_all[c])
        scale = jnp.exp(
            by_item(item, lambda c: peaks[c, 0]) - by_item(item, lambda c: log_all[c, 0])
        )
        factor.append(scale)
        factor_delta.append(scale * by_item(item, lambda c: log_all[c, 1]))
    block_rows = width // (lines * 4 * size)
    uses = []

    def stage_blocks(low):
        slot = len(uses) % 2
        if len(uses) >= 2:
            sends, copy = uses[len(uses) - 2]
            finish_sends(sends)
            copy.wait()
        for k in range(lines * 4):
            for core in range(size):
                base = (k * size + core) * block_rows
                stage[slot, k // 4, (k // 2) % 2, k % 2, core] = low[base : base + block_rows]
        return slot

    def split_cores(low, group, half, wait):
        slot = stage_blocks(low)
        columns = pl.ds(group * SPAN, SPAN)
        sends = place.swap_cores(
            lambda p: stage.at[slot, :, :, :, p], lambda c: wait.at[c, :, :, :, :, columns]
        )
        keep_half(slot, columns, half, sends)

    def keep_half(slot, columns, half, sends):
        copy = pltpu.make_async_copy(
            stage.at[slot, :, :, :, me], half.at[:, :, :, :, columns], half_sem.at[slot]
        )
        copy.start()
        uses.append((sends, copy))

    stores = []

    def store(source, target):
        copy = pltpu.make_async_copy(source, target, store_sem.at[len(stores)])
        copy.start()
        stores.append(copy)

    outs = Scatter(place, out_blocks, (out_first, out_second, None), temp, scatter_sem, None)
    finish(attended_swap)
    finish(update_swap)
    updates = update_all[...].reshape(size * rows, width)
    for group in range(GROUPS):
        span = slice(group * SPAN, (group + 1) * SPAN)
        attends = attended_all[:, :, span].reshape(size * rows, SPAN)
        low = dot(updates, attends, 0, 0)
        for k in range(lines * 4):
            base = k * size * block_rows
            mine = low[base : base + block_rows]
            for core in range(1, size):
                base += block_rows
                mine = jnp.where(me == core, low[base : base + block_rows], mine)
            out_blocks[k // 4, (k // 2) % 2, k % 2, :, span] = mine.astype(BF16)
    outs.first_half()
    for copy in loads[1:]:
        copy.wait()
    shifts = []
    for group in range(GROUPS):
        span = slice(group * SPAN, (group + 1) * SPAN)
        at = slice(group * step, (group + 1) * step)
        column(group + 1).start()
        column(group).wait()
        weight = None
        for item in range(2):
            spread = spread_heads(grad_items[item, :, span])
            heads = range(group * GROUP, (group + 1) * GROUP)
            scale = jnp.concatenate([own_columns(factor[item], h) for h in heads], 0)
            shifts.append(
                across_lanes(
                    jnp.concatenate([own_columns(factor_delta[item], h) for h in heads], 0)
                )
            )
            spread = (spread.astype(F32) * scale).astype(BF16)
            part = dot(mixed[item, at], spread, 0, 0)
            weight = part if weight is None else weight + part
            mixed[item, at] = dot(spread, column_weight[group % 2], 1, 1).astype(BF16)
        split_cores(weight.astype(BF16), group, value_half, value_wait)
    for item in range(2):
        store(mixed.at[item], into_out.at[item])
    gather.second_half()
    for group in range(GROUPS):
        span = slice(group * SPAN, (group + 1) * SPAN)
        at = slice(group * step, (group + 1) * step)
        if group + 1 < GROUPS:
            column(GROUPS + group + 1).start()
        column(GROUPS + group).wait()
        weight = None
        for item, keys, weights, scores in (
            (0, norm_full, weight_full, score_full),
            (1, norm_image, weight_image, score_image),
        ):
            item_rows = slice(item * lat_all, (item + 1) * lat_all)
            prob_grad = dot(keys[...], mixed[item, at], 1, 1)
            score = weights[:, at].astype(F32) * (prob_grad - shifts[2 * group + item])
            score = score.astype(BF16)
            scores[:, at] = score
            pulled = dot(score, keys[...], 0, 0).astype(BF16)
            query_part[item_rows, span] = (
                fold_heads(dot(pulled, column_weight[group % 2], 1, 0)) * SCALE
            )
            part = dot(pulled, spread_heads(queries[item_rows, span]), 0, 0)
            weight = part if weight is None else weight + part
        split_cores((weight * SCALE).astype(BF16), group, key_half, key_wait)
        if group == 1:
            outs.second_half()
    store(score_full, score_full_out)
    store(score_image, score_image_out)
    query_swap = place.swap_cores(lambda p: query_part, lambda c: query_land.at[c])
    finish(query_swap)
    total_query = query_part[...]
    for origin in cores:
        total_query += query_land[origin]
    query_all[...] = total_query.astype(BF16)
    for group in range(GROUPS):
        span = slice(group * SPAN, (group + 1) * SPAN)
        slot = stage_blocks(dot(latent_norm[...], query_all[:, span], 0, 0).astype(BF16))
        keep_half(slot, pl.ds(group * SPAN, SPAN), query_half, [])
    for sends, copy in uses[-2:]:
        finish_sends(sends)
        copy.wait()
    for sends, _ in uses:
        finish_arrivals(sends)
    finish(cotangent_swap)
    outs.plane_sum()
    store(out_blocks.at[:, place.high, place.low], out_plane)
    gather.end()
    for copy in stores:
        copy.wait()


def latent_pass(
    chips,
    size,
    counts,
    value_parts,
    peaks,
    latents,
    cotangent_all,
    gain_ffn,
    shift_ffn,
    out_weight,
    in_weight,
    down_weight,
    kv_weight,
    mixed,
    norm_full,
    norm_image,
    weight_full,
    weight_image,
    cotangent_rows,
    queries,
    latent_norm,
):
    lines = chips // 4
    local, width = latents.shape[1:]
    inner = HEADS * HEAD_DIM
    rows = 2 * local
    lat_all = local * size
    hidden_units = in_weight.shape[1]
    chunk = 512 if hidden_units % 512 == 0 else 256
    block_rows = width // (chips * size)
    blocks = (lines, 2, 2, block_rows, inner)
    gathered = (lines, 2, 2, rows, width)
    shape = jax.ShapeDtypeStruct
    copies = 3 * lines + 24 * size + 20
    return pl.pallas_call(
        functools.partial(latent_kernel, lines, size, chunk),
        out_shape=[
            shape(latents.shape, BF16),
            shape((rows, width), F32),
            shape((2, width), F32),
            shape(mixed.shape, BF16),
            shape(weight_full.shape, BF16),
            shape(weight_image.shape, BF16),
            shape((2 * lat_all, inner), BF16),
            shape((lines, block_rows, inner), BF16),
            shape(blocks, BF16),
            shape(blocks, BF16),
            shape(blocks, BF16),
            shape(gathered, BF16),
            shape((size,) + gathered, BF16),
            shape((size,) + blocks, BF16),
            shape((size,) + blocks, BF16),
            *Scatter.lands(lines, block_rows, inner)[:2],
        ],
        in_specs=[SMEM] + [VMEM] * 6 + [ANY] * 10 + [VMEM] * 2,
        out_specs=[VMEM] * 3 + [ANY] * 3 + [VMEM] + [ANY] * 10,
        scratch_shapes=[
            pltpu.VMEM(out_weight.shape, BF16),
            pltpu.VMEM((DEPTH, width, chunk), BF16),
            pltpu.VMEM((DEPTH, chunk, width), BF16),
            pltpu.VMEM((2, width, SPAN), BF16),
            pltpu.VMEM(norm_full.shape, BF16),
            pltpu.VMEM(norm_image.shape, BF16),
            pltpu.VMEM(weight_full.shape, BF16),
            pltpu.VMEM(weight_image.shape, BF16),
            pltpu.VMEM(weight_full.shape, BF16),
            pltpu.VMEM(weight_image.shape, BF16),
            pltpu.VMEM(mixed.shape, BF16),
            pltpu.VMEM((size, rows, width), F32),
            pltpu.VMEM((size, 2, rows, 128), F32),
            pltpu.VMEM((size, rows, width), BF16),
            pltpu.VMEM((2, size, rows, width), F32),
            pltpu.VMEM((size, 2, rows, width), F32),
            pltpu.VMEM((2, rows, width), F32),
            pltpu.VMEM((rows, 128), F32),
            pltpu.VMEM((size, rows, inner), BF16),
            pltpu.VMEM((size, rows, width), BF16),
            pltpu.VMEM((size, rows, inner), BF16),
            pltpu.VMEM((size, 2, rows, 128), F32),
            pltpu.VMEM((2, lat_all, inner), BF16),
            pltpu.VMEM((2, lines, 2, 2, size, block_rows, SPAN), BF16),
            pltpu.VMEM((2 * lat_all, inner), F32),
            pltpu.VMEM((size, 2 * lat_all, inner), F32),
            pltpu.VMEM(blocks, BF16),
            pltpu.VMEM((2, lines // 2, 2, 1, block_rows, inner), BF16),
            pltpu.SemaphoreType.DMA((6,)),
            pltpu.SemaphoreType.DMA((2, DEPTH)),
            pltpu.SemaphoreType.DMA((2,)),
            pltpu.SemaphoreType.DMA((2,)),
            pltpu.SemaphoreType.DMA((5,)),
            pltpu.SemaphoreType.DMA((max(2, lines),)),
            pltpu.SemaphoreType.DMA((2,)),
            pltpu.SemaphoreType.DMA((copies,)),
            pltpu.SemaphoreType.DMA((copies,)),
        ],
        compiler_params=params(collective_id=1, has_side_effects=True),
    )(
        counts,
        value_parts,
        peaks,
        latents,
        cotangent_all,
        gain_ffn,
        shift_ffn,
        out_weight,
        in_weight,
        down_weight,
        kv_weight,
        mixed,
        norm_full,
        norm_image,
        weight_full,
        weight_image,
        cotangent_rows,
        queries,
        latent_norm,
    )


def backward_kernel(
    frames,
    lines,
    size,
    counts,
    media,
    latents,
    gain_media,
    gain_latent,
    shift_latent,
    time_embed,
    query_hbm,
    weight_full_hbm,
    weight_image_hbm,
    score_full_hbm,
    score_image_hbm,
    absorbed_hbm,
    into_hbm,
    out_plane,
    query_half,
    key_half,
    value_half,
    key_wait,
    value_wait,
    ffn_rows,
    cotangent_rows,
    cotangent_other,
    query_all,
    state_grad,
    ffn_gains,
    in_hbm,
    down_hbm,
    slot_grad,
    latent_grad,
    out_sum,
    query_sum,
    key_sum,
    value_sum,
    units_out,
    small_out,
    ffn_other,
    units_middle,
    out_line,
    query_first,
    query_second,
    query_line,
    key_first,
    key_second,
    key_line,
    out_blocks,
    query_blocks,
    key_blocks,
    value_blocks,
    temp,
    column_weight,
    weight_full,
    weight_image,
    score_full,
    score_image,
    absorbed,
    into,
    in_share,
    down_share,
    buffer,
    share_sum,
    units,
    block,
    result,
    times,
    small,
    small_land,
    small_sums,
    value_first,
    value_second,
    value_line,
    load_sem,
    column_sem,
    buffer_sem,
    result_sem,
    scatter_sem,
    move_sem,
    send_sem,
    recv_sem,
):
    inner = HEADS * HEAD_DIM
    width = media.shape[-1]
    place = Place(lines, size, send_sem, recv_sem)
    me = place.me
    cores = others(size, me)
    first_full = counts[0] > counts[1]
    local = latents.shape[1]
    lat_all = local * size
    half = lines // 2
    share = down_share.shape[0]
    down_first = pl.multiple_of(place.dp * share, share)
    offset = lax.rem(place.dp * share, 128)
    in_first = pl.multiple_of(place.dp * share - offset, 128)

    loads = [
        pltpu.make_async_copy(source, target, load_sem.at[k])
        for k, (source, target) in enumerate(
            (
                (out_plane, out_blocks),
                (query_half, query_blocks),
                (key_half, key_blocks),
                (value_half, value_blocks),
                (weight_full_hbm, weight_full),
                (weight_image_hbm, weight_image),
                (score_full_hbm, score_full),
                (score_image_hbm, score_image),
                (into_hbm, into),
                (absorbed_hbm, absorbed),
                (in_hbm.at[:, pl.ds(in_first, in_share.shape[1])], in_share),
                (down_hbm.at[pl.ds(down_first, share), :], down_share),
            )
        )
    ]

    def column(group):
        return pltpu.make_async_copy(
            query_hbm.at[:, pl.ds(group * SPAN, SPAN)],
            column_weight.at[group % 2],
            column_sem.at[group % 2],
        )

    own_pieces = [(ffn_rows, cotangent_rows, line) for line in range(lines)]
    pieces = own_pieces + [
        (ffn_other.at[core], cotangent_other.at[core], line) for core in cores for line in range(lines)
    ]
    device_rows = ffn_rows.shape[3]
    piece_rows = 4 * device_rows

    def piece(k):
        ffn_source, cotangent_source, line = pieces[k]
        return [
            pltpu.make_async_copy(
                source.at[line, n // 2, n % 2],
                buffer.at[k % 2, j, pl.ds(n * device_rows, device_rows)],
                buffer_sem.at[k % 2, j, n],
            )
            for j, source in ((0, ffn_source), (1, cotangent_source))
            for n in range(4)
        ]

    for copy in loads[:2] + piece(0) + loads[10:] + loads[2:10]:
        copy.start()
    column(0).start()
    place.greet()

    def scatter(blocks, lands, out):
        return Scatter(place, blocks, lands, temp, scatter_sem, out)

    quer = scatter(query_blocks, (query_first, query_second, query_line), query_sum)
    keys = scatter(key_blocks, (key_first, key_second, key_line), key_sum)
    vals = NearScatter(
        place, value_blocks, (value_first, value_second, value_line), None, None, value_sum
    )

    def add_cores(blocks, wait):
        for origin in cores:
            for k in range(2):
                load = pltpu.make_async_copy(
                    wait.at[origin, pl.ds(k * half, half)], temp.at[k], scatter_sem.at[k]
                )
                load.start()
            for k in range(2):
                pltpu.make_async_copy(
                    wait.at[origin, pl.ds(k * half, half)], temp.at[k], scatter_sem.at[k]
                ).wait()

            @pl.loop(0, half)
            def _(line):
                for k in range(2):
                    for high in range(2):
                        for low in range(2):
                            mine = blocks[k * half + line, high, low].astype(F32)
                            mine += temp[k, line, high, low].astype(F32)
                            blocks[k * half + line, high, low] = mine.astype(BF16)

    outs = LineSum(place, out_blocks, (None, None, out_line), temp, scatter_sem, out_sum)
    for copy in loads[:2]:
        copy.wait()
    outs.line_low()
    quer.first_half()
    ffn_swap = place.swap_cores(lambda p: ffn_rows, lambda c: ffn_other.at[c])
    small[...] = jnp.zeros_like(small)
    times[...] = time_embed[...].astype(F32)

    for copy in loads[10:]:
        copy.wait()
    in_part = in_share[:, :share]
    for first in range(64, in_share.shape[1] - share + 1, 64):
        in_part = jnp.where(offset == first, in_share[:, first : first + share], in_part)
    in_share[:, :share] = in_part
    for k in range(len(pieces)):
        if k + 1 == len(own_pieces):
            finish(ffn_swap)
        if k == 2:
            loads[2].wait()
            add_cores(key_blocks, key_wait)
            keys.first_half()
            outs.line_high()
        if k == 6:
            loads[3].wait()
            add_cores(value_blocks, value_wait)
            quer.second_half()
            vals.first_half()
        if k + 1 < len(pieces):
            for copy in piece(k + 1):
                copy.start()
        for copy in piece(k):
            copy.wait()
        ffn_piece = buffer[k % 2, 0, :piece_rows]
        cotangent_piece = buffer[k % 2, 1, :piece_rows]
        activated, slope = gelu_parts(dot(ffn_piece, in_share[:, :share], 1, 0))
        pre_grad = (dot(cotangent_piece, down_share[...], 1, 1) * slope).astype(BF16)
        up = dot(ffn_piece, pre_grad, 0, 0)
        down = dot(cotangent_piece, activated.astype(BF16), 0, 0)
        if k == 0:
            share_sum[0], share_sum[1] = up, down
        else:
            share_sum[0] += up
            share_sum[1] += down
    unit_rows = width // (lines * 4)
    for k in range(lines * 4):
        at = slice(k * unit_rows, (k + 1) * unit_rows)
        both = jnp.concatenate([share_sum[0, at], share_sum[1, at]], 1)
        units[k // 4, (k // 2) % 2, k % 2] = both.astype(BF16)
    moved = Move(place, units, units_middle, units_out, move_sem)
    moved.along_line()

    def fetch(frame):
        return pltpu.make_async_copy(
            media.at[:, pl.ds(frame * PATCH, PATCH)], buffer.at[frame % 2], buffer_sem.at[frame % 2, 0, 0]
        )

    fetch(0).start()
    outs.end()
    for copy in loads[4:10]:
        copy.wait()

    def back(scores, weights, item, at, count):
        rows = slice(at, at + count)
        return dot(scores[rows], absorbed[item], 1, 0) + dot(weights[rows], into[item], 1, 0)

    row_grad = [
        back(score_full, weight_full, 0, frames * PATCH, local),
        back(score_image, weight_image, 1, PATCH, local),
    ]
    row_grad = jnp.concatenate(row_grad, 0)
    mine = [
        query_all[pl.ds(pl.multiple_of(item * lat_all + me * local, local), local)]
        for item in range(2)
    ]
    mine = jnp.concatenate(mine, 0)
    for group in range(GROUPS):
        if group + 1 < GROUPS:
            column(group + 1).start()
        column(group).wait()
        span = slice(group * SPAN, (group + 1) * SPAN)
        row_grad += dot(mine[:, span], column_weight[group % 2], 1, 1)
    own = jnp.concatenate(
        in_order(first_full, (latents[0].astype(F32), latents[1].astype(F32))), 0
    )
    unit, inverse = normalize(own)
    small[2:3] = jnp.sum(row_grad * unit, 0, keepdims=True)
    small[3:4] = jnp.sum(row_grad, 0, keepdims=True)
    small[4:6] = ffn_gains[...]
    row_grad = state_grad[...] + norm_back(unit, inverse, vector(gain_latent), row_grad)
    for k, value in enumerate(in_order(first_full, (row_grad[:local], row_grad[local:]))):
        latent_grad[k] = value

    keys.second_half()
    quer.plane_sum()
    quer.line_low()

    gain = vector(gain_media)
    total = Total(place, small, small_land, small_sums)

    def norm_frame(frame, slot, pick_first, target):
        at_time = 6 + me * frames + frame
        time_row = times[pl.ds(me * frames + frame, 1)]

        @pl.loop(0, PATCH // ROWS)
        def _(part):
            at = pl.ds(pl.multiple_of(part * ROWS, ROWS), ROWS)
            values = jnp.where(
                pick_first, buffer[slot, 0, at].astype(F32), buffer[slot, 1, at].astype(F32)
            )
            unit, inverse = normalize(values + time_row)
            grad = block[at]
            rows_grad = norm_back(unit, inverse, gain, grad)
            target[at] = rows_grad.astype(BF16)
            small[0:1] += jnp.sum(grad * unit, 0, keepdims=True)
            small[1:2] += jnp.sum(grad, 0, keepdims=True)
            small[pl.ds(at_time, 1)] += jnp.sum(rows_grad, 0, keepdims=True)

    puts = []
    for k in range(frames + 1):
        frame = max(0, k - 1)
        if k != 1:
            fetch(frame).wait()
        if k >= 1 and frame + 1 < frames:
            fetch(frame + 1).start()
        if k == 0:
            block[...] = back(score_image, weight_image, 1, 0, PATCH)
        else:
            block[...] = back(score_full, weight_full, 0, frame * PATCH, PATCH)
        if k >= 2:
            puts[k - 2].wait()
        picked = jnp.logical_not(first_full) if k == 0 else first_full
        norm_frame(frame, frame % 2, picked, result.at[k % 2])
        puts.append(
            pltpu.make_async_copy(
                result.at[k % 2], slot_grad.at[pl.ds(k * PATCH, PATCH)], result_sem.at[k % 2]
            )
        )
        puts[k].start()
        if k == 2:
            vals.second_half()
    total.in_chip()
    keys.plane_sum()
    keys.line_low()
    total.low()
    quer.line_high()
    vals.plane_sum()
    vals.send_line()
    total.high()
    moved.in_plane()
    total.along_line()
    keys.line_high()
    total.end(small_out)
    quer.end()
    keys.end()
    vals.end_line()
    moved.end()
    for put in puts[max(0, frames - 1) :]:
        put.wait()


def attend_backward(
    chips,
    size,
    counts,
    media,
    latents,
    gain_media,
    gain_latent,
    shift_latent,
    time_embed,
    query_weight,
    weight_full,
    weight_image,
    score_full,
    score_image,
    absorbed,
    into,
    out_plane,
    query_half,
    key_half,
    value_half,
    key_wait,
    value_wait,
    ffn_rows,
    cotangent_rows,
    cotangent_other,
    query_all,
    state_grad,
    ffn_gains,
    in_weight,
    down_weight,
):
    width = media.shape[-1]
    inner = HEADS * HEAD_DIM
    lines = chips // 4
    frames = media.shape[1] // PATCH
    block_rows = width // (chips * size)
    blocks = (lines, 2, 2, block_rows, inner)
    share = in_weight.shape[1] // chips
    unit = (lines, 2, 2, width // chips, 2 * share)
    small = (6 + time_embed.shape[0] + 7) // 8 * 8
    shape = jax.ShapeDtypeStruct
    copies = 8 * lines + 10 * size + 24
    lands = Scatter.lands(lines, block_rows, inner)
    return pl.pallas_call(
        functools.partial(backward_kernel, frames, lines, size),
        out_shape=[
            shape(((frames + 1) * PATCH, width), BF16),
            shape(latents.shape, F32),
            *[shape((block_rows, inner), F32)] * 4,
            shape(unit, BF16),
            shape((small, width), F32),
            shape((size,) + ffn_rows.shape, BF16),
            shape(unit, BF16),
            lands[2],
            *lands * 2,
        ],
        in_specs=[SMEM, ANY] + [VMEM] * 5 + [ANY] * 16 + [VMEM] * 3 + [ANY] * 2,
        out_specs=[ANY] + [VMEM] * 5 + [ANY, VMEM] + [ANY] * 9,
        scratch_shapes=[
            pltpu.VMEM((lines, block_rows, inner), BF16),
            *[pltpu.VMEM(blocks, BF16)] * 3,
            pltpu.VMEM((2, lines // 2, 2, 2, block_rows, inner), BF16),
            pltpu.VMEM((2, width, SPAN), BF16),
            pltpu.VMEM(weight_full.shape, BF16),
            pltpu.VMEM(weight_image.shape, BF16),
            pltpu.VMEM(weight_full.shape, BF16),
            pltpu.VMEM(weight_image.shape, BF16),
            pltpu.VMEM(absorbed.shape, BF16),
            pltpu.VMEM(into.shape, BF16),
            pltpu.VMEM((width, (share + 64 + 127) // 128 * 128), BF16),
            pltpu.VMEM((share, width), BF16),
            pltpu.VMEM((2, 2, PATCH, width), BF16),
            pltpu.VMEM((2, width, share), F32),
            pltpu.VMEM(unit, BF16),
            pltpu.VMEM((PATCH, width), F32),
            pltpu.VMEM((2, PATCH, width), BF16),
            pltpu.VMEM(time_embed.shape, F32),
            pltpu.VMEM((small, width), F32),
            *Total.scratch(lines, size, (small, width)),
            *[pltpu.VMEM(land.shape, BF16) for land in lands],
            pltpu.SemaphoreType.DMA((12,)),
            pltpu.SemaphoreType.DMA((2,)),
            pltpu.SemaphoreType.DMA((2, 2, 4)),
            pltpu.SemaphoreType.DMA((2,)),
            pltpu.SemaphoreType.DMA((max(4, lines),)),
            pltpu.SemaphoreType.DMA((2,)),
            pltpu.SemaphoreType.DMA((copies,)),
            pltpu.SemaphoreType.DMA((copies,)),
        ],
        compiler_params=params(collective_id=2, has_side_effects=True),
    )(
        counts,
        media,
        latents,
        gain_media,
        gain_latent,
        shift_latent,
        time_embed,
        query_weight,
        weight_full,
        weight_image,
        score_full,
        score_image,
        absorbed,
        into,
        out_plane,
        query_half,
        key_half,
        value_half,
        key_wait,
        value_wait,
        ffn_rows,
        cotangent_rows,
        cotangent_other,
        query_all,
        state_grad,
        ffn_gains,
        in_weight,
        down_weight,
    )


def result_kernel(
    chips,
    flags,
    slots,
    units,
    latent_in,
    latent_grad_in,
    key_in,
    value_in,
    query_in,
    out_in,
    media_grad,
    up,
    down,
    latent_out,
    latent_grad,
    key_value,
    query,
    out,
):
    item, frame = pl.program_id(0), pl.program_id(1)
    alive = (item == flags[0]) | (frame == 0)
    media_grad[0] = jnp.where(alive, slots[...].astype(F32), 0.0)

    @pl.when((item == 0) & (frame == 0))
    def _():
        share = units.shape[-1] // 2
        for pair in range(chips // 2):
            at = slice(pair * 2 * share, (pair + 1) * 2 * share)
            left, right = units[2 * pair].astype(F32), units[2 * pair + 1].astype(F32)
            up[:, at] = jnp.concatenate([left[:, :share], right[:, :share]], 1)
            down[:, at] = jnp.concatenate([left[:, share:], right[:, share:]], 1)
        latent_out[...] = latent_in[...]
        latent_grad[...] = latent_grad_in[...]
        inner = key_in.shape[-1]
        key_value[:, :inner] = key_in[...]
        key_value[:, inner:] = value_in[...]
        query[...] = query_in[...]
        out[...] = out_in[...]


def final_form(counts, slots, units, latent_out, latent_grad, sums, frames):
    chips, rows, columns = units.shape
    width = slots.shape[-1]
    block_rows = sums[0].shape[0]
    full = jnp.where(counts[0] > counts[1], 0, 1).astype(jnp.int32).reshape(1)
    shape = jax.ShapeDtypeStruct

    def whole(array_shape):
        return pl.BlockSpec(array_shape, lambda i, f, flags: (0,) * len(array_shape))

    outs = [
        ((rows, chips * columns // 2), F32),
        ((rows, chips * columns // 2), F32),
        (latent_out.shape, BF16),
        (latent_grad.shape, F32),
        ((block_rows, 2 * width), F32),
        ((block_rows, width), F32),
        ((block_rows, width), F32),
    ]
    return pl.pallas_call(
        functools.partial(result_kernel, chips),
        out_shape=[shape((2, frames * PATCH, width), F32)] + [shape(*out) for out in outs],
        grid_spec=pltpu.PrefetchScalarGridSpec(
            num_scalar_prefetch=1,
            grid=(2, frames),
            in_specs=[
                pl.BlockSpec(
                    (PATCH, width), lambda i, f, flags: (jnp.where(i == flags[0], f + 1, 0), 0)
                ),
                whole(units.shape),
                whole(latent_out.shape),
                whole(latent_grad.shape),
                *[whole(part.shape) for part in sums],
            ],
            out_specs=[pl.BlockSpec((1, PATCH, width), lambda i, f, flags: (i, f, 0))]
            + [whole(out[0]) for out in outs],
        ),
        compiler_params=params(),
    )(full, slots, units, latent_out, latent_grad, *sums)


def per_device(
    chips,
    size,
    media,
    frame_counts,
    latents,
    norm_media_gain,
    norm_media_shift,
    norm_latent_gain,
    norm_latent_shift,
    time_embed,
    query_weight,
    key_value_weight,
    out_weight,
    ffn_norm_gain,
    ffn_norm_shift,
    ffn_in_weight,
    ffn_out_weight,
    out_cotangent,
):
    dp, me = lax.axis_index("dp"), lax.axis_index("mp")
    width = media.shape[-1]
    share = ffn_in_weight.shape[1] // chips
    (
        norm_full,
        norm_image,
        weight_full,
        weight_image,
        absorbed,
        mixed,
        value_parts,
        peaks,
        latent_norm,
        queries,
        cotangent_all,
        cotangent_rows,
    ) = attend_forward(
        chips,
        size,
        frame_counts,
        media,
        latents,
        out_cotangent,
        norm_media_gain,
        norm_media_shift,
        norm_latent_gain,
        norm_latent_shift,
        time_embed,
        query_weight,
        key_value_weight,
    )
    (
        latent_out,
        state_grad,
        ffn_gains,
        into,
        score_full,
        score_image,
        query_all,
        out_plane,
        query_half,
        key_half,
        value_half,
        ffn_rows,
        cotangent_other,
        key_wait,
        value_wait,
        *_,
    ) = latent_pass(
        chips,
        size,
        frame_counts,
        value_parts,
        peaks,
        latents,
        cotangent_all,
        ffn_norm_gain,
        ffn_norm_shift,
        out_weight,
        ffn_in_weight,
        ffn_out_weight,
        key_value_weight,
        mixed,
        norm_full,
        norm_image,
        weight_full,
        weight_image,
        cotangent_rows,
        queries,
        latent_norm,
    )
    slot_grad, latent_grad, out_sum, query_sum, key_sum, value_sum, units, small, *_ = (
        attend_backward(
            chips,
            size,
            frame_counts,
            media,
            latents,
            norm_media_gain,
            norm_latent_gain,
            norm_latent_shift,
            time_embed,
            query_weight,
            weight_full,
            weight_image,
            score_full,
            score_image,
            absorbed,
            into,
            out_plane,
            query_half,
            key_half,
            value_half,
            key_wait,
            value_wait,
            ffn_rows,
            cotangent_rows,
            cotangent_other,
            query_all,
            state_grad,
            ffn_gains,
            ffn_in_weight,
            ffn_out_weight,
        )
    )
    units = units.reshape(chips, width // chips, 2 * share)
    sums = (key_sum, value_sum, query_sum, out_sum)
    media_grad, up_sum, down_sum, latent_out, latent_grad, key_value_sum, query_sum, out_sum = (
        final_form(
            frame_counts, slot_grad, units, latent_out, latent_grad, sums, media.shape[1] // PATCH
        )
    )
    place = (dp * size + me) * (width // (chips * size))
    small = lax.dynamic_slice_in_dim(small, place, width // (chips * size), 1)
    return (
        latent_out,
        latent_grad,
        media_grad,
        small[0],
        small[1],
        small[2],
        small[3],
        small[6 : 6 + time_embed.shape[0]],
        query_sum,
        key_value_sum,
        out_sum.T,
        small[4],
        small[5],
        up_sum,
        down_sum.T,
    )


def layer_norm(values_in, gain, shift):
    row_mean = jnp.mean(values_in, -1, keepdims=True)
    centered = values_in - row_mean
    variance = jnp.mean(centered * centered, -1, keepdims=True)
    return centered * lax.rsqrt(variance + EPSILON) * gain + shift


def plain_norm_back(values_in, gain, shift, gradient):
    result, pullback = jax.vjp(layer_norm, values_in, gain, shift)
    return pullback(gradient)


def gelu_exact(values_in):
    return jax.nn.gelu(values_in, approximate=False)


def rescale_heads(values_in, factor):
    shaped = values_in.reshape(values_in.shape[:-1] + (factor.shape[-1], -1))
    return (shaped * factor[..., None]).reshape(values_in.shape)


def plain_device(
    media,
    frame_counts,
    latents,
    norm_media_gain,
    norm_media_shift,
    norm_latent_gain,
    norm_latent_shift,
    time_embed,
    query_weight,
    key_value_weight,
    out_weight,
    ffn_norm_gain,
    ffn_norm_shift,
    ffn_in_weight,
    ffn_out_weight,
    out_cotangent,
):
    item_count, local_keys, model_width = media.shape
    latent_local = latents.shape[1]
    inner = HEADS * HEAD_DIM
    frames_local = local_keys // PATCH
    key_count = local_keys + latent_local
    mp_index = lax.axis_index("mp")
    latent_start = mp_index * latent_local
    score_scale = HEAD_DIM ** (-0.5)
    gain_m = norm_media_gain.astype(jnp.float32)
    shift_m = norm_media_shift.astype(jnp.float32)
    gain_l = norm_latent_gain.astype(jnp.float32)
    shift_l = norm_latent_shift.astype(jnp.float32)
    gain_f = ffn_norm_gain.astype(jnp.float32)
    shift_f = ffn_norm_shift.astype(jnp.float32)
    frame_ids = mp_index * frames_local + jnp.arange(frames_local)
    frame_live = frame_ids[None, :] < frame_counts[:, None]
    key_alive = jnp.concatenate(
        [jnp.repeat(frame_live, PATCH, axis=1), jnp.ones((item_count, latent_local), bool)], axis=1
    )
    alive_mask = key_alive[:, None, None, :]
    time_rows = lax.dynamic_slice_in_dim(
        time_embed, mp_index * frames_local, frames_local, 0
    ).astype(jnp.float32)
    with_time = (
        media.astype(jnp.float32).reshape(item_count, frames_local, PATCH, model_width)
        + time_rows[None, :, None, :]
    )
    with_time = with_time.reshape(item_count * local_keys, model_width)
    media_norm = layer_norm(with_time, gain_m, shift_m).astype(jnp.bfloat16)
    latent_in = latents.astype(jnp.float32)
    latent_norm = layer_norm(latent_in, gain_l, shift_l).astype(jnp.bfloat16)
    media_kv = jnp.dot(media_norm, key_value_weight, preferred_element_type=jnp.float32).astype(
        jnp.bfloat16
    )
    latent_kv = jnp.einsum(
        "ild,de->ile", latent_norm, key_value_weight, preferred_element_type=jnp.float32
    ).astype(jnp.bfloat16)
    keys_values = jnp.concatenate(
        [media_kv.reshape(item_count, local_keys, 2 * inner), latent_kv], axis=1
    )
    key_heads = keys_values[..., :inner].reshape(item_count, key_count, HEADS, HEAD_DIM)
    value_heads = keys_values[..., inner:].reshape(item_count, key_count, HEADS, HEAD_DIM)
    query_own = jnp.einsum(
        "ild,de->ile", latent_norm, query_weight, preferred_element_type=jnp.float32
    ).astype(jnp.bfloat16)
    queries = lax.all_gather(query_own, "mp", axis=1, tiled=True)
    lat_all = queries.shape[1]
    query_heads = queries.reshape(item_count, lat_all, HEADS, HEAD_DIM)
    scores = (
        jnp.einsum("iqhd,ikhd->ihqk", query_heads, key_heads, preferred_element_type=jnp.float32)
        * score_scale
    )
    masked = jnp.where(alive_mask, scores, -1e30)
    peak_score = jnp.max(masked, -1)
    weights = jnp.where(alive_mask, jnp.exp(masked - peak_score[..., None]), 0.0)
    weight_sum = jnp.sum(weights, -1).transpose(0, 2, 1)
    peak_score = peak_score.transpose(0, 2, 1)
    numerator = jnp.einsum(
        "ihqk,ikhd->iqhd",
        weights.astype(jnp.bfloat16),
        value_heads,
        preferred_element_type=jnp.float32,
    ).reshape(item_count, lat_all, inner)
    peak_all = lax.pmax(peak_score, "mp")
    factor = jnp.exp(peak_score - peak_all)
    weight_own, numerator_own = (
        lax.psum_scatter(weight_sum * factor, "mp", scatter_dimension=1, tiled=True),
        lax.psum_scatter(rescale_heads(numerator, factor), "mp", scatter_dimension=1, tiled=True),
    )
    peak_own = lax.dynamic_slice_in_dim(peak_all, latent_start, latent_local, 1)
    log_sum_own = peak_own + jnp.log(weight_own)
    attended_exact = rescale_heads(numerator_own, 1.0 / weight_own)
    attended_low = attended_exact.astype(jnp.bfloat16)
    update = jnp.einsum("ile,ed->ild", attended_low, out_weight, preferred_element_type=jnp.float32)
    hidden_state = latent_in + update
    ffn_norm = layer_norm(hidden_state, gain_f, shift_f).astype(jnp.bfloat16)
    ffn_norm_rows = ffn_norm.transpose(1, 0, 2)
    gathered = lax.all_gather(ffn_norm_rows, "mp", axis=0, tiled=True)
    pre_act = jnp.einsum("lid,df->lif", gathered, ffn_in_weight, preferred_element_type=jnp.float32)
    activated = gelu_exact(pre_act).astype(jnp.bfloat16)
    ffn_norm_all = gathered
    block = activated
    ffn_result = lax.psum_scatter(
        jnp.einsum("lif,fd->lid", block, ffn_out_weight, preferred_element_type=jnp.float32),
        "mp",
        scatter_dimension=0,
        tiled=True,
    )
    latent_out = (hidden_state + ffn_result.transpose(1, 0, 2)).astype(jnp.bfloat16)
    cotangent_rows = out_cotangent.transpose(1, 0, 2)
    gathered = lax.all_gather(cotangent_rows, "mp", axis=0, tiled=True)
    act_grad = jnp.einsum(
        "lid,fd->lif", gathered, ffn_out_weight, preferred_element_type=jnp.float32
    )
    result, pullback = jax.vjp(gelu_exact, pre_act)
    pre_grad = pullback(act_grad)[0].astype(jnp.bfloat16)
    ffn_down_grad = jnp.einsum(
        "lif,lid->fd", activated, gathered, preferred_element_type=jnp.float32
    )
    ffn_up_grad = jnp.einsum(
        "lid,lif->df", ffn_norm_all, pre_grad, preferred_element_type=jnp.float32
    )
    block = pre_grad
    ffn_norm_grad = lax.psum_scatter(
        jnp.einsum("lif,df->lid", block, ffn_in_weight, preferred_element_type=jnp.float32),
        "mp",
        scatter_dimension=0,
        tiled=True,
    ).transpose(1, 0, 2)
    state_part, gain_f_grad, shift_f_grad = plain_norm_back(hidden_state, gain_f, shift_f, ffn_norm_grad)
    state_grad = out_cotangent.astype(jnp.float32) + state_part
    update_grad = state_grad.astype(jnp.bfloat16)
    out_grad_local = jnp.einsum(
        "ile,ild->ed", attended_low, update_grad, preferred_element_type=jnp.float32
    )
    attended_grad = jnp.einsum(
        "ild,ed->ile", update_grad, out_weight, preferred_element_type=jnp.float32
    ).astype(jnp.bfloat16)
    row_delta = jnp.sum(
        (attended_grad.astype(jnp.float32) * attended_exact).reshape(
            item_count, latent_local, HEADS, HEAD_DIM
        ),
        -1,
    )
    grad_all, delta_all, log_sum_all = (
        lax.all_gather(attended_grad.astype(jnp.float32), "mp", axis=1, tiled=True),
        lax.all_gather(row_delta, "mp", axis=1, tiled=True),
        lax.all_gather(log_sum_own, "mp", axis=1, tiled=True),
    )
    grad_heads = grad_all.astype(jnp.bfloat16).reshape(item_count, lat_all, HEADS, HEAD_DIM)
    scores_again = (
        jnp.einsum("iqhd,ikhd->ihqk", query_heads, key_heads, preferred_element_type=jnp.float32)
        * score_scale
    )
    probability = jnp.where(
        alive_mask, jnp.exp(scores_again - log_sum_all.transpose(0, 2, 1)[..., None]), 0.0
    )
    prob_grad = jnp.einsum(
        "iqhd,ikhd->ihqk", grad_heads, value_heads, preferred_element_type=jnp.float32
    )
    score_grad = (probability * (prob_grad - delta_all.transpose(0, 2, 1)[..., None])).astype(
        jnp.bfloat16
    )
    query_part_grad = (
        jnp.einsum("ihqk,ikhd->iqhd", score_grad, key_heads, preferred_element_type=jnp.float32)
        * score_scale
    ).reshape(item_count, lat_all, inner)
    key_grad = (
        jnp.einsum("ihqk,iqhd->ikhd", score_grad, query_heads, preferred_element_type=jnp.float32)
        * score_scale
    )
    value_grad = jnp.einsum(
        "ihqk,iqhd->ikhd",
        probability.astype(jnp.bfloat16),
        grad_heads,
        preferred_element_type=jnp.float32,
    )
    kv_grad = jnp.concatenate(
        [
            key_grad.reshape(item_count, key_count, inner),
            value_grad.reshape(item_count, key_count, inner),
        ],
        -1,
    ).astype(jnp.bfloat16)
    query_grad = lax.psum_scatter(query_part_grad, "mp", scatter_dimension=1, tiled=True).astype(
        jnp.bfloat16
    )
    media_kv_grad = kv_grad[:, :local_keys].reshape(item_count * local_keys, 2 * inner)
    latent_kv_grad = kv_grad[:, local_keys:]
    kv_weight_local = jnp.einsum(
        "rd,re->de", media_norm, media_kv_grad, preferred_element_type=jnp.float32
    ) + jnp.einsum("ild,ile->de", latent_norm, latent_kv_grad, preferred_element_type=jnp.float32)
    query_weight_local = jnp.einsum(
        "ild,ile->de", latent_norm, query_grad, preferred_element_type=jnp.float32
    )
    media_norm_grad = jnp.einsum(
        "re,de->rd", media_kv_grad, key_value_weight, preferred_element_type=jnp.float32
    )
    latent_norm_grad = jnp.einsum(
        "ile,de->ild", latent_kv_grad, key_value_weight, preferred_element_type=jnp.float32
    ) + jnp.einsum("ile,de->ild", query_grad, query_weight, preferred_element_type=jnp.float32)
    media_pre_grad, gain_m_grad, shift_m_grad = plain_norm_back(
        with_time, gain_m, shift_m, media_norm_grad
    )
    latent_part, gain_l_grad, shift_l_grad = plain_norm_back(latent_in, gain_l, shift_l, latent_norm_grad)
    latent_grad = state_grad + latent_part
    media_grad = media_pre_grad.reshape(item_count, local_keys, model_width)
    time_local = jnp.sum(
        media_pre_grad.reshape(item_count, frames_local, PATCH, model_width), (0, 2)
    )
    time_grad = lax.dynamic_update_slice_in_dim(
        jnp.zeros((time_embed.shape[0], model_width), jnp.float32),
        time_local,
        mp_index * frames_local,
        0,
    )
    small_grads = jnp.concatenate(
        [
            jnp.stack(
                [gain_m_grad, shift_m_grad, gain_l_grad, shift_l_grad, gain_f_grad, shift_f_grad], 1
            ),
            time_grad.T,
        ],
        1,
    )
    query_sum, kv_sum, out_sum, small_sum = (
        lax.psum_scatter(query_weight_local, ("dp", "mp"), scatter_dimension=0, tiled=True),
        lax.psum_scatter(kv_weight_local, ("dp", "mp"), scatter_dimension=0, tiled=True),
        lax.psum_scatter(out_grad_local.T, ("dp", "mp"), scatter_dimension=0, tiled=True),
        lax.psum_scatter(small_grads, ("dp", "mp"), scatter_dimension=0, tiled=True),
    )
    ffn_up_sum, ffn_down_sum = (
        lax.psum_scatter(ffn_up_grad, "dp", scatter_dimension=0, tiled=True),
        lax.psum_scatter(ffn_down_grad.T, "dp", scatter_dimension=0, tiled=True),
    )
    return (
        latent_out,
        latent_grad,
        media_grad,
        small_sum[:, 0],
        small_sum[:, 1],
        small_sum[:, 2],
        small_sum[:, 3],
        small_sum[:, 6:].T,
        query_sum,
        kv_sum,
        out_sum.T,
        small_sum[:, 4],
        small_sum[:, 5],
        ffn_up_sum,
        ffn_down_sum.T,
    )


def solution(mesh):
    placed = (
        P("dp", "mp", None),
        P("dp"),
        P("dp", "mp", None),
        P(),
        P(),
        P(),
        P(),
        P(),
        P(),
        P(),
        P(),
        P(),
        P(),
        P(None, "mp"),
        P("mp", None),
        P("dp", "mp", None),
    )
    chips, size = mesh.shape["dp"], mesh.shape["mp"]

    def device(*arrays):
        tiled = arrays[0].shape[-1] % (chips * size * 16) == 0 and arrays[2].shape[1] % 16 == 0
        if tiled and chips == 16:
            return per_device(chips, size, *arrays)
        return plain_device(*arrays)

    return jax.shard_map(
        device,
        mesh=mesh,
        in_specs=placed,
        out_specs=(
            P("dp", "mp", None),
            P("dp", "mp", None),
            P("dp", "mp", None),
            P(("dp", "mp")),
            P(("dp", "mp")),
            P(("dp", "mp")),
            P(("dp", "mp")),
            P(None, ("dp", "mp")),
            P(("dp", "mp"), None),
            P(("dp", "mp"), None),
            P(None, ("dp", "mp")),
            P(("dp", "mp")),
            P(("dp", "mp")),
            P("dp", "mp"),
            P("mp", "dp"),
        ),
        check_vma=False,
    )
```

```python
import functools

import jax
import jax.numpy as jnp
from jax import lax
from jax.experimental import pallas as pl
from jax.experimental.pallas import tpu as pltpu
from jax.sharding import PartitionSpec as P

HEADS = 16
HEAD_DIM = 96
PATCH = 256
GROUP = 4
SPAN = GROUP * HEAD_DIM
GROUPS = HEADS // GROUP
LATENT_PAD = 32
EPSILON = 1e-05
SCALE = HEAD_DIM ** (-0.5)
F32 = jnp.float32
BF16 = jnp.bfloat16
MESH = pl.DeviceIdType.MESH
VMEM_LIMIT = 60 * 1024 * 1024

VMEM = pl.BlockSpec(memory_space=pltpu.VMEM)
SMEM = pl.BlockSpec(memory_space=pltpu.SMEM)
ANY = pl.BlockSpec(memory_space=pl.ANY)


def dot(left, right, left_axis, right_axis):
    return lax.dot_general(
        left,
        right,
        (((left_axis,), (right_axis,)), ((), ())),
        preferred_element_type=F32,
    )


def normalize(rows):
    mean = jnp.mean(rows, -1, keepdims=True)
    centered = rows - mean
    variance = jnp.mean(centered * centered, -1, keepdims=True)
    inverse = lax.rsqrt(variance + EPSILON)
    return centered * inverse, inverse


def norm_back(unit, inverse, gain, gradient):
    scaled = gradient * gain
    return inverse * (
        scaled
        - jnp.mean(scaled, -1, keepdims=True)
        - unit * jnp.mean(scaled * unit, -1, keepdims=True)
    )


def lane_head(rows):
    column = lax.broadcasted_iota(jnp.int32, (rows, SPAN), 1)
    head = jnp.zeros((rows, SPAN), jnp.int32)
    for h in range(1, GROUP):
        head += (column >= h * HEAD_DIM).astype(jnp.int32)
    return head


def spread_heads(rows):
    head = lane_head(rows.shape[0])
    zero = jnp.zeros_like(rows)
    return jnp.concatenate([jnp.where(head == h, rows, zero) for h in range(GROUP)], 0)


def fold_heads(rows):
    count = rows.shape[0] // GROUP
    head = lane_head(count)
    total = jnp.zeros((count, SPAN), F32)
    for h in range(GROUP):
        total += jnp.where(head == h, rows[h * count : (h + 1) * count], 0.0)
    return total


def dot_exact(left, selector):
    total = None
    for _ in range(3):
        term = left.astype(BF16)
        left = left - term.astype(F32)
        part = dot(term, selector, 1, 0)
        total = part if total is None else total + part
    return total


def head_selector():
    low = lax.broadcasted_iota(jnp.int32, (128, HEADS * HEAD_DIM), 0) * HEAD_DIM
    column = lax.broadcasted_iota(jnp.int32, (128, HEADS * HEAD_DIM), 1)
    return ((column >= low) & (column < low + HEAD_DIM)).astype(F32).astype(BF16)


def head_sums(rows):
    count = rows.shape[0]
    head = lane_head(count)
    lane = lax.broadcasted_iota(jnp.int32, (count, 128), 1)
    result = jnp.zeros((count, 128), F32)
    for group in range(GROUPS):
        span = rows[:, group * SPAN : (group + 1) * SPAN]
        for h in range(GROUP):
            total = jnp.sum(jnp.where(head == h, span, 0.0), 1, keepdims=True)
            result += jnp.where(lane == group * GROUP + h, total, 0.0)
    return result


def own_columns(rows, head):
    lane = lax.broadcasted_iota(jnp.int32, rows.shape, 1)
    return jnp.sum(jnp.where(lane == head, rows, 0.0), 1, keepdims=True)


def across_lanes(column):
    return jnp.transpose(jnp.broadcast_to(column, (column.shape[0], 128)))[0:1]


def down_rows(row):
    return jnp.transpose(jnp.broadcast_to(row, (128, row.shape[1])))


def vector(ref):
    return ref[...].astype(F32).reshape(1, ref.shape[-1])


def gelu_parts(pre):
    cdf = 0.5 * (1.0 + lax.erf(pre * (0.5**0.5)))
    return pre * cdf, cdf + pre * (jnp.exp(-0.5 * pre * pre) * 0.3989422804014327)


def params(**more):
    return pltpu.CompilerParams(vmem_limit_bytes=VMEM_LIMIT, **more)


def greet(devices):
    barrier = pltpu.get_barrier_semaphore()
    for device in devices:
        pl.semaphore_signal(barrier, inc=1, device_id=device, device_id_type=MESH)
    pl.semaphore_wait(barrier, len(devices))


def others(axis_size, me):
    return [lax.rem(me + k, axis_size) for k in range(1, axis_size)]


class Place:
    def __init__(self, lines, size, send_sem, recv_sem):
        self.lines, self.size = lines, size
        self.dp, self.me = lax.axis_index("dp"), lax.axis_index("mp")
        self.line = self.dp // 4
        self.high = lax.rem(self.dp // 2, 2)
        self.low = lax.rem(self.dp, 2)
        self.send_sem, self.recv_sem = send_sem, recv_sem
        self.used = 0

    def at(self, line, high, low):
        return (line * 4 + high * 2 + low, self.me)

    def low_peer(self):
        return self.at(self.line, self.high, 1 - self.low)

    def high_peer(self):
        return self.at(self.line, 1 - self.high, self.low)

    def across(self):
        return self.at(self.line, 1 - self.high, 1 - self.low)

    def greet(self):
        greet(
            [self.low_peer(), self.high_peer(), self.across()]
            + [self.at(peer, self.high, self.low) for peer in others(self.lines, self.line)]
            + [(self.dp, peer) for peer in others(self.size, self.me)]
        )

    def exchange(self, source, target, land, device):
        index = self.used
        self.used += 1

        def copy(destination):
            return pltpu.make_async_remote_copy(
                src_ref=source,
                dst_ref=destination,
                send_sem=self.send_sem.at[index],
                recv_sem=self.recv_sem.at[index],
                device_id=device,
                device_id_type=MESH,
            )

        pair = (copy(target), copy(land))
        pair[0].start()
        return pair

    def swap(self, me, count, device_of, source_of, land_of):
        pairs = []
        for k in range(1, count):
            peer, origin = lax.rem(me + k, count), lax.rem(me + count - k, count)
            pairs.append(
                self.exchange(source_of(peer), land_of(me), land_of(origin), device_of(peer))
            )
        return pairs

    def swap_cores(self, source_of, land_of):
        return self.swap(self.me, self.size, lambda p: (self.dp, p), source_of, land_of)

    def swap_lines(self, source_of, land_of):
        return self.swap(
            self.line, self.lines, lambda p: self.at(p, self.high, self.low), source_of, land_of
        )


def finish_sends(pairs):
    for copy, _ in pairs:
        copy.wait_send()


def finish_arrivals(pairs):
    for _, arrival in pairs:
        arrival.wait_recv()


def finish(pairs):
    finish_arrivals(pairs)
    finish_sends(pairs)


class Gather:
    def __init__(self, place, rows, out, sem):
        self.place, self.rows, self.out, self.sem = place, rows, out, sem

    def along_line(self):
        p, out = self.place, self.out
        self.keep = pltpu.make_async_copy(
            self.rows, out.at[p.line, p.high, p.low], self.sem
        )
        self.keep.start()
        self.pairs = p.swap_lines(
            lambda peer: self.rows, lambda line: out.at[line, p.high, p.low]
        )

    def first_half(self):
        p, out = self.place, self.out
        self.keep.wait()
        finish(self.pairs)
        half = p.lines // 2
        near, far = pl.ds(0, half), pl.ds(half, p.lines - half)
        self.pairs = [
            p.exchange(
                out.at[near, p.high, p.low],
                out.at[near, p.high, p.low],
                out.at[near, p.high, 1 - p.low],
                p.low_peer(),
            ),
            p.exchange(
                out.at[far, p.high, p.low],
                out.at[far, p.high, p.low],
                out.at[far, 1 - p.high, p.low],
                p.high_peer(),
            ),
        ]

    def second_half(self):
        p, out = self.place, self.out
        finish(self.pairs)
        half = p.lines // 2
        near, far = pl.ds(0, half), pl.ds(half, p.lines - half)
        self.pairs = [
            p.exchange(
                out.at[near, p.high],
                out.at[near, p.high],
                out.at[near, 1 - p.high],
                p.high_peer(),
            ),
            p.exchange(
                out.at[far, :, p.low],
                out.at[far, :, p.low],
                out.at[far, :, 1 - p.low],
                p.low_peer(),
            ),
        ]

    def end(self):
        finish(self.pairs)


class Scatter:
    def __init__(self, place, blocks, lands, temp, sem, out):
        self.place, self.blocks, self.lands, self.out = place, blocks, lands, out
        self.temp, self.sem = temp, sem

    @staticmethod
    def lands(lines, rows, columns):
        half = lines // 2
        return [
            jax.ShapeDtypeStruct((2, half, 2, rows, columns), BF16),
            jax.ShapeDtypeStruct((2, half, rows, columns), BF16),
            jax.ShapeDtypeStruct((lines, rows, columns), BF16),
        ]

    def load(self, pairs):
        copies = [
            pltpu.make_async_copy(source, target, self.sem.at[k])
            for k, (source, target) in enumerate(pairs)
        ]
        for copy in copies:
            copy.start()
        for copy in copies:
            copy.wait()

    def first_half(self):
        p, blocks, land = self.place, self.blocks, self.lands[0]
        half = p.lines // 2
        near, far = pl.ds(0, half), pl.ds(half, half)
        self.pairs = [
            p.exchange(blocks.at[near, :, 1 - p.low], land.at[0], land.at[0], p.low_peer()),
            p.exchange(blocks.at[far, 1 - p.high], land.at[1], land.at[1], p.high_peer()),
        ]

    def second_half(self):
        p, blocks, land, into, temp = self.place, self.blocks, *self.lands[:2], self.temp
        half = p.lines // 2
        near, far = pl.ds(0, half), pl.ds(half, half)
        finish(self.pairs)
        self.load([(land.at[k], temp.at[k, :, :, 0]) for k in range(2)])

        @pl.loop(0, half)
        def _(line):
            for k in range(2):
                mine = blocks[line, k, p.low].astype(F32) + temp[0, line, k, 0].astype(F32)
                blocks[line, k, p.low] = mine.astype(BF16)
                mine = blocks[half + line, p.high, k].astype(F32) + temp[1, line, k, 0].astype(F32)
                blocks[half + line, p.high, k] = mine.astype(BF16)

        self.pairs = [
            p.exchange(blocks.at[near, 1 - p.high, p.low], into.at[0], into.at[0], p.high_peer()),
            p.exchange(blocks.at[far, p.high, 1 - p.low], into.at[1], into.at[1], p.low_peer()),
        ]

    def mine(self, line):
        return self.blocks.at[line, self.place.high, self.place.low]

    def plane_sum(self):
        p, blocks, temp, into = self.place, self.blocks, self.temp, self.lands[1]
        half = p.lines // 2
        finish(self.pairs)
        self.load([(into.at[k], temp.at[k, :, 0, 0]) for k in range(2)])

        @pl.loop(0, half)
        def _(line):
            for k in range(2):
                mine = blocks[k * half + line, p.high, p.low].astype(F32)
                mine += temp[k, line, 0, 0].astype(F32)
                blocks[k * half + line, p.high, p.low] = mine.astype(BF16)

    def line_low(self):
        p, land = self.place, self.lands[2]
        high, low = p.line // 2, lax.rem(p.line, 2)
        peer = p.at(2 * high + 1 - low, p.high, p.low)
        self.pairs = [
            p.exchange(self.mine(2 * k + 1 - low), land.at[k], land.at[k], peer) for k in range(2)
        ]

    def line_high(self):
        p, land, temp = self.place, self.lands[2], self.temp
        high, low = p.line // 2, lax.rem(p.line, 2)
        finish(self.pairs)
        self.load([(land.at[k], temp.at[k, 0, 0, 0]) for k in range(2)])
        for k in range(2):
            mine = self.mine(2 * k + low)
            mine[...] = (mine[...].astype(F32) + temp[k, 0, 0, 0].astype(F32)).astype(BF16)
        peer = 2 * (1 - high) + low
        self.pairs = [
            p.exchange(self.mine(peer), land.at[2], land.at[2], p.at(peer, p.high, p.low))
        ]

    def end(self):
        land, temp = self.lands[2], self.temp
        finish(self.pairs)
        self.load([(land.at[2], temp.at[0, 0, 0, 0])])
        mine = self.mine(self.place.line)
        self.out[...] = mine[...].astype(F32) + temp[0, 0, 0, 0].astype(F32)


class NearScatter(Scatter):
    def second_half(self):
        p, blocks, land, into = self.place, self.blocks, self.lands[0], self.lands[1]
        half = p.lines // 2
        near, far = pl.ds(0, half), pl.ds(half, half)
        finish(self.pairs)

        @pl.loop(0, half)
        def _(line):
            for k in range(2):
                mine = blocks[line, k, p.low].astype(F32) + land[0, line, k].astype(F32)
                blocks[line, k, p.low] = mine.astype(BF16)
                mine = blocks[half + line, p.high, k].astype(F32) + land[1, line, k].astype(F32)
                blocks[half + line, p.high, k] = mine.astype(BF16)

        self.pairs = [
            p.exchange(blocks.at[near, 1 - p.high, p.low], into.at[0], into.at[0], p.high_peer()),
            p.exchange(blocks.at[far, p.high, 1 - p.low], into.at[1], into.at[1], p.low_peer()),
        ]

    def plane_sum(self):
        p, blocks, into = self.place, self.blocks, self.lands[1]
        half = p.lines // 2
        finish(self.pairs)

        @pl.loop(0, half)
        def _(line):
            for k in range(2):
                mine = blocks[k * half + line, p.high, p.low].astype(F32)
                mine += into[k, line].astype(F32)
                blocks[k * half + line, p.high, p.low] = mine.astype(BF16)

    def send_line(self):
        land = self.lands[2]
        self.pairs = self.place.swap_lines(self.mine, lambda line: land.at[line])

    def end_line(self):
        p, land = self.place, self.lands[2]
        finish(self.pairs)
        total = self.mine(p.line)[...].astype(F32)
        for peer in others(p.lines, p.line):
            total += land[peer].astype(F32)
        self.out[...] = total


class LineSum(Scatter):
    def mine(self, line):
        return self.blocks.at[line]


class Move:
    def __init__(self, place, blocks, middle, out, sem):
        self.place, self.blocks, self.middle, self.out, self.sem = place, blocks, middle, out, sem

    def along_line(self):
        p, blocks, middle = self.place, self.blocks, self.middle
        self.keep = pltpu.make_async_copy(blocks.at[p.line], middle.at[p.line], self.sem.at[0])
        self.keep.start()
        self.pairs = p.swap_lines(lambda peer: blocks.at[peer], lambda line: middle.at[line])

    def in_plane(self):
        p, middle, out = self.place, self.middle, self.out
        self.keep.wait()
        finish(self.pairs)
        self.keep = pltpu.make_async_copy(
            middle.at[:, p.high, p.low], out.at[:, p.high, p.low], self.sem.at[1]
        )
        self.keep.start()
        self.pairs = []
        for device, high, low in (
            (p.low_peer(), p.high, 1 - p.low),
            (p.high_peer(), 1 - p.high, p.low),
            (p.across(), 1 - p.high, 1 - p.low),
        ):
            self.pairs.append(
                p.exchange(
                    middle.at[:, high, low],
                    out.at[:, p.high, p.low],
                    out.at[:, high, low],
                    device,
                )
            )

    def end(self):
        self.keep.wait()
        finish(self.pairs)


class Total:
    def __init__(self, place, array, land, sums):
        self.place, self.array, self.land, self.sums = place, array, land, sums

    @staticmethod
    def scratch(lines, size, shape):
        return [pltpu.VMEM((size + 2 + lines,) + shape, F32), pltpu.VMEM((3,) + shape, F32)]

    def in_chip(self):
        self.pairs = self.place.swap_cores(lambda peer: self.array, lambda core: self.land.at[core])

    def low(self):
        p = self.place
        finish(self.pairs)
        total = self.array[...]
        for peer in others(p.size, p.me):
            total += self.land[peer]
        self.sums[0] = total
        land = self.land.at[p.size]
        self.pairs = [p.exchange(self.sums.at[0], land, land, p.low_peer())]

    def high(self):
        p = self.place
        finish(self.pairs)
        self.sums[1] = self.sums[0] + self.land[p.size]
        land = self.land.at[p.size + 1]
        self.pairs = [p.exchange(self.sums.at[1], land, land, p.high_peer())]

    def along_line(self):
        p = self.place
        finish(self.pairs)
        self.sums[2] = self.sums[1] + self.land[p.size + 1]
        self.pairs = p.swap_lines(
            lambda peer: self.sums.at[2], lambda line: self.land.at[p.size + 2 + line]
        )

    def end(self, out):
        p = self.place
        finish(self.pairs)
        total = self.sums[2]
        for peer in others(p.lines, p.line):
            total += self.land[p.size + 2 + peer]
        out[...] = total


ROWS = 64


def in_order(first_full, pair):
    return jnp.where(first_full, pair[0], pair[1]), jnp.where(first_full, pair[1], pair[0])


def forward_kernel(
    frames,
    lines,
    size,
    counts,
    media,
    latents,
    cotangent,
    gain_media,
    shift_media,
    gain_latent,
    shift_latent,
    time_embed,
    query_hbm,
    kv_hbm,
    norm_full_out,
    norm_image_out,
    weight_full_out,
    weight_image_out,
    absorbed_out,
    mixed_out,
    value_out,
    peak_out,
    latent_norm,
    queries,
    cotangent_all,
    cotangent_rows,
    own,
    latent_all,
    norm_full,
    norm_image,
    weight_full,
    weight_image,
    absorbed,
    mixed,
    query_weight,
    kv_weight,
    buffer,
    times,
    media_sem,
    load_sem,
    store_sem,
    gather_sem,
    send_sem,
    recv_sem,
):
    inner = HEADS * HEAD_DIM
    place = Place(lines, size, send_sem, recv_sem)
    me = place.me
    local = latents.shape[1]
    rows = 2 * local
    lat_all = local * size
    first_full = counts[0] > counts[1]
    image_alive = me * frames < jnp.minimum(counts[0], counts[1])

    def fetch(frame, slot):
        return pltpu.make_async_copy(
            media.at[:, pl.ds(frame * PATCH, PATCH)], buffer.at[slot], media_sem.at[slot]
        )

    load_query = pltpu.make_async_copy(query_hbm, query_weight, load_sem.at[0])
    load_kv = pltpu.make_async_copy(kv_hbm, kv_weight, load_sem.at[1])
    times[...] = time_embed[...].astype(F32)
    fetch(0, 0).start()
    load_query.start()
    load_kv.start()
    place.greet()
    for k, array in ((0, latents), (1, cotangent)):
        pair = in_order(first_full, (array[0].astype(F32), array[1].astype(F32)))
        own[k] = jnp.concatenate(pair, 0).astype(BF16)
    latent_swap = place.swap_cores(lambda p: own.at[0], lambda c: latent_all.at[c])
    cotangent_swap = place.swap_cores(lambda p: own.at[1], lambda c: cotangent_all.at[c])
    gather = Gather(place, own.at[1], cotangent_rows, gather_sem.at[0])
    gather.along_line()
    latent_all[me] = own[0]
    cotangent_all[me] = own[1]

    gain_m, shift_m = vector(gain_media), vector(shift_media)
    gain_l, shift_l = vector(gain_latent), vector(shift_latent)

    def normalize_frame(frame, slot, pick_first, target, base):
        time_row = times[pl.ds(me * frames + frame, 1)]

        @pl.loop(0, PATCH // ROWS)
        def _(part):
            at = pl.multiple_of(part * ROWS, ROWS)
            values = jnp.where(
                pick_first,
                buffer[slot, 0, pl.ds(at, ROWS)].astype(F32),
                buffer[slot, 1, pl.ds(at, ROWS)].astype(F32),
            )
            unit, _ = normalize(values + time_row)
            target[pl.ds(pl.multiple_of(base + at, ROWS), ROWS)] = (unit * gain_m + shift_m).astype(
                BF16
            )

    @pl.loop(0, frames)
    def _(frame):
        slot = lax.rem(frame, 2)
        fetch(frame, slot).wait()

        @pl.when(frame + 1 < frames)
        def _():
            fetch(frame + 1, 1 - slot).start()

        normalize_frame(frame, slot, first_full, norm_full, frame * PATCH)

        @pl.when(frame == 0)
        def _():
            normalize_frame(frame, slot, jnp.logical_not(first_full), norm_image, 0)

    unit, _ = normalize(own[0].astype(F32))
    low = (unit * gain_l + shift_l).astype(BF16)
    norm_full[frames * PATCH : frames * PATCH + local] = low[:local]
    norm_image[PATCH : PATCH + local] = low[local:]
    finish(latent_swap)
    for item in range(2):
        for core in range(size):
            unit, _ = normalize(latent_all[core, item * local : (item + 1) * local].astype(F32))
            at = item * lat_all + core * local
            latent_norm[at : at + local] = (unit * gain_l + shift_l).astype(BF16)
    stores = []

    def store(source, target):
        copy = pltpu.make_async_copy(source, target, store_sem.at[len(stores)])
        copy.start()
        stores.append(copy)

    store(norm_full, norm_full_out)
    store(norm_image, norm_image_out)
    load_query.wait()

    @pl.loop(0, GROUPS)
    def _(group):
        span = pl.ds(pl.multiple_of(group * SPAN, SPAN), SPAN)
        queries[:, span] = dot(latent_norm[...], query_weight[:, span], 1, 0).astype(BF16)

    load_kv.wait()
    step = GROUP * lat_all
    lane = lax.broadcasted_iota(jnp.int32, (lat_all, 128), 1)
    outer_lane = lax.broadcasted_iota(jnp.int32, (rows, 128), 1)
    for core in range(size):
        peak_out[core, 0] = jnp.zeros((rows, 128), F32)
        peak_out[core, 1] = jnp.where(outer_lane < HEADS, 0.0, 1.0)
    for item, keys, weights, weights_out in (
        (0, norm_full, weight_full, weight_full_out),
        (1, norm_image, weight_image, weight_image_out),
    ):
        count = keys.shape[0]
        row = lax.broadcasted_iota(jnp.int32, (count, 1), 0)
        live = (row >= count - local) | image_alive

        def attend_group(group, item=item, keys=keys, weights=weights, live=live):
            span = pl.ds(pl.multiple_of(group * SPAN, SPAN), SPAN)
            value_span = pl.ds(pl.multiple_of(inner + group * SPAN, SPAN), SPAN)
            at = pl.ds(pl.multiple_of(group * step, step), step)
            spread = spread_heads(queries[item * lat_all : (item + 1) * lat_all, span])
            key_rows = (dot(spread, kv_weight[:, span], 1, 1) * SCALE).astype(BF16)
            absorbed[item, at] = key_rows
            scores = dot(keys[...], key_rows, 1, 1)
            if item == 1:
                scores = jnp.where(live, scores, -1e30)
            peak = jnp.max(scores, 0, keepdims=True)
            weight = jnp.exp(scores - peak)
            if item == 1:
                weight = jnp.where(live, weight, 0.0)
            total = jnp.sum(weight, 0, keepdims=True)
            low = weight.astype(BF16)
            weights[:, at] = low
            mix = dot(low, keys[...], 0, 0).astype(BF16)
            mixed[item, at] = mix
            values = fold_heads(dot(mix, kv_weight[:, value_span], 1, 0))
            statistics = []
            for row_values in (peak, total):
                down = down_rows(row_values)
                picked = jnp.zeros((lat_all, 128), F32)
                for h in range(GROUP):
                    rows_of_head = down[h * lat_all : (h + 1) * lat_all]
                    picked += jnp.where(lane == group * GROUP + h, rows_of_head, 0.0)
                statistics.append(picked)
            for core in range(size):
                mine = slice(core * local, (core + 1) * local)
                into = slice(item * local, (item + 1) * local)
                value_out[core, into, span] = values[mine]
                for k in range(2):
                    peak_out[core, k, into] += statistics[k][mine]

        if item == 0:
            pl.loop(0, 1)(attend_group)
            gather.first_half()
            pl.loop(1, GROUPS - 1)(attend_group)
            gather.second_half()
            pl.loop(GROUPS - 1, GROUPS)(attend_group)
        else:
            pl.loop(0, GROUPS)(attend_group)
        store(weights, weights_out)
        store(absorbed.at[item], absorbed_out.at[item])
        store(mixed.at[item], mixed_out.at[item])
    for copy in stores:
        copy.wait()
    finish(cotangent_swap)
    gather.end()


def attend_forward(
    chips,
    size,
    counts,
    media,
    latents,
    cotangent,
    gain_media,
    shift_media,
    gain_latent,
    shift_latent,
    time_embed,
    query_weight,
    kv_weight,
):
    width = media.shape[-1]
    inner = HEADS * HEAD_DIM
    lines = chips // 4
    frames = media.shape[1] // PATCH
    local = latents.shape[1]
    rows = 2 * local
    lat_all = local * size
    keys = (frames * PATCH + local, PATCH + local)
    slots = HEADS * lat_all
    shape = jax.ShapeDtypeStruct
    copies = lines + 2 * size + 8
    return pl.pallas_call(
        functools.partial(forward_kernel, frames, lines, size),
        out_shape=[
            shape((keys[0], width), BF16),
            shape((keys[1], width), BF16),
            shape((keys[0], slots), BF16),
            shape((keys[1], slots), BF16),
            shape((2, slots, width), BF16),
            shape((2, slots, width), BF16),
            shape((size, rows, inner), F32),
            shape((size, 2, rows, 128), F32),
            shape((2 * lat_all, width), BF16),
            shape((2 * lat_all, inner), BF16),
            shape((size, rows, width), BF16),
            shape((lines, 2, 2, rows, width), BF16),
        ],
        in_specs=[SMEM, ANY] + [VMEM] * 7 + [ANY] * 2,
        out_specs=[ANY] * 6 + [VMEM] * 5 + [ANY],
        scratch_shapes=[
            pltpu.VMEM((2, rows, width), BF16),
            pltpu.VMEM((size, rows, width), BF16),
            pltpu.VMEM((keys[0], width), BF16),
            pltpu.VMEM((keys[1], width), BF16),
            pltpu.VMEM((keys[0], slots), BF16),
            pltpu.VMEM((keys[1], slots), BF16),
            pltpu.VMEM((2, slots, width), BF16),
            pltpu.VMEM((2, slots, width), BF16),
            pltpu.VMEM(query_weight.shape, BF16),
            pltpu.VMEM(kv_weight.shape, BF16),
            pltpu.VMEM((2, 2, PATCH, width), BF16),
            pltpu.VMEM(time_embed.shape, F32),
            pltpu.SemaphoreType.DMA((2,)),
            pltpu.SemaphoreType.DMA((2,)),
            pltpu.SemaphoreType.DMA((8,)),
            pltpu.SemaphoreType.DMA((1,)),
            pltpu.SemaphoreType.DMA((copies,)),
            pltpu.SemaphoreType.DMA((copies,)),
        ],
        compiler_params=params(collective_id=0, has_side_effects=True),
    )(
        counts,
        media,
        latents,
        cotangent,
        gain_media,
        shift_media,
        gain_latent,
        shift_latent,
        time_embed,
        query_weight,
        kv_weight,
    )


DEPTH = 2


def latent_kernel(
    lines,
    size,
    chunk,
    counts,
    value_parts,
    peaks,
    latents,
    cotangent_all,
    gain_ffn,
    shift_ffn,
    out_hbm,
    in_hbm,
    down_hbm,
    kv_hbm,
    mixed_hbm,
    norm_full_hbm,
    norm_image_hbm,
    weight_full_hbm,
    weight_image_hbm,
    cotangent_rows,
    queries,
    latent_norm,
    latent_out,
    state_grad,
    gains,
    into_out,
    score_full_out,
    score_image_out,
    query_all,
    out_plane,
    query_half,
    key_half,
    value_half,
    ffn_rows,
    cotangent_other,
    key_wait,
    value_wait,
    out_first,
    out_second,
    out_weight,
    in_weight,
    down_weight,
    column_weight,
    norm_full,
    norm_image,
    weight_full,
    weight_image,
    score_full,
    score_image,
    mixed,
    value_land,
    peak_land,
    ffn_norm,
    partial,
    partial_land,
    kept,
    kept_log,
    attended_all,
    update_all,
    grad_all,
    log_all,
    grad_items,
    stage,
    query_part,
    query_land,
    out_blocks,
    temp,
    load_sem,
    weight_sem,
    column_sem,
    half_sem,
    store_sem,
    scatter_sem,
    gather_sem,
    send_sem,
    recv_sem,
):
    inner = HEADS * HEAD_DIM
    place = Place(lines, size, send_sem, recv_sem)
    me = place.me
    first_full = counts[0] > counts[1]
    local, width = latents.shape[1:]
    rows = 2 * local
    lat_all = local * size
    step = GROUP * lat_all
    chunks = in_hbm.shape[1] // chunk
    cores = others(size, me)

    def weights(c):
        at = pl.ds(pl.multiple_of(c * chunk, chunk), chunk)
        slot = lax.rem(c, DEPTH)
        return (
            pltpu.make_async_copy(in_hbm.at[:, at], in_weight.at[slot], weight_sem.at[0, slot]),
            pltpu.make_async_copy(down_hbm.at[at, :], down_weight.at[slot], weight_sem.at[1, slot]),
        )

    loads = [
        pltpu.make_async_copy(out_hbm, out_weight, load_sem.at[0]),
        pltpu.make_async_copy(mixed_hbm, mixed, load_sem.at[1]),
        pltpu.make_async_copy(norm_full_hbm, norm_full, load_sem.at[2]),
        pltpu.make_async_copy(norm_image_hbm, norm_image, load_sem.at[3]),
        pltpu.make_async_copy(weight_full_hbm, weight_full, load_sem.at[4]),
        pltpu.make_async_copy(weight_image_hbm, weight_image, load_sem.at[5]),
    ]

    def column(n):
        first = inner + n * SPAN if n < GROUPS else (n - GROUPS) * SPAN
        return pltpu.make_async_copy(
            kv_hbm.at[:, pl.ds(first, SPAN)], column_weight.at[n % 2], column_sem.at[n % 2]
        )

    loads[0].start()
    for c in range(min(DEPTH, chunks)):
        for copy in weights(c):
            copy.start()
    for copy in loads[1:]:
        copy.start()
    column(0).start()
    place.greet()
    values_swap = place.swap_cores(lambda p: value_parts.at[p], lambda c: value_land.at[c])
    peaks_swap = place.swap_cores(lambda p: peaks.at[p], lambda c: peak_land.at[c])
    cotangent_swap = place.swap_cores(
        lambda p: cotangent_rows, lambda c: cotangent_other.at[c]
    )
    value_land[me] = value_parts[me]
    peak_land[me] = peaks[me]
    selector = head_selector()
    finish(values_swap)
    finish(peaks_swap)
    peak = peak_land[0, 0]
    for s in range(1, size):
        peak = jnp.maximum(peak, peak_land[s, 0])
    factors = [jnp.exp(peak_land[s, 0] - peak) for s in range(size)]
    total = factors[0] * peak_land[0, 1]
    for s in range(1, size):
        total += factors[s] * peak_land[s, 1]
    kept_log[...] = peak + jnp.log(total)
    attended = jnp.zeros((rows, width), F32)
    for s in range(size):
        attended += value_land[s] * dot_exact(factors[s] / total, selector)
    kept[0] = attended
    attended_low = attended.astype(BF16)
    attended_all[me] = attended_low
    loads[0].wait()
    hidden = dot(attended_low, out_weight[...], 1, 0)
    hidden += jnp.concatenate(
        in_order(first_full, (latents[0].astype(F32), latents[1].astype(F32))), 0
    )
    kept[1] = hidden
    gain, shift = vector(gain_ffn), vector(shift_ffn)
    unit, _ = normalize(hidden)
    ffn_norm[me] = (unit * gain + shift).astype(BF16)
    norm_swap = place.swap_cores(lambda p: ffn_norm.at[me], lambda c: ffn_norm.at[c])
    gather = Gather(place, ffn_norm.at[me], ffn_rows, gather_sem.at[0])
    gather.along_line()
    attended_swap = place.swap_cores(lambda p: attended_all.at[me], lambda c: attended_all.at[c])
    partial[...] = jnp.zeros_like(partial)
    finish(norm_swap)

    def feed_forward(c):
        for copy in weights(c):
            copy.wait()
        slot = lax.rem(c, DEPTH)
        all_rows = ffn_norm[...].reshape(size * rows, width)
        cotangents = cotangent_all[...].reshape(size * rows, width)
        activated, slope = gelu_parts(dot(all_rows, in_weight[slot], 1, 0))
        activated = activated.astype(BF16)
        act_grad = dot(cotangents, down_weight[slot], 1, 1)
        pre_grad = (act_grad * slope).astype(BF16)
        partial[0] += dot(activated, down_weight[slot], 1, 0).reshape(size, rows, width)
        partial[1] += dot(pre_grad, in_weight[slot], 1, 1).reshape(size, rows, width)

        @pl.when(c + DEPTH < chunks)
        def _():
            for copy in weights(c + DEPTH):
                copy.start()

    pl.loop(0, chunks)(feed_forward)
    sums_swap = place.swap_cores(lambda p: partial.at[:, p], lambda c: partial_land.at[c])
    gather.first_half()
    finish(sums_swap)
    ffn_sum, norm_grad = partial[0, me], partial[1, me]
    for origin in cores:
        ffn_sum += partial_land[origin, 0]
        norm_grad += partial_land[origin, 1]
    hidden = kept[1]
    unit, inverse = normalize(hidden)
    result = hidden + ffn_sum
    for k, value in enumerate(in_order(first_full, (result[:local], result[local:]))):
        latent_out[k] = value.astype(BF16)
    gains[0:1] = jnp.sum(norm_grad * unit, 0, keepdims=True)
    gains[1:2] = jnp.sum(norm_grad, 0, keepdims=True)
    state = cotangent_all[me].astype(F32) + norm_back(unit, inverse, gain, norm_grad)
    state_grad[...] = state
    update = state.astype(BF16)
    update_all[me] = update
    grad = dot(update, out_weight[...], 1, 1).astype(BF16)
    grad_all[me] = grad
    log_all[me, 0] = kept_log[...]
    log_all[me, 1] = head_sums(grad.astype(F32) * kept[0])
    grad_swap = place.swap_cores(lambda p: grad_all.at[me], lambda c: grad_all.at[c])
    log_swap = place.swap_cores(lambda p: log_all.at[me], lambda c: log_all.at[c])
    update_swap = place.swap_cores(lambda p: update_all.at[me], lambda c: update_all.at[c])
    finish(grad_swap)
    finish(log_swap)

    def by_item(item, of_core):
        part = slice(item * local, (item + 1) * local)
        return jnp.concatenate([of_core(core)[part] for core in range(size)], 0)

    factor, factor_delta = [], []
    for item in range(2):
        grad_items[item] = by_item(item, lambda c: grad_all[c])
        scale = jnp.exp(
            by_item(item, lambda c: peaks[c, 0]) - by_item(item, lambda c: log_all[c, 0])
        )
        factor.append(scale)
        factor_delta.append(scale * by_item(item, lambda c: log_all[c, 1]))
    block_rows = width // (lines * 4 * size)
    uses = []

    def stage_blocks(low):
        slot = len(uses) % 2
        if len(uses) >= 2:
            sends, copy = uses[len(uses) - 2]
            finish_sends(sends)
            copy.wait()
        for k in range(lines * 4):
            for core in range(size):
                base = (k * size + core) * block_rows
                stage[slot, k // 4, (k // 2) % 2, k % 2, core] = low[base : base + block_rows]
        return slot

    def split_cores(low, group, half, wait):
        slot = stage_blocks(low)
        columns = pl.ds(group * SPAN, SPAN)
        sends = place.swap_cores(
            lambda p: stage.at[slot, :, :, :, p], lambda c: wait.at[c, :, :, :, :, columns]
        )
        keep_half(slot, columns, half, sends)

    def keep_half(slot, columns, half, sends):
        copy = pltpu.make_async_copy(
            stage.at[slot, :, :, :, me], half.at[:, :, :, :, columns], half_sem.at[slot]
        )
        copy.start()
        uses.append((sends, copy))

    stores = []

    def store(source, target):
        copy = pltpu.make_async_copy(source, target, store_sem.at[len(stores)])
        copy.start()
        stores.append(copy)

    outs = Scatter(place, out_blocks, (out_first, out_second, None), temp, scatter_sem, None)
    finish(attended_swap)
    finish(update_swap)
    updates = update_all[...].reshape(size * rows, width)
    for group in range(GROUPS):
        span = slice(group * SPAN, (group + 1) * SPAN)
        attends = attended_all[:, :, span].reshape(size * rows, SPAN)
        low = dot(updates, attends, 0, 0)
        for k in range(lines * 4):
            base = k * size * block_rows
            mine = low[base : base + block_rows]
            for core in range(1, size):
                base += block_rows
                mine = jnp.where(me == core, low[base : base + block_rows], mine)
            out_blocks[k // 4, (k // 2) % 2, k % 2, :, span] = mine.astype(BF16)
    outs.first_half()
    for copy in loads[1:]:
        copy.wait()
    shifts = []
    for group in range(GROUPS):
        span = slice(group * SPAN, (group + 1) * SPAN)
        at = slice(group * step, (group + 1) * step)
        column(group + 1).start()
        column(group).wait()
        weight = None
        for item in range(2):
            spread = spread_heads(grad_items[item, :, span])
            heads = range(group * GROUP, (group + 1) * GROUP)
            scale = jnp.concatenate([own_columns(factor[item], h) for h in heads], 0)
            shifts.append(
                across_lanes(
                    jnp.concatenate([own_columns(factor_delta[item], h) for h in heads], 0)
                )
            )
            spread = (spread.astype(F32) * scale).astype(BF16)
            part = dot(mixed[item, at], spread, 0, 0)
            weight = part if weight is None else weight + part
            mixed[item, at] = dot(spread, column_weight[group % 2], 1, 1).astype(BF16)
        split_cores(weight.astype(BF16), group, value_half, value_wait)
    for item in range(2):
        store(mixed.at[item], into_out.at[item])
    gather.second_half()
    for group in range(GROUPS):
        span = slice(group * SPAN, (group + 1) * SPAN)
        at = slice(group * step, (group + 1) * step)
        if group + 1 < GROUPS:
            column(GROUPS + group + 1).start()
        column(GROUPS + group).wait()
        weight = None
        for item, keys, weights, scores in (
            (0, norm_full, weight_full, score_full),
            (1, norm_image, weight_image, score_image),
        ):
            item_rows = slice(item * lat_all, (item + 1) * lat_all)
            prob_grad = dot(keys[...], mixed[item, at], 1, 1)
            score = weights[:, at].astype(F32) * (prob_grad - shifts[2 * group + item])
            score = score.astype(BF16)
            scores[:, at] = score
            pulled = dot(score, keys[...], 0, 0).astype(BF16)
            query_part[item_rows, span] = (
                fold_heads(dot(pulled, column_weight[group % 2], 1, 0)) * SCALE
            )
            part = dot(pulled, spread_heads(queries[item_rows, span]), 0, 0)
            weight = part if weight is None else weight + part
        split_cores((weight * SCALE).astype(BF16), group, key_half, key_wait)
        if group == 1:
            outs.second_half()
    store(score_full, score_full_out)
    store(score_image, score_image_out)
    query_swap = place.swap_cores(lambda p: query_part, lambda c: query_land.at[c])
    finish(query_swap)
    total_query = query_part[...]
    for origin in cores:
        total_query += query_land[origin]
    query_all[...] = total_query.astype(BF16)
    for group in range(GROUPS):
        span = slice(group * SPAN, (group + 1) * SPAN)
        slot = stage_blocks(dot(latent_norm[...], query_all[:, span], 0, 0).astype(BF16))
        keep_half(slot, pl.ds(group * SPAN, SPAN), query_half, [])
    for sends, copy in uses[-2:]:
        finish_sends(sends)
        copy.wait()
    for sends, _ in uses:
        finish_arrivals(sends)
    finish(cotangent_swap)
    outs.plane_sum()
    store(out_blocks.at[:, place.high, place.low], out_plane)
    gather.end()
    for copy in stores:
        copy.wait()


def latent_pass(
    chips,
    size,
    counts,
    value_parts,
    peaks,
    latents,
    cotangent_all,
    gain_ffn,
    shift_ffn,
    out_weight,
    in_weight,
    down_weight,
    kv_weight,
    mixed,
    norm_full,
    norm_image,
    weight_full,
    weight_image,
    cotangent_rows,
    queries,
    latent_norm,
):
    lines = chips // 4
    local, width = latents.shape[1:]
    inner = HEADS * HEAD_DIM
    rows = 2 * local
    lat_all = local * size
    hidden_units = in_weight.shape[1]
    chunk = 512 if hidden_units % 512 == 0 else 256
    block_rows = width // (chips * size)
    blocks = (lines, 2, 2, block_rows, inner)
    gathered = (lines, 2, 2, rows, width)
    shape = jax.ShapeDtypeStruct
    copies = 3 * lines + 24 * size + 20
    return pl.pallas_call(
        functools.partial(latent_kernel, lines, size, chunk),
        out_shape=[
            shape(latents.shape, BF16),
            shape((rows, width), F32),
            shape((2, width), F32),
            shape(mixed.shape, BF16),
            shape(weight_full.shape, BF16),
            shape(weight_image.shape, BF16),
            shape((2 * lat_all, inner), BF16),
            shape((lines, block_rows, inner), BF16),
            shape(blocks, BF16),
            shape(blocks, BF16),
            shape(blocks, BF16),
            shape(gathered, BF16),
            shape((size,) + gathered, BF16),
            shape((size,) + blocks, BF16),
            shape((size,) + blocks, BF16),
            *Scatter.lands(lines, block_rows, inner)[:2],
        ],
        in_specs=[SMEM] + [VMEM] * 6 + [ANY] * 10 + [VMEM] * 2,
        out_specs=[VMEM] * 3 + [ANY] * 3 + [VMEM] + [ANY] * 10,
        scratch_shapes=[
            pltpu.VMEM(out_weight.shape, BF16),
            pltpu.VMEM((DEPTH, width, chunk), BF16),
            pltpu.VMEM((DEPTH, chunk, width), BF16),
            pltpu.VMEM((2, width, SPAN), BF16),
            pltpu.VMEM(norm_full.shape, BF16),
            pltpu.VMEM(norm_image.shape, BF16),
            pltpu.VMEM(weight_full.shape, BF16),
            pltpu.VMEM(weight_image.shape, BF16),
            pltpu.VMEM(weight_full.shape, BF16),
            pltpu.VMEM(weight_image.shape, BF16),
            pltpu.VMEM(mixed.shape, BF16),
            pltpu.VMEM((size, rows, width), F32),
            pltpu.VMEM((size, 2, rows, 128), F32),
            pltpu.VMEM((size, rows, width), BF16),
            pltpu.VMEM((2, size, rows, width), F32),
            pltpu.VMEM((size, 2, rows, width), F32),
            pltpu.VMEM((2, rows, width), F32),
            pltpu.VMEM((rows, 128), F32),
            pltpu.VMEM((size, rows, inner), BF16),
            pltpu.VMEM((size, rows, width), BF16),
            pltpu.VMEM((size, rows, inner), BF16),
            pltpu.VMEM((size, 2, rows, 128), F32),
            pltpu.VMEM((2, lat_all, inner), BF16),
            pltpu.VMEM((2, lines, 2, 2, size, block_rows, SPAN), BF16),
            pltpu.VMEM((2 * lat_all, inner), F32),
            pltpu.VMEM((size, 2 * lat_all, inner), F32),
            pltpu.VMEM(blocks, BF16),
            pltpu.VMEM((2, lines // 2, 2, 1, block_rows, inner), BF16),
            pltpu.SemaphoreType.DMA((6,)),
            pltpu.SemaphoreType.DMA((2, DEPTH)),
            pltpu.SemaphoreType.DMA((2,)),
            pltpu.SemaphoreType.DMA((2,)),
            pltpu.SemaphoreType.DMA((5,)),
            pltpu.SemaphoreType.DMA((max(2, lines),)),
            pltpu.SemaphoreType.DMA((2,)),
            pltpu.SemaphoreType.DMA((copies,)),
            pltpu.SemaphoreType.DMA((copies,)),
        ],
        compiler_params=params(collective_id=1, has_side_effects=True),
    )(
        counts,
        value_parts,
        peaks,
        latents,
        cotangent_all,
        gain_ffn,
        shift_ffn,
        out_weight,
        in_weight,
        down_weight,
        kv_weight,
        mixed,
        norm_full,
        norm_image,
        weight_full,
        weight_image,
        cotangent_rows,
        queries,
        latent_norm,
    )


def backward_kernel(
    frames,
    lines,
    size,
    counts,
    media,
    latents,
    gain_media,
    gain_latent,
    shift_latent,
    time_embed,
    query_hbm,
    weight_full_hbm,
    weight_image_hbm,
    score_full_hbm,
    score_image_hbm,
    absorbed_hbm,
    into_hbm,
    out_plane,
    query_half,
    key_half,
    value_half,
    key_wait,
    value_wait,
    ffn_rows,
    cotangent_rows,
    cotangent_other,
    query_all,
    state_grad,
    ffn_gains,
    in_hbm,
    down_hbm,
    slot_grad,
    latent_grad,
    out_sum,
    query_sum,
    key_sum,
    value_sum,
    units_out,
    small_out,
    ffn_other,
    units_middle,
    out_line,
    query_first,
    query_second,
    query_line,
    key_first,
    key_second,
    key_line,
    out_blocks,
    query_blocks,
    key_blocks,
    value_blocks,
    temp,
    column_weight,
    weight_full,
    weight_image,
    score_full,
    score_image,
    absorbed,
    into,
    in_share,
    down_share,
    buffer,
    share_sum,
    units,
    block,
    result,
    times,
    small,
    small_land,
    small_sums,
    value_first,
    value_second,
    value_line,
    load_sem,
    column_sem,
    buffer_sem,
    result_sem,
    scatter_sem,
    move_sem,
    send_sem,
    recv_sem,
):
    inner = HEADS * HEAD_DIM
    width = media.shape[-1]
    place = Place(lines, size, send_sem, recv_sem)
    me = place.me
    cores = others(size, me)
    first_full = counts[0] > counts[1]
    local = latents.shape[1]
    lat_all = local * size
    half = lines // 2
    share = down_share.shape[0]
    down_first = pl.multiple_of(place.dp * share, share)
    offset = lax.rem(place.dp * share, 128)
    in_first = pl.multiple_of(place.dp * share - offset, 128)

    loads = [
        pltpu.make_async_copy(source, target, load_sem.at[k])
        for k, (source, target) in enumerate(
            (
                (out_plane, out_blocks),
                (query_half, query_blocks),
                (key_half, key_blocks),
                (value_half, value_blocks),
                (weight_full_hbm, weight_full),
                (weight_image_hbm, weight_image),
                (score_full_hbm, score_full),
                (score_image_hbm, score_image),
                (into_hbm, into),
                (absorbed_hbm, absorbed),
                (in_hbm.at[:, pl.ds(in_first, in_share.shape[1])], in_share),
                (down_hbm.at[pl.ds(down_first, share), :], down_share),
            )
        )
    ]

    def column(group):
        return pltpu.make_async_copy(
            query_hbm.at[:, pl.ds(group * SPAN, SPAN)],
            column_weight.at[group % 2],
            column_sem.at[group % 2],
        )

    own_pieces = [(ffn_rows, cotangent_rows, line) for line in range(lines)]
    pieces = own_pieces + [
        (ffn_other.at[core], cotangent_other.at[core], line) for core in cores for line in range(lines)
    ]
    device_rows = ffn_rows.shape[3]
    piece_rows = 4 * device_rows

    def piece(k):
        ffn_source, cotangent_source, line = pieces[k]
        return [
            pltpu.make_async_copy(
                source.at[line, n // 2, n % 2],
                buffer.at[k % 2, j, pl.ds(n * device_rows, device_rows)],
                buffer_sem.at[k % 2, j, n],
            )
            for j, source in ((0, ffn_source), (1, cotangent_source))
            for n in range(4)
        ]

    for copy in loads[:2] + piece(0) + loads[10:] + loads[2:10]:
        copy.start()
    column(0).start()
    place.greet()

    def scatter(blocks, lands, out):
        return Scatter(place, blocks, lands, temp, scatter_sem, out)

    quer = scatter(query_blocks, (query_first, query_second, query_line), query_sum)
    keys = scatter(key_blocks, (key_first, key_second, key_line), key_sum)
    vals = NearScatter(
        place, value_blocks, (value_first, value_second, value_line), None, None, value_sum
    )

    def add_cores(blocks, wait):
        for origin in cores:
            for k in range(2):
                load = pltpu.make_async_copy(
                    wait.at[origin, pl.ds(k * half, half)], temp.at[k], scatter_sem.at[k]
                )
                load.start()
            for k in range(2):
                pltpu.make_async_copy(
                    wait.at[origin, pl.ds(k * half, half)], temp.at[k], scatter_sem.at[k]
                ).wait()

            @pl.loop(0, half)
            def _(line):
                for k in range(2):
                    for high in range(2):
                        for low in range(2):
                            mine = blocks[k * half + line, high, low].astype(F32)
                            mine += temp[k, line, high, low].astype(F32)
                            blocks[k * half + line, high, low] = mine.astype(BF16)

    outs = LineSum(place, out_blocks, (None, None, out_line), temp, scatter_sem, out_sum)
    for copy in loads[:2]:
        copy.wait()
    outs.line_low()
    quer.first_half()
    ffn_swap = place.swap_cores(lambda p: ffn_rows, lambda c: ffn_other.at[c])
    small[...] = jnp.zeros_like(small)
    times[...] = time_embed[...].astype(F32)

    for copy in loads[10:]:
        copy.wait()
    in_part = in_share[:, :share]
    for first in range(64, in_share.shape[1] - share + 1, 64):
        in_part = jnp.where(offset == first, in_share[:, first : first + share], in_part)
    in_share[:, :share] = in_part
    for k in range(len(pieces)):
        if k + 1 == len(own_pieces):
            finish(ffn_swap)
        if k == 2:
            loads[2].wait()
            add_cores(key_blocks, key_wait)
            keys.first_half()
            outs.line_high()
        if k == 6:
            loads[3].wait()
            add_cores(value_blocks, value_wait)
            quer.second_half()
            vals.first_half()
        if k + 1 < len(pieces):
            for copy in piece(k + 1):
                copy.start()
        for copy in piece(k):
            copy.wait()
        ffn_piece = buffer[k % 2, 0, :piece_rows]
        cotangent_piece = buffer[k % 2, 1, :piece_rows]
        activated, slope = gelu_parts(dot(ffn_piece, in_share[:, :share], 1, 0))
        pre_grad = (dot(cotangent_piece, down_share[...], 1, 1) * slope).astype(BF16)
        up = dot(ffn_piece, pre_grad, 0, 0)
        down = dot(cotangent_piece, activated.astype(BF16), 0, 0)
        if k == 0:
            share_sum[0], share_sum[1] = up, down
        else:
            share_sum[0] += up
            share_sum[1] += down
    unit_rows = width // (lines * 4)
    for k in range(lines * 4):
        at = slice(k * unit_rows, (k + 1) * unit_rows)
        both = jnp.concatenate([share_sum[0, at], share_sum[1, at]], 1)
        units[k // 4, (k // 2) % 2, k % 2] = both.astype(BF16)
    moved = Move(place, units, units_middle, units_out, move_sem)
    moved.along_line()

    def fetch(frame):
        return pltpu.make_async_copy(
            media.at[:, pl.ds(frame * PATCH, PATCH)], buffer.at[frame % 2], buffer_sem.at[frame % 2, 0, 0]
        )

    fetch(0).start()
    outs.end()
    for copy in loads[4:10]:
        copy.wait()

    def back(scores, weights, item, at, count):
        rows = slice(at, at + count)
        return dot(scores[rows], absorbed[item], 1, 0) + dot(weights[rows], into[item], 1, 0)

    row_grad = [
        back(score_full, weight_full, 0, frames * PATCH, local),
        back(score_image, weight_image, 1, PATCH, local),
    ]
    row_grad = jnp.concatenate(row_grad, 0)
    mine = [
        query_all[pl.ds(pl.multiple_of(item * lat_all + me * local, local), local)]
        for item in range(2)
    ]
    mine = jnp.concatenate(mine, 0)
    for group in range(GROUPS):
        if group + 1 < GROUPS:
            column(group + 1).start()
        column(group).wait()
        span = slice(group * SPAN, (group + 1) * SPAN)
        row_grad += dot(mine[:, span], column_weight[group % 2], 1, 1)
    own = jnp.concatenate(
        in_order(first_full, (latents[0].astype(F32), latents[1].astype(F32))), 0
    )
    unit, inverse = normalize(own)
    small[2:3] = jnp.sum(row_grad * unit, 0, keepdims=True)
    small[3:4] = jnp.sum(row_grad, 0, keepdims=True)
    small[4:6] = ffn_gains[...]
    row_grad = state_grad[...] + norm_back(unit, inverse, vector(gain_latent), row_grad)
    for k, value in enumerate(in_order(first_full, (row_grad[:local], row_grad[local:]))):
        latent_grad[k] = value

    keys.second_half()
    quer.plane_sum()
    quer.line_low()

    gain = vector(gain_media)
    total = Total(place, small, small_land, small_sums)

    def norm_frame(frame, slot, pick_first, target):
        at_time = 6 + me * frames + frame
        time_row = times[pl.ds(me * frames + frame, 1)]

        @pl.loop(0, PATCH // ROWS)
        def _(part):
            at = pl.ds(pl.multiple_of(part * ROWS, ROWS), ROWS)
            values = jnp.where(
                pick_first, buffer[slot, 0, at].astype(F32), buffer[slot, 1, at].astype(F32)
            )
            unit, inverse = normalize(values + time_row)
            grad = block[at]
            rows_grad = norm_back(unit, inverse, gain, grad)
            target[at] = rows_grad.astype(BF16)
            small[0:1] += jnp.sum(grad * unit, 0, keepdims=True)
            small[1:2] += jnp.sum(grad, 0, keepdims=True)
            small[pl.ds(at_time, 1)] += jnp.sum(rows_grad, 0, keepdims=True)

    puts = []
    for k in range(frames + 1):
        frame = max(0, k - 1)
        if k != 1:
            fetch(frame).wait()
        if k >= 1 and frame + 1 < frames:
            fetch(frame + 1).start()
        if k == 0:
            block[...] = back(score_image, weight_image, 1, 0, PATCH)
        else:
            block[...] = back(score_full, weight_full, 0, frame * PATCH, PATCH)
        if k >= 2:
            puts[k - 2].wait()
        picked = jnp.logical_not(first_full) if k == 0 else first_full
        norm_frame(frame, frame % 2, picked, result.at[k % 2])
        puts.append(
            pltpu.make_async_copy(
                result.at[k % 2], slot_grad.at[pl.ds(k * PATCH, PATCH)], result_sem.at[k % 2]
            )
        )
        puts[k].start()
        if k == 2:
            vals.second_half()
    total.in_chip()
    keys.plane_sum()
    keys.line_low()
    total.low()
    quer.line_high()
    vals.plane_sum()
    vals.send_line()
    total.high()
    moved.in_plane()
    total.along_line()
    keys.line_high()
    total.end(small_out)
    quer.end()
    keys.end()
    vals.end_line()
    moved.end()
    for put in puts[max(0, frames - 1) :]:
        put.wait()


def attend_backward(
    chips,
    size,
    counts,
    media,
    latents,
    gain_media,
    gain_latent,
    shift_latent,
    time_embed,
    query_weight,
    weight_full,
    weight_image,
    score_full,
    score_image,
    absorbed,
    into,
    out_plane,
    query_half,
    key_half,
    value_half,
    key_wait,
    value_wait,
    ffn_rows,
    cotangent_rows,
    cotangent_other,
    query_all,
    state_grad,
    ffn_gains,
    in_weight,
    down_weight,
):
    width = media.shape[-1]
    inner = HEADS * HEAD_DIM
    lines = chips // 4
    frames = media.shape[1] // PATCH
    block_rows = width // (chips * size)
    blocks = (lines, 2, 2, block_rows, inner)
    share = in_weight.shape[1] // chips
    unit = (lines, 2, 2, width // chips, 2 * share)
    small = (6 + time_embed.shape[0] + 7) // 8 * 8
    shape = jax.ShapeDtypeStruct
    copies = 8 * lines + 10 * size + 24
    lands = Scatter.lands(lines, block_rows, inner)
    return pl.pallas_call(
        functools.partial(backward_kernel, frames, lines, size),
        out_shape=[
            shape(((frames + 1) * PATCH, width), BF16),
            shape(latents.shape, F32),
            *[shape((block_rows, inner), F32)] * 4,
            shape(unit, BF16),
            shape((small, width), F32),
            shape((size,) + ffn_rows.shape, BF16),
            shape(unit, BF16),
            lands[2],
            *lands * 2,
        ],
        in_specs=[SMEM, ANY] + [VMEM] * 5 + [ANY] * 16 + [VMEM] * 3 + [ANY] * 2,
        out_specs=[ANY] + [VMEM] * 5 + [ANY, VMEM] + [ANY] * 9,
        scratch_shapes=[
            pltpu.VMEM((lines, block_rows, inner), BF16),
            *[pltpu.VMEM(blocks, BF16)] * 3,
            pltpu.VMEM((2, lines // 2, 2, 2, block_rows, inner), BF16),
            pltpu.VMEM((2, width, SPAN), BF16),
            pltpu.VMEM(weight_full.shape, BF16),
            pltpu.VMEM(weight_image.shape, BF16),
            pltpu.VMEM(weight_full.shape, BF16),
            pltpu.VMEM(weight_image.shape, BF16),
            pltpu.VMEM(absorbed.shape, BF16),
            pltpu.VMEM(into.shape, BF16),
            pltpu.VMEM((width, (share + 64 + 127) // 128 * 128), BF16),
            pltpu.VMEM((share, width), BF16),
            pltpu.VMEM((2, 2, PATCH, width), BF16),
            pltpu.VMEM((2, width, share), F32),
            pltpu.VMEM(unit, BF16),
            pltpu.VMEM((PATCH, width), F32),
            pltpu.VMEM((2, PATCH, width), BF16),
            pltpu.VMEM(time_embed.shape, F32),
            pltpu.VMEM((small, width), F32),
            *Total.scratch(lines, size, (small, width)),
            *[pltpu.VMEM(land.shape, BF16) for land in lands],
            pltpu.SemaphoreType.DMA((12,)),
            pltpu.SemaphoreType.DMA((2,)),
            pltpu.SemaphoreType.DMA((2, 2, 4)),
            pltpu.SemaphoreType.DMA((2,)),
            pltpu.SemaphoreType.DMA((max(4, lines),)),
            pltpu.SemaphoreType.DMA((2,)),
            pltpu.SemaphoreType.DMA((copies,)),
            pltpu.SemaphoreType.DMA((copies,)),
        ],
        compiler_params=params(collective_id=2, has_side_effects=True),
    )(
        counts,
        media,
        latents,
        gain_media,
        gain_latent,
        shift_latent,
        time_embed,
        query_weight,
        weight_full,
        weight_image,
        score_full,
        score_image,
        absorbed,
        into,
        out_plane,
        query_half,
        key_half,
        value_half,
        key_wait,
        value_wait,
        ffn_rows,
        cotangent_rows,
        cotangent_other,
        query_all,
        state_grad,
        ffn_gains,
        in_weight,
        down_weight,
    )


def result_kernel(
    chips,
    flags,
    slots,
    units,
    latent_in,
    latent_grad_in,
    key_in,
    value_in,
    query_in,
    out_in,
    media_grad,
    up,
    down,
    latent_out,
    latent_grad,
    key_value,
    query,
    out,
):
    item, frame = pl.program_id(0), pl.program_id(1)
    alive = (item == flags[0]) | (frame == 0)
    media_grad[0] = jnp.where(alive, slots[...].astype(F32), 0.0)

    @pl.when((item == 0) & (frame == 0))
    def _():
        share = units.shape[-1] // 2
        for pair in range(chips // 2):
            at = slice(pair * 2 * share, (pair + 1) * 2 * share)
            left, right = units[2 * pair].astype(F32), units[2 * pair + 1].astype(F32)
            up[:, at] = jnp.concatenate([left[:, :share], right[:, :share]], 1)
            down[:, at] = jnp.concatenate([left[:, share:], right[:, share:]], 1)
        latent_out[...] = latent_in[...]
        latent_grad[...] = latent_grad_in[...]
        inner = key_in.shape[-1]
        key_value[:, :inner] = key_in[...]
        key_value[:, inner:] = value_in[...]
        query[...] = query_in[...]
        out[...] = out_in[...]


def final_form(counts, slots, units, latent_out, latent_grad, sums, frames):
    chips, rows, columns = units.shape
    width = slots.shape[-1]
    block_rows = sums[0].shape[0]
    full = jnp.where(counts[0] > counts[1], 0, 1).astype(jnp.int32).reshape(1)
    shape = jax.ShapeDtypeStruct

    def whole(array_shape):
        return pl.BlockSpec(array_shape, lambda i, f, flags: (0,) * len(array_shape))

    outs = [
        ((rows, chips * columns // 2), F32),
        ((rows, chips * columns // 2), F32),
        (latent_out.shape, BF16),
        (latent_grad.shape, F32),
        ((block_rows, 2 * width), F32),
        ((block_rows, width), F32),
        ((block_rows, width), F32),
    ]
    return pl.pallas_call(
        functools.partial(result_kernel, chips),
        out_shape=[shape((2, frames * PATCH, width), F32)] + [shape(*out) for out in outs],
        grid_spec=pltpu.PrefetchScalarGridSpec(
            num_scalar_prefetch=1,
            grid=(2, frames),
            in_specs=[
                pl.BlockSpec(
                    (PATCH, width), lambda i, f, flags: (jnp.where(i == flags[0], f + 1, 0), 0)
                ),
                whole(units.shape),
                whole(latent_out.shape),
                whole(latent_grad.shape),
                *[whole(part.shape) for part in sums],
            ],
            out_specs=[pl.BlockSpec((1, PATCH, width), lambda i, f, flags: (i, f, 0))]
            + [whole(out[0]) for out in outs],
        ),
        compiler_params=params(),
    )(full, slots, units, latent_out, latent_grad, *sums)


def per_device(
    chips,
    size,
    media,
    frame_counts,
    latents,
    norm_media_gain,
    norm_media_shift,
    norm_latent_gain,
    norm_latent_shift,
    time_embed,
    query_weight,
    key_value_weight,
    out_weight,
    ffn_norm_gain,
    ffn_norm_shift,
    ffn_in_weight,
    ffn_out_weight,
    out_cotangent,
):
    dp, me = lax.axis_index("dp"), lax.axis_index("mp")
    width = media.shape[-1]
    share = ffn_in_weight.shape[1] // chips
    (
        norm_full,
        norm_image,
        weight_full,
        weight_image,
        absorbed,
        mixed,
        value_parts,
        peaks,
        latent_norm,
        queries,
        cotangent_all,
        cotangent_rows,
    ) = attend_forward(
        chips,
        size,
        frame_counts,
        media,
        latents,
        out_cotangent,
        norm_media_gain,
        norm_media_shift,
        norm_latent_gain,
        norm_latent_shift,
        time_embed,
        query_weight,
        key_value_weight,
    )
    (
        latent_out,
        state_grad,
        ffn_gains,
        into,
        score_full,
        score_image,
        query_all,
        out_plane,
        query_half,
        key_half,
        value_half,
        ffn_rows,
        cotangent_other,
        key_wait,
        value_wait,
        *_,
    ) = latent_pass(
        chips,
        size,
        frame_counts,
        value_parts,
        peaks,
        latents,
        cotangent_all,
        ffn_norm_gain,
        ffn_norm_shift,
        out_weight,
        ffn_in_weight,
        ffn_out_weight,
        key_value_weight,
        mixed,
        norm_full,
        norm_image,
        weight_full,
        weight_image,
        cotangent_rows,
        queries,
        latent_norm,
    )
    slot_grad, latent_grad, out_sum, query_sum, key_sum, value_sum, units, small, *_ = (
        attend_backward(
            chips,
            size,
            frame_counts,
            media,
            latents,
            norm_media_gain,
            norm_latent_gain,
            norm_latent_shift,
            time_embed,
            query_weight,
            weight_full,
            weight_image,
            score_full,
            score_image,
            absorbed,
            into,
            out_plane,
            query_half,
            key_half,
            value_half,
            key_wait,
            value_wait,
            ffn_rows,
            cotangent_rows,
            cotangent_other,
            query_all,
            state_grad,
            ffn_gains,
            ffn_in_weight,
            ffn_out_weight,
        )
    )
    units = units.reshape(chips, width // chips, 2 * share)
    sums = (key_sum, value_sum, query_sum, out_sum)
    media_grad, up_sum, down_sum, latent_out, latent_grad, key_value_sum, query_sum, out_sum = (
        final_form(
            frame_counts, slot_grad, units, latent_out, latent_grad, sums, media.shape[1] // PATCH
        )
    )
    place = (dp * size + me) * (width // (chips * size))
    small = lax.dynamic_slice_in_dim(small, place, width // (chips * size), 1)
    return (
        latent_out,
        latent_grad,
        media_grad,
        small[0],
        small[1],
        small[2],
        small[3],
        small[6 : 6 + time_embed.shape[0]],
        query_sum,
        key_value_sum,
        out_sum.T,
        small[4],
        small[5],
        up_sum,
        down_sum.T,
    )


def layer_norm(values_in, gain, shift):
    row_mean = jnp.mean(values_in, -1, keepdims=True)
    centered = values_in - row_mean
    variance = jnp.mean(centered * centered, -1, keepdims=True)
    return centered * lax.rsqrt(variance + EPSILON) * gain + shift


def plain_norm_back(values_in, gain, shift, gradient):
    result, pullback = jax.vjp(layer_norm, values_in, gain, shift)
    return pullback(gradient)


def gelu_exact(values_in):
    return jax.nn.gelu(values_in, approximate=False)


def rescale_heads(values_in, factor):
    shaped = values_in.reshape(values_in.shape[:-1] + (factor.shape[-1], -1))
    return (shaped * factor[..., None]).reshape(values_in.shape)


def plain_device(
    media,
    frame_counts,
    latents,
    norm_media_gain,
    norm_media_shift,
    norm_latent_gain,
    norm_latent_shift,
    time_embed,
    query_weight,
    key_value_weight,
    out_weight,
    ffn_norm_gain,
    ffn_norm_shift,
    ffn_in_weight,
    ffn_out_weight,
    out_cotangent,
):
    item_count, local_keys, model_width = media.shape
    latent_local = latents.shape[1]
    inner = HEADS * HEAD_DIM
    frames_local = local_keys // PATCH
    key_count = local_keys + latent_local
    mp_index = lax.axis_index("mp")
    latent_start = mp_index * latent_local
    score_scale = HEAD_DIM ** (-0.5)
    gain_m = norm_media_gain.astype(jnp.float32)
    shift_m = norm_media_shift.astype(jnp.float32)
    gain_l = norm_latent_gain.astype(jnp.float32)
    shift_l = norm_latent_shift.astype(jnp.float32)
    gain_f = ffn_norm_gain.astype(jnp.float32)
    shift_f = ffn_norm_shift.astype(jnp.float32)
    frame_ids = mp_index * frames_local + jnp.arange(frames_local)
    frame_live = frame_ids[None, :] < frame_counts[:, None]
    key_alive = jnp.concatenate(
        [jnp.repeat(frame_live, PATCH, axis=1), jnp.ones((item_count, latent_local), bool)], axis=1
    )
    alive_mask = key_alive[:, None, None, :]
    time_rows = lax.dynamic_slice_in_dim(
        time_embed, mp_index * frames_local, frames_local, 0
    ).astype(jnp.float32)
    with_time = (
        media.astype(jnp.float32).reshape(item_count, frames_local, PATCH, model_width)
        + time_rows[None, :, None, :]
    )
    with_time = with_time.reshape(item_count * local_keys, model_width)
    media_norm = layer_norm(with_time, gain_m, shift_m).astype(jnp.bfloat16)
    latent_in = latents.astype(jnp.float32)
    latent_norm = layer_norm(latent_in, gain_l, shift_l).astype(jnp.bfloat16)
    media_kv = jnp.dot(media_norm, key_value_weight, preferred_element_type=jnp.float32).astype(
        jnp.bfloat16
    )
    latent_kv = jnp.einsum(
        "ild,de->ile", latent_norm, key_value_weight, preferred_element_type=jnp.float32
    ).astype(jnp.bfloat16)
    keys_values = jnp.concatenate(
        [media_kv.reshape(item_count, local_keys, 2 * inner), latent_kv], axis=1
    )
    key_heads = keys_values[..., :inner].reshape(item_count, key_count, HEADS, HEAD_DIM)
    value_heads = keys_values[..., inner:].reshape(item_count, key_count, HEADS, HEAD_DIM)
    query_own = jnp.einsum(
        "ild,de->ile", latent_norm, query_weight, preferred_element_type=jnp.float32
    ).astype(jnp.bfloat16)
    queries = lax.all_gather(query_own, "mp", axis=1, tiled=True)
    lat_all = queries.shape[1]
    query_heads = queries.reshape(item_count, lat_all, HEADS, HEAD_DIM)
    scores = (
        jnp.einsum("iqhd,ikhd->ihqk", query_heads, key_heads, preferred_element_type=jnp.float32)
        * score_scale
    )
    masked = jnp.where(alive_mask, scores, -1e30)
    peak_score = jnp.max(masked, -1)
    weights = jnp.where(alive_mask, jnp.exp(masked - peak_score[..., None]), 0.0)
    weight_sum = jnp.sum(weights, -1).transpose(0, 2, 1)
    peak_score = peak_score.transpose(0, 2, 1)
    numerator = jnp.einsum(
        "ihqk,ikhd->iqhd",
        weights.astype(jnp.bfloat16),
        value_heads,
        preferred_element_type=jnp.float32,
    ).reshape(item_count, lat_all, inner)
    peak_all = lax.pmax(peak_score, "mp")
    factor = jnp.exp(peak_score - peak_all)
    weight_own, numerator_own = (
        lax.psum_scatter(weight_sum * factor, "mp", scatter_dimension=1, tiled=True),
        lax.psum_scatter(rescale_heads(numerator, factor), "mp", scatter_dimension=1, tiled=True),
    )
    peak_own = lax.dynamic_slice_in_dim(peak_all, latent_start, latent_local, 1)
    log_sum_own = peak_own + jnp.log(weight_own)
    attended_exact = rescale_heads(numerator_own, 1.0 / weight_own)
    attended_low = attended_exact.astype(jnp.bfloat16)
    update = jnp.einsum("ile,ed->ild", attended_low, out_weight, preferred_element_type=jnp.float32)
    hidden_state = latent_in + update
    ffn_norm = layer_norm(hidden_state, gain_f, shift_f).astype(jnp.bfloat16)
    ffn_norm_rows = ffn_norm.transpose(1, 0, 2)
    gathered = lax.all_gather(ffn_norm_rows, "mp", axis=0, tiled=True)
    pre_act = jnp.einsum("lid,df->lif", gathered, ffn_in_weight, preferred_element_type=jnp.float32)
    activated = gelu_exact(pre_act).astype(jnp.bfloat16)
    ffn_norm_all = gathered
    block = activated
    ffn_result = lax.psum_scatter(
        jnp.einsum("lif,fd->lid", block, ffn_out_weight, preferred_element_type=jnp.float32),
        "mp",
        scatter_dimension=0,
        tiled=True,
    )
    latent_out = (hidden_state + ffn_result.transpose(1, 0, 2)).astype(jnp.bfloat16)
    cotangent_rows = out_cotangent.transpose(1, 0, 2)
    gathered = lax.all_gather(cotangent_rows, "mp", axis=0, tiled=True)
    act_grad = jnp.einsum(
        "lid,fd->lif", gathered, ffn_out_weight, preferred_element_type=jnp.float32
    )
    result, pullback = jax.vjp(gelu_exact, pre_act)
    pre_grad = pullback(act_grad)[0].astype(jnp.bfloat16)
    ffn_down_grad = jnp.einsum(
        "lif,lid->fd", activated, gathered, preferred_element_type=jnp.float32
    )
    ffn_up_grad = jnp.einsum(
        "lid,lif->df", ffn_norm_all, pre_grad, preferred_element_type=jnp.float32
    )
    block = pre_grad
    ffn_norm_grad = lax.psum_scatter(
        jnp.einsum("lif,df->lid", block, ffn_in_weight, preferred_element_type=jnp.float32),
        "mp",
        scatter_dimension=0,
        tiled=True,
    ).transpose(1, 0, 2)
    state_part, gain_f_grad, shift_f_grad = plain_norm_back(hidden_state, gain_f, shift_f, ffn_norm_grad)
    state_grad = out_cotangent.astype(jnp.float32) + state_part
    update_grad = state_grad.astype(jnp.bfloat16)
    out_grad_local = jnp.einsum(
        "ile,ild->ed", attended_low, update_grad, preferred_element_type=jnp.float32
    )
    attended_grad = jnp.einsum(
        "ild,ed->ile", update_grad, out_weight, preferred_element_type=jnp.float32
    ).astype(jnp.bfloat16)
    row_delta = jnp.sum(
        (attended_grad.astype(jnp.float32) * attended_exact).reshape(
            item_count, latent_local, HEADS, HEAD_DIM
        ),
        -1,
    )
    grad_all, delta_all, log_sum_all = (
        lax.all_gather(attended_grad.astype(jnp.float32), "mp", axis=1, tiled=True),
        lax.all_gather(row_delta, "mp", axis=1, tiled=True),
        lax.all_gather(log_sum_own, "mp", axis=1, tiled=True),
    )
    grad_heads = grad_all.astype(jnp.bfloat16).reshape(item_count, lat_all, HEADS, HEAD_DIM)
    scores_again = (
        jnp.einsum("iqhd,ikhd->ihqk", query_heads, key_heads, preferred_element_type=jnp.float32)
        * score_scale
    )
    probability = jnp.where(
        alive_mask, jnp.exp(scores_again - log_sum_all.transpose(0, 2, 1)[..., None]), 0.0
    )
    prob_grad = jnp.einsum(
        "iqhd,ikhd->ihqk", grad_heads, value_heads, preferred_element_type=jnp.float32
    )
    score_grad = (probability * (prob_grad - delta_all.transpose(0, 2, 1)[..., None])).astype(
        jnp.bfloat16
    )
    query_part_grad = (
        jnp.einsum("ihqk,ikhd->iqhd", score_grad, key_heads, preferred_element_type=jnp.float32)
        * score_scale
    ).reshape(item_count, lat_all, inner)
    key_grad = (
        jnp.einsum("ihqk,iqhd->ikhd", score_grad, query_heads, preferred_element_type=jnp.float32)
        * score_scale
    )
    value_grad = jnp.einsum(
        "ihqk,iqhd->ikhd",
        probability.astype(jnp.bfloat16),
        grad_heads,
        preferred_element_type=jnp.float32,
    )
    kv_grad = jnp.concatenate(
        [
            key_grad.reshape(item_count, key_count, inner),
            value_grad.reshape(item_count, key_count, inner),
        ],
        -1,
    ).astype(jnp.bfloat16)
    query_grad = lax.psum_scatter(query_part_grad, "mp", scatter_dimension=1, tiled=True).astype(
        jnp.bfloat16
    )
    media_kv_grad = kv_grad[:, :local_keys].reshape(item_count * local_keys, 2 * inner)
    latent_kv_grad = kv_grad[:, local_keys:]
    kv_weight_local = jnp.einsum(
        "rd,re->de", media_norm, media_kv_grad, preferred_element_type=jnp.float32
    ) + jnp.einsum("ild,ile->de", latent_norm, latent_kv_grad, preferred_element_type=jnp.float32)
    query_weight_local = jnp.einsum(
        "ild,ile->de", latent_norm, query_grad, preferred_element_type=jnp.float32
    )
    media_norm_grad = jnp.einsum(
        "re,de->rd", media_kv_grad, key_value_weight, preferred_element_type=jnp.float32
    )
    latent_norm_grad = jnp.einsum(
        "ile,de->ild", latent_kv_grad, key_value_weight, preferred_element_type=jnp.float32
    ) + jnp.einsum("ile,de->ild", query_grad, query_weight, preferred_element_type=jnp.float32)
    media_pre_grad, gain_m_grad, shift_m_grad = plain_norm_back(
        with_time, gain_m, shift_m, media_norm_grad
    )
    latent_part, gain_l_grad, shift_l_grad = plain_norm_back(latent_in, gain_l, shift_l, latent_norm_grad)
    latent_grad = state_grad + latent_part
    media_grad = media_pre_grad.reshape(item_count, local_keys, model_width)
    time_local = jnp.sum(
        media_pre_grad.reshape(item_count, frames_local, PATCH, model_width), (0, 2)
    )
    time_grad = lax.dynamic_update_slice_in_dim(
        jnp.zeros((time_embed.shape[0], model_width), jnp.float32),
        time_local,
        mp_index * frames_local,
        0,
    )
    small_grads = jnp.concatenate(
        [
            jnp.stack(
                [gain_m_grad, shift_m_grad, gain_l_grad, shift_l_grad, gain_f_grad, shift_f_grad], 1
            ),
            time_grad.T,
        ],
        1,
    )
    query_sum, kv_sum, out_sum, small_sum = (
        lax.psum_scatter(query_weight_local, ("dp", "mp"), scatter_dimension=0, tiled=True),
        lax.psum_scatter(kv_weight_local, ("dp", "mp"), scatter_dimension=0, tiled=True),
        lax.psum_scatter(out_grad_local.T, ("dp", "mp"), scatter_dimension=0, tiled=True),
        lax.psum_scatter(small_grads, ("dp", "mp"), scatter_dimension=0, tiled=True),
    )
    ffn_up_sum, ffn_down_sum = (
        lax.psum_scatter(ffn_up_grad, "dp", scatter_dimension=0, tiled=True),
        lax.psum_scatter(ffn_down_grad.T, "dp", scatter_dimension=0, tiled=True),
    )
    return (
        latent_out,
        latent_grad,
        media_grad,
        small_sum[:, 0],
        small_sum[:, 1],
        small_sum[:, 2],
        small_sum[:, 3],
        small_sum[:, 6:].T,
        query_sum,
        kv_sum,
        out_sum.T,
        small_sum[:, 4],
        small_sum[:, 5],
        ffn_up_sum,
        ffn_down_sum.T,
    )


def solution(mesh):
    placed = (
        P("dp", "mp", None),
        P("dp"),
        P("dp", "mp", None),
        P(),
        P(),
        P(),
        P(),
        P(),
        P(),
        P(),
        P(),
        P(),
        P(),
        P(None, "mp"),
        P("mp", None),
        P("dp", "mp", None),
    )
    chips, size = mesh.shape["dp"], mesh.shape["mp"]

    def device(*arrays):
        tiled = arrays[0].shape[-1] % (chips * size * 16) == 0 and arrays[2].shape[1] % 16 == 0
        if tiled and chips == 16:
            return per_device(chips, size, *arrays)
        return plain_device(*arrays)

    return jax.shard_map(
        device,
        mesh=mesh,
        in_specs=placed,
        out_specs=(
            P("dp", "mp", None),
            P("dp", "mp", None),
            P("dp", "mp", None),
            P(("dp", "mp")),
            P(("dp", "mp")),
            P(("dp", "mp")),
            P(("dp", "mp")),
            P(None, ("dp", "mp")),
            P(("dp", "mp"), None),
            P(("dp", "mp"), None),
            P(None, ("dp", "mp")),
            P(("dp", "mp")),
            P(("dp", "mp")),
            P("dp", "mp"),
            P("mp", "dp"),
        ),
        check_vma=False,
    )
```
